32 devices in a mesh: seq: 8 (over z, x), fsdp: 4 (over y, core).
Axes of the slice: x: 2, y: 2, z: 4, core: 2. Of those that a mesh axis runs over, the one named last changes fastest.
Arguments:
- tokens: bfloat16 [4, 1024, 2560], P('fsdp', 'seq'), may hold values from -6 to 6
- w_x: bfloat16 [2560, 2560], P(('seq', 'fsdp')), may hold values from -0.125 to 0.125
- w_y: bfloat16 [2560, 2560], P(('seq', 'fsdp')), may hold values from -0.125 to 0.125
- w_out: bfloat16 [2560, 2560], P(('seq', 'fsdp')), may hold values from -0.3125 to 0.3125
- gate_w: bfloat16 [2, 256, 2560], P(None, None, ('seq', 'fsdp')), may hold values from -0.375 to 0.375
- gain_in: bfloat16 [2560], P(('seq', 'fsdp')), may hold values from 0.5 to 1.5
- gain_mlp: bfloat16 [2560], P(('seq', 'fsdp')), may hold values from 0.5 to 1.5
- conv_w: bfloat16 [4, 2560], P(None, ('seq', 'fsdp')), may hold values from -3 to 3
- gate_b: bfloat16 [2, 2560], P(None, ('seq', 'fsdp')), may hold values from -3 to 3
- rate: bfloat16 [2560], P(('seq', 'fsdp')), may hold values from 4.863739e-05 to 0.049804688
- w_gate: bfloat16 [2560, 7680], P('seq', 'fsdp'), may hold values from -0.125 to 0.125
- w_up: bfloat16 [2560, 7680], P('seq', 'fsdp'), may hold values from -0.125 to 0.125
- w_down: bfloat16 [7680, 2560], P('fsdp', 'seq'), may hold values from -0.125 to 0.125
- cotangent: bfloat16 [4, 1024, 2560], P('fsdp', 'seq'), may hold values from -6 to 6
Outputs:
- result: bfloat16 [4, 1024, 2560], P('fsdp', 'seq')
- tokens_grad: float32 [4, 1024, 2560], P('fsdp', 'seq')
- grad_w_x: float32 [2560, 2560], P(('seq', 'fsdp'))
- grad_w_y: float32 [2560, 2560], P(('seq', 'fsdp'))
- grad_w_out: float32 [2560, 2560], P(('seq', 'fsdp'))
- grad_gate_w: float32 [2, 256, 2560], P(None, None, ('seq', 'fsdp'))
- grad_gain_in: float32 [2560], P(('seq', 'fsdp'))
- grad_gain_mlp: float32 [2560], P(('seq', 'fsdp'))
- grad_conv_w: float32 [4, 2560], P(None, ('seq', 'fsdp'))
- grad_gate_b: float32 [2, 2560], P(None, ('seq', 'fsdp'))
- grad_rate: float32 [2560], P(('seq', 'fsdp'))
- grad_w_gate: float32 [2560, 7680], P('seq', 'fsdp')
- grad_w_up: float32 [2560, 7680], P('seq', 'fsdp')
- grad_w_down: float32 [7680, 2560], P('fsdp', 'seq')
The draws below stay inside these ranges and needn't reach their ends.
All inputs are finite; a program needn't handle non-finite values.
Results may differ from the reference program's by a relative error of at most 0.03.
Values may be sent and summed in bfloat16 or wider, within the bound.
No kernel may reach another device: no remote copies, remote signals or barrier semaphores. Data moves between devices by JAX's collectives and lax.ppermute only.
A program may use at most 512 MiB of HBM per device.

```python
import math
import jax
import jax.numpy as jnp
from jax import lax

D = 2560
HEADS = 10
HD = 256
R = 2560
FF = 7680
WIDTH = 4
LENGTH = 1024
SEQS = 4


def level_of(key, extent, shards, smallest, largest):
    loudness = 1.0
    for axis_at, shards_of in shards:
        steps = jax.random.uniform(jax.random.fold_in(jax.random.fold_in(key, 6), axis_at), (shards_of,), jnp.float32, smallest / len(shards), largest / len(shards))
        loudness = loudness * jnp.repeat(jnp.exp(steps), extent[axis_at] // shards_of).reshape((-1,) + (1,) * (len(extent) - 1 - axis_at))
    return loudness


def normal_values(rng, shape, width, reach, cuts=(), dtype=jnp.bfloat16):
    level = level_of(rng, shape, cuts, -0.22, 0.18) if cuts else 1.0
    result = jax.random.normal(rng, shape, jnp.float32) * width * level
    return jnp.minimum(jnp.maximum(result, -reach), reach).astype(dtype)


def setup_inputs(seed: int = 0) -> dict:
    key_list = jax.random.split(jax.random.key(seed), 15)
    return {
        "tokens": normal_values(key_list[0], (SEQS, LENGTH, D), 1.0, 6.0, ((0, 4), (1, 8))),
        "w_x": normal_values(key_list[1], (D, R), D ** -0.5, 0.125, ((0, 32),)),
        "w_y": normal_values(key_list[2], (D, R), D ** -0.5, 0.125, ((0, 32),)),
        "w_out": normal_values(key_list[3], (R, D), (R // 8) ** -0.5, 0.3125, ((0, 32),)),
        "gate_w": normal_values(key_list[4], (2, HD, R), HD ** -0.5, 0.375, ((2, 32),)),
        "gain_in": jnp.clip(1.0 + 0.1 * jax.random.normal(key_list[5], (D,), jnp.float32), 0.5, 1.5).astype(jnp.bfloat16),
        "gain_mlp": jnp.clip(1.0 + 0.1 * jax.random.normal(key_list[6], (D,), jnp.float32), 0.5, 1.5).astype(jnp.bfloat16),
        "conv_w": normal_values(key_list[7], (WIDTH, R), 0.5, 3.0, ((1, 32),)),
        "gate_b": normal_values(key_list[8], (2, R), 1.0, 3.0, ((1, 32),)),
        "rate": jnp.clip(jnp.exp(math.log(0.049804688) - 6.931472 * jax.random.uniform(key_list[9], (R,), jnp.float32) ** level_of(key_list[9], (R,), ((0, 32),), -0.2, 0.2)), 4.863739013671875e-05, 0.049804688).astype(jnp.bfloat16),
        "w_gate": normal_values(key_list[10], (D, FF), D ** -0.5, 0.125, ((0, 8), (1, 4))),
        "w_up": normal_values(key_list[11], (D, FF), D ** -0.5, 0.125, ((0, 8), (1, 4))),
        "w_down": normal_values(key_list[12], (FF, D), (FF // 4) ** -0.5, 0.125, ((0, 4), (1, 8))),
        "cotangent": normal_values(key_list[13], (SEQS, LENGTH, D), 1.0, 6.0, ((0, 4), (1, 8))),
    }


@jax.custom_vjp
def low(v):
    return lax.optimization_barrier(v.astype(jnp.bfloat16)).astype(jnp.float32)

@jax.custom_vjp
def low_back(v):
    return v

def low_keep(v):
    return (low(v), None)

def low_pass(kept, grad):
    return (grad,)

def back_keep(v):
    return (v, None)

def back_low(kept, grad):
    return (low(grad),)
low.defvjp(low_keep, low_pass)
low_back.defvjp(back_keep, back_low)
EPS = 1e-06
PRECISE = lax.Precision.HIGHEST

def precise(left, right):
    return jnp.dot(left, right, precision=PRECISE, preferred_element_type=jnp.float32)

def rms_scale(values, gain_scale):
    return values * lax.rsqrt(lax.optimization_barrier(jnp.mean(values * values, axis=-1, keepdims=True)) + EPS) * gain_scale

def gelu_tanh(values):
    return jax.nn.gelu(values, approximate=True)

def affine_pair(earlier, latter):
    return (earlier[0] * latter[0], earlier[1] * latter[0] + latter[1])

def causal_conv(extended, conv_full, tok_count):
    conv_out = conv_full[0] * extended[WIDTH - 1:WIDTH - 1 + tok_count]
    for tap_index in range(1, WIDTH):
        conv_out = conv_out + conv_full[tap_index] * extended[WIDTH - 1 - tap_index:WIDTH - 1 - tap_index + tok_count]
    return conv_out

def recurrence_inputs(conv_out, gate_full, bias_full, rate_full):
    tok_count = conv_out.shape[0]
    blocks = gate_full.reshape(2, HD, HEADS, HD)
    grouped = conv_out.reshape(tok_count, HEADS, HD)
    pre_a = jnp.einsum('thi,ihj->thj', grouped, blocks[0], precision=PRECISE).reshape(tok_count, -1) + bias_full[0]
    pre_x = jnp.einsum('thi,ihj->thj', grouped, blocks[1], precision=PRECISE).reshape(tok_count, -1) + bias_full[1]
    log_decay = -8.0 * jax.nn.sigmoid(pre_a) * rate_full
    decays = jnp.exp(log_decay)
    drives = jnp.sqrt(-jnp.expm1(2.0 * log_decay)) * jax.nn.sigmoid(pre_x) * conv_out
    return (decays, drives)

def sequence_block(tok_rows, w_x, w_y, w_out, gate_w, gain_in, gain_mlp, conv_w, gate_b, rate, w_gate, w_up, w_down):
    tok_count = tok_rows.shape[0]
    normed = low(rms_scale(tok_rows, gain_in))
    branch_x = low_back(low(precise(normed, w_x)))
    branch_y = low_back(precise(normed, w_y))
    extended = jnp.pad(branch_x, ((WIDTH - 1, 0), (0, 0)))
    conv_out = causal_conv(extended, conv_w, tok_count)
    decays, drives = recurrence_inputs(conv_out, gate_w, gate_b, rate)
    unused, states = lax.associative_scan(affine_pair, (decays, drives), axis=0)
    mixed_rows = low(states * gelu_tanh(branch_y))
    residual = tok_rows + low_back(precise(mixed_rows, w_out))
    normed_mlp = low(rms_scale(residual, gain_mlp))
    gate_pre = low_back(precise(normed_mlp, w_gate))
    up_proj = low_back(precise(normed_mlp, w_up))
    hidden = low(gelu_tanh(gate_pre) * up_proj)
    return residual + low_back(precise(hidden, w_down))

def reference(tokens, w_x, w_y, w_out, gate_w, gain_in, gain_mlp, conv_w, gate_b, rate, w_gate, w_up, w_down, cotangent):
    inputs = tuple((item.astype(jnp.float32) for item in (tokens, w_x, w_y, w_out, gate_w, gain_in, gain_mlp, conv_w, gate_b, rate, w_gate, w_up, w_down)))

    def entire(tok_all, p_x, p_y, p_out, p_gate, p_gain, p_gain_mlp, p_conv, p_bias, p_rate, p_wgate, p_wup, p_wdown):

        def one_sequence(tok_rows):
            return sequence_block(tok_rows, p_x, p_y, p_out, p_gate, p_gain, p_gain_mlp, p_conv, p_bias, p_rate, p_wgate, p_wup, p_wdown)
        return lax.map(jax.checkpoint(one_sequence), tok_all)
    outputs, pullback = jax.vjp(entire, *inputs)
    grads = pullback(cotangent.astype(jnp.float32))
    return (outputs.astype(jnp.bfloat16), grads[0], grads[1], grads[2], grads[3], grads[4], grads[5], grads[6], grads[7], grads[8], grads[9], grads[10], grads[11], grads[12])
```

```python
import functools

import jax
import jax.numpy as jnp
from jax import lax
from jax.experimental import pallas as pl
from jax.experimental.pallas import tpu as pltpu
from jax.sharding import Mesh
from jax.sharding import PartitionSpec as P

HEADS = 10
HD = 256
WIDTH = 4
HALO = 16
EPS = 1e-06
BF = jnp.bfloat16
F32 = jnp.float32


def swap(value, axis):
    return lax.ppermute(value, axis, [(0, 1), (1, 0)])


def shifted(value, axes, by, count, wrap=False):
    pairs = [(i, (i + by) % count) for i in range(count) if wrap or 0 <= i + by < count]
    return lax.ppermute(value, axes, pairs)


def pick(flag, first, second):
    return jnp.where(flag, first, second)


def cycle(length):
    return [z * 2 for z in range(length)] + [z * 2 + 1 for z in reversed(range(length))]


def around(length):
    walk = cycle(length)
    count = len(walk)
    forth = [(walk[i], walk[(i + 1) % count]) for i in range(count)]
    back = [(j, i) for i, j in forth]
    return walk, forth, back


def place_in(walk, index):
    inverse = [0] * len(walk)
    for position, linear in enumerate(walk):
        inverse[linear] = position
    return jnp.asarray(inverse, jnp.int32)[index]


def after(value, other):
    return lax.optimization_barrier((value, other))[0]


def dot(left, right, dims):
    return lax.dot_general(left, right, (dims, ((), ())), preferred_element_type=F32)


def product(left, right):
    return dot(left, right, ((1,), (0,)))


def product_t(left, right):
    return dot(left, right, ((1,), (1,)))


def t_product(left, right):
    return dot(left, right, ((0,), (0,)))


def rms_scale(values, gain_scale):
    return values * lax.rsqrt(jnp.mean(values * values, axis=-1, keepdims=True) + EPS) * gain_scale


def gelu_tanh(values):
    return jax.nn.gelu(values, approximate=True)


def gated_product(left, right):
    return gelu_tanh(left) * right


def gelu_both(v):
    inner = 0.7978845608028654 * (v + 0.044715 * v * v * v)
    th = jnp.tanh(inner)
    value = 0.5 * v * (1.0 + th)
    slope = 0.5 * (1.0 + th) + 0.5 * v * (1.0 - th * th) * 0.7978845608028654 * (1.0 + 0.134145 * v * v)
    return value, slope


def minus_expm1(v):
    series = jnp.full_like(v, 1.0)
    for n in range(11, 1, -1):
        series = 1.0 + series * v * (1.0 / n)
    return jnp.where(v > -1.0, -v * series, 1.0 - jnp.exp(v))


def two_parts(v):
    high = v.astype(BF)
    return high, (v - high.astype(F32)).astype(BF)


def wide_dot(left, right, dims):
    high, low = two_parts(left)
    return dot(high, right, dims) + dot(low, right, dims)


def moved(values, by, fill, rows):
    count = values.shape[0]
    rolled = pltpu.roll(values, by % count, 0)
    inside = rows >= by if by > 0 else rows < count + by
    return jnp.where(inside, rolled, fill)


def scan_rows(decay, drive, rows, backward):
    step = 1
    while step < decay.shape[0]:
        by = -step if backward else step
        drive = drive + decay * moved(drive, by, 0.0, rows)
        decay = decay * moved(decay, by, 1.0, rows)
        step *= 2
    return decay, drive


def conv_taps(rows_ref, halo_ref):
    rows = rows_ref[0].astype(F32)
    extended = jnp.concatenate([halo_ref[0].astype(F32), rows], axis=0)
    count = rows.shape[0]
    return [rows] + [extended[HALO - k : HALO - k + count] for k in range(1, WIDTH)]


def gates(conv_out, gate_ref, prm_ref):
    nt = ((1,), (1,))
    high, low = two_parts(conv_out)
    pre_a = dot(high, gate_ref[0], nt) + dot(low, gate_ref[0], nt) + prm_ref[4:5, :]
    pre_x = dot(high, gate_ref[1], nt) + dot(low, gate_ref[1], nt) + prm_ref[5:6, :]
    sig_a = jax.nn.sigmoid(pre_a)
    sig_x = jax.nn.sigmoid(pre_x)
    log_decay = -8.0 * sig_a * prm_ref[6:7, :]
    return sig_a, sig_x, jnp.exp(log_decay), jnp.sqrt(minus_expm1(2.0 * log_decay))


def forward_kernel(rows_ref, halo_ref, prm_ref, gate_ref, decay_ref, local_ref, cum_ref):
    taps = conv_taps(rows_ref, halo_ref)
    conv_out = sum(prm_ref[k : k + 1, :] * taps[k] for k in range(WIDTH))
    sig_a, sig_x, decays, root = gates(conv_out, gate_ref, prm_ref)
    drives = root * sig_x * conv_out
    decay_ref[0] = decays
    rows = lax.broadcasted_iota(jnp.int32, decays.shape, 0)
    cum, local = scan_rows(decays, drives, rows, False)
    cum_ref[0] = cum
    local_ref[0] = local


def back_scan_kernel(d_mixed_ref, branch_y_ref, states_ref, decay_ref, d_y_ref, local_ref, cum_ref):
    value, slope = gelu_both(branch_y_ref[0])
    d_mixed = d_mixed_ref[0]
    d_y_ref[0] = (d_mixed * states_ref[0] * slope).astype(BF)
    rows = lax.broadcasted_iota(jnp.int32, d_mixed.shape, 0)
    coeffs = moved(decay_ref[0], -1, 1.0, rows)
    cum, local = scan_rows(coeffs, d_mixed * value, rows, True)
    cum_ref[0] = cum
    local_ref[0] = local


def backward_kernel(
    rows_ref, halo_ref, prm_ref, gate_ref, local_ref, cum_ref, ends_ref, states_ref,
    d_conv_ref, d_gate_ref, d_prm_ref,
):
    taps = conv_taps(rows_ref, halo_ref)
    conv_out = sum(prm_ref[k : k + 1, :] * taps[k] for k in range(WIDTH))
    sig_a, sig_x, decays, root = gates(conv_out, gate_ref, prm_ref)
    rows = lax.broadcasted_iota(jnp.int32, decays.shape, 0)
    grad = local_ref[0] + cum_ref[0] * ends_ref[0, 0:1, :]
    before = jnp.where(rows >= 1, pltpu.roll(states_ref[0], 1, 0), ends_ref[0, 1:2, :])
    d_log = grad * before * decays - grad * sig_x * conv_out * (decays * decays / root)
    d_pre_a = d_log * (-8.0 * prm_ref[6:7, :]) * sig_a * (1.0 - sig_a)
    d_pre_x = grad * root * conv_out * sig_x * (1.0 - sig_x)
    nn, tn = ((1,), (0,)), ((0,), (0,))
    a_high, a_low = two_parts(d_pre_a)
    x_high, x_low = two_parts(d_pre_x)
    c_high, c_low = two_parts(conv_out)
    d_conv = grad * root * sig_x
    d_conv = d_conv + (dot(a_high, gate_ref[0], nn) + dot(a_low, gate_ref[0], nn))
    d_conv = d_conv + (dot(x_high, gate_ref[1], nn) + dot(x_low, gate_ref[1], nn))
    d_conv_ref[0] = d_conv
    d_gate_a = dot(a_high, c_high, tn) + dot(a_low, c_high, tn) + dot(a_high, c_low, tn)
    d_gate_x = dot(x_high, c_high, tn) + dot(x_low, c_high, tn) + dot(x_high, c_low, tn)
    total = lambda v: jnp.sum(v, axis=0, keepdims=True)
    sums = [total(d_conv * taps[k]) for k in range(WIDTH)]
    sums += [total(d_pre_a), total(d_pre_x), total(d_log * (-8.0 * sig_a))]
    sums.append(jnp.zeros_like(sums[0]))
    d_prm = jnp.concatenate(sums, axis=0)
    first = pl.program_id(1) == 0

    @pl.when(first)
    def _():
        d_gate_ref[0] = d_gate_a
        d_gate_ref[1] = d_gate_x
        d_prm_ref[...] = d_prm

    @pl.when(jnp.logical_not(first))
    def _():
        d_gate_ref[0] += d_gate_a
        d_gate_ref[1] += d_gate_x
        d_prm_ref[...] += d_prm


def head_specs(tok):
    rows = pl.BlockSpec((1, tok, HD), lambda h, q: (q, 0, h))
    halo = pl.BlockSpec((1, HALO, HD), lambda h, q: (q, 0, h))
    prm = pl.BlockSpec((8, HD), lambda h, q: (0, h))
    gate = pl.BlockSpec((2, HD, HD), lambda h, q: (0, h, 0))
    ends = pl.BlockSpec((1, 8, HD), lambda h, q: (q, 0, h))
    return rows, halo, prm, gate, ends


PARAMS = dict(vmem_limit_bytes=40 * 1024 * 1024)


def forward_call(branch_x, halo, prm, gate):
    seqs, tok, half = branch_x.shape
    rows_s, halo_s, prm_s, gate_s, _ = head_specs(tok)
    out = jax.ShapeDtypeStruct(branch_x.shape, F32)
    return pl.pallas_call(
        forward_kernel,
        grid=(half // HD, seqs),
        in_specs=[rows_s, halo_s, prm_s, gate_s],
        out_specs=[rows_s] * 3,
        out_shape=[out] * 3,
        compiler_params=pltpu.CompilerParams(**PARAMS),
        name="recurrence_forward",
    )(branch_x, halo, prm, gate)


def back_scan_call(d_mixed, branch_y, states, decays):
    seqs, tok, half = d_mixed.shape
    rows_s = head_specs(tok)[0]
    out = jax.ShapeDtypeStruct(d_mixed.shape, F32)
    return pl.pallas_call(
        back_scan_kernel,
        grid=(half // HD, seqs),
        in_specs=[rows_s] * 4,
        out_specs=[rows_s] * 3,
        out_shape=[jax.ShapeDtypeStruct(d_mixed.shape, BF), out, out],
        compiler_params=pltpu.CompilerParams(**PARAMS),
        name="recurrence_back_scan",
    )(d_mixed, branch_y, states, decays)


def backward_call(branch_x, halo, prm, gate, local, cum, ends, states):
    seqs, tok, half = branch_x.shape
    rows_s, halo_s, prm_s, gate_s, ends_s = head_specs(tok)
    return pl.pallas_call(
        backward_kernel,
        grid=(half // HD, seqs),
        in_specs=[rows_s, halo_s, prm_s, gate_s, rows_s, rows_s, ends_s, rows_s],
        out_specs=[rows_s, gate_s, prm_s],
        out_shape=[
            jax.ShapeDtypeStruct(branch_x.shape, F32),
            jax.ShapeDtypeStruct(gate.shape, F32),
            jax.ShapeDtypeStruct(prm.shape, F32),
        ],
        compiler_params=pltpu.CompilerParams(**PARAMS),
        name="recurrence_backward",
    )(branch_x, halo, prm, gate, local, cum, ends, states)


def gather_small(value, zn, z, x, y, c):
    value = value[None]
    for axis, at in (("c", c), ("y", y), ("x", x)):
        other = swap(value, axis)
        value = pick(at == 0, jnp.concatenate([value, other]), jnp.concatenate([other, value]))
    whole = jnp.zeros((zn,) + value.shape, value.dtype)
    whole = lax.dynamic_update_slice_in_dim(whole, value[None], z, 0)
    for by in range(1, zn):
        came = shifted(value, "z", by, zn, True)
        whole = lax.dynamic_update_slice_in_dim(whole, came[None], lax.rem(z - by + zn, zn), 0)
    return whole.reshape((-1,) + value.shape[1:])


def sum_small(value, axes, zn):
    for axis in axes:
        value = value + swap(value, axis)
    return value + sum(shifted(value, "z", by, zn, True) for by in range(1, zn))


def carried(decay, drive, count, by):
    both = jnp.stack([decay, drive])
    state = jnp.zeros_like(drive)
    came = [shifted(both, ("z", "x"), by * far, count) for far in range(count - 1, 0, -1)]
    for part in came:
        state = part[0] * state + part[1]
    return state


def per_device(
    zn, fold,
    tokens, w_x, w_y, w_out, gate_w, gain_in, gain_mlp, conv_w, gate_b, rate,
    w_gate, w_up, w_down, cotangent,
):
    z, x, y, c = (lax.axis_index(axis) for axis in ("z", "x", "y", "c"))
    zh = zn // 2
    seq_count = 2 * zn
    tok, width = tokens.shape[1], tokens.shape[2]
    share = w_x.shape[0]
    wide_r = w_x.shape[1]
    half = wide_r // 2
    rows_ff, cols_ff = w_gate.shape
    walk, forth, back = around(zn)
    ring_count = len(walk)
    at_x = place_in(walk, z * 2 + x)
    walk_of = jnp.asarray(walk, jnp.int32)
    cw_from = [walk_of[lax.rem(at_x - k + ring_count, ring_count)] for k in range(ring_count)]
    ccw_from = [walk_of[lax.rem(at_x + k, ring_count)] for k in range(ring_count)]
    zx, zy = ("z", "x"), ("z", "y")

    spread = []
    for other in (0, 1):
        pairs = []
        for h in (0, 1):
            for zl in range(zh):
                for ys in (0, 1):
                    k = ys ^ other
                    pairs.append(((h * zh + zl) * 2 + ys, (k * zh + zl) * 2 + h))
        spread.append(pairs)
    gathered_back = [[(b, a) for a, b in pairs] for pairs in spread]

    tok_own = tokens[0]
    tok_pair = jnp.stack([tok_own, swap(tok_own, "y")])
    smalls = jnp.concatenate([gain_in[None], gain_mlp[None], conv_w, gate_b, rate[None]]).astype(F32)
    smalls = gather_small(smalls, zn, z, x, y, c)
    smalls = smalls.transpose(1, 0, 2).reshape(smalls.shape[1], -1)
    gain_first, gain_second = smalls[0], smalls[1]
    prm = jnp.pad(smalls[2:], ((0, 1), (0, 0)))
    prm = pick(y == 0, prm[:, :half], prm[:, half:])

    xy_first = jnp.concatenate([w_x[:, :half], w_y[:, :half]], axis=1)
    xy_second = jnp.concatenate([w_x[:, half:], w_y[:, half:]], axis=1)
    xy_own = pick(y == 0, xy_first, xy_second)
    xy_other = swap(pick(y == 0, xy_second, xy_first), "y")
    gate_t = gate_w.transpose(0, 2, 1)
    gate_pieces = [
        lax.ppermute(pick(y == 0, gate_t[k], gate_t[1 - k]), zy, spread[k]) for k in (0, 1)
    ]

    forth_part = jnp.concatenate([xy_own, gate_pieces[0]], axis=1)
    back_part = jnp.concatenate([xy_other, gate_pieces[1]], axis=1)
    full_xy = jnp.zeros((seq_count, 2, 2, share, wide_r), BF)
    gates_t = jnp.zeros((2, zh * 2, 2, 2, share, HD), BF)
    for k in range(ring_count):
        if k:
            forth_part = lax.ppermute(forth_part, zx, forth)
            back_part = lax.ppermute(back_part, zx, back)
        both = jnp.stack([forth_part, back_part])
        others = swap(both, "c")
        for core, parts in ((c, both), (1 - c, others)):
            for d, src in ((0, cw_from[k]), (1, ccw_from[k])):
                blk = parts[d]
                y_blk = y if d == 0 else 1 - y
                full_xy = lax.dynamic_update_slice(
                    full_xy, blk[None, None, None, :, :wide_r], (src, y_blk, core, 0, 0)
                )
                src_z, src_x = src // 2, lax.rem(src, 2)
                src_h, src_l = src_z // zh, lax.rem(src_z, zh)
                y_src = src_h if d == 0 else 1 - src_h
                gates_t = lax.dynamic_update_slice(
                    gates_t, blk[None, None, None, None, :, wide_r:],
                    (src_h, src_l * 2 + src_x, y_src, core, 0, 0),
                )
    full_xy = full_xy.reshape(-1, wide_r)
    gates_t = gates_t.reshape(2, half, HD)
    last = forth_part

    out_halves = [w_out[:, :half], w_out[:, half:]]
    out_parts = [
        lax.ppermute(pick(y == 0, out_halves[k], out_halves[1 - k]), zy, spread[k]) for k in (0, 1)
    ]
    forth_part, back_part = after(tuple(out_parts), last)
    full_out = jnp.zeros((2, zh * 2, 2, 2, share, half), BF)
    for k in range(ring_count):
        if k:
            forth_part = lax.ppermute(forth_part, zx, forth)
            back_part = lax.ppermute(back_part, zx, back)
        both = jnp.stack([forth_part, back_part])
        others = swap(both, "c")
        for core, parts in ((c, both), (1 - c, others)):
            for d, src in ((0, cw_from[k]), (1, ccw_from[k])):
                src_z, src_x = src // 2, lax.rem(src, 2)
                src_h, src_l = src_z // zh, lax.rem(src_z, zh)
                y_src = src_h if d == 0 else 1 - src_h
                full_out = lax.dynamic_update_slice(
                    full_out, parts[d][None, None, None, None],
                    (src_h, src_l * 2 + src_x, y_src, core, 0, 0),
                )
    full_out = full_out.reshape(2, half, half)
    full_out = jnp.concatenate([full_out[0], full_out[1]], axis=1)
    last = forth_part

    padded = zn * fold
    widen = lambda w: jnp.pad(w, ((0, 0), (0, padded - cols_ff)))
    ff_all = jnp.stack([widen(w_gate), widen(w_up), widen(w_down.T)])
    ff_all = ff_all.reshape(3, rows_ff, zn, fold).transpose(2, 1, 0, 3).reshape(zn, rows_ff, 3 * fold)
    ff_all = after(ff_all, last)
    w_gu = jnp.zeros((zn, 2, rows_ff, 2 * fold), BF)
    w_dt = jnp.zeros((zn, 2, rows_ff, fold), BF)

    def put_ff(w_gu, w_dt, piece, z_at):
        across = swap(piece, "x")
        for x_at, part in ((x, piece), (1 - x, across)):
            w_gu = lax.dynamic_update_slice(w_gu, part[None, None, :, : 2 * fold], (z_at, x_at, 0, 0))
            w_dt = lax.dynamic_update_slice(w_dt, part[None, None, :, 2 * fold :], (z_at, x_at, 0, 0))
        return w_gu, w_dt

    w_gu, w_dt = put_ff(w_gu, w_dt, lax.dynamic_index_in_dim(ff_all, z, 0, False), z)
    for far in range(1, zn):
        to = lax.rem(z + far, zn)
        came = shifted(lax.dynamic_index_in_dim(ff_all, to, 0, False), "z", far, zn, True)
        w_gu, w_dt = put_ff(w_gu, w_dt, came, lax.rem(z - far + zn, zn))
    w_gu = w_gu.reshape(-1, 2 * fold)
    w_dt = w_dt.reshape(-1, fold)

    cot = cotangent[0]
    cut = tok // 2

    def both_cores(part):
        return jnp.concatenate([part, swap(part, "c")])

    forth_part, back_part = after((cot[:cut], cot[cut:]), last)
    cot_steps = []
    for k in range(ring_count):
        if k:
            forth_part = lax.ppermute(forth_part, zy, forth)
            back_part = lax.ppermute(back_part, zy, back)
        cot_steps.append(both_cores(jnp.concatenate([forth_part, back_part])))

    tok_f = tok_pair.astype(F32)
    normed = rms_scale(tok_f, gain_first).astype(BF).reshape(2 * tok, width)
    branches = product(normed, full_xy)
    branch_x = branches[:, :half].astype(BF).reshape(2, tok, half)
    branch_y = branches[:, half:].reshape(2, tok, half)
    halo = shifted(branch_x[:, tok - HALO :], zx, 1, seq_count)
    decays, local, cum = forward_call(branch_x, halo, prm, gates_t)
    state_in = carried(cum[:, -1], local[:, -1], seq_count, 1)
    states = local + cum * state_in[:, None]
    mixed = (states * gelu_tanh(branch_y)).astype(BF).reshape(2 * tok, half)
    out_sum = product(mixed, full_out)
    residual = tok_own.astype(F32) + out_sum[:tok] + swap(out_sum[tok:].astype(BF), "y").astype(F32)
    normed_mlp = rms_scale(residual, gain_second).astype(BF)

    forth_part, back_part = normed_mlp[:cut], normed_mlp[cut:]
    row_steps, hidden_steps, d_gu_steps, out_steps = [], [], [], []
    first_sum, d_forth, d_back = None, None, None
    for k in range(ring_count):
        if k:
            forth_part = lax.ppermute(forth_part, zy, forth)
            back_part = lax.ppermute(back_part, zy, back)
        rows = both_cores(jnp.concatenate([forth_part, back_part]))
        gu = product(rows, w_gu)
        d_hidden = product(cot_steps[k], w_dt)
        gate_pre, up_proj = gu[:, :fold], gu[:, fold:]
        hidden, pull = jax.vjp(gated_product, gate_pre, up_proj)
        hidden = hidden.astype(BF)
        d_gu = jnp.concatenate([item.astype(BF) for item in pull(d_hidden)], axis=1)
        row_steps.append(rows)
        hidden_steps.append(hidden)
        d_gu_steps.append(d_gu)
        d_rows = product_t(d_gu, w_gu)
        d_own = d_rows[:tok] + swap(d_rows[tok:].astype(BF), "c").astype(F32)
        if k == 0:
            first_sum = d_own
        elif k == 1:
            d_forth, d_back = d_own[:cut].astype(BF), d_own[cut:].astype(BF)
        else:
            d_forth = (lax.ppermute(d_forth, zy, forth).astype(F32) + d_own[:cut]).astype(BF)
            d_back = (lax.ppermute(d_back, zy, back).astype(F32) + d_own[cut:]).astype(BF)
    d_forth = lax.ppermute(d_forth, zy, forth).astype(F32) + first_sum[:cut]
    d_back = lax.ppermute(d_back, zy, back).astype(F32) + first_sum[cut:]
    d_normed_mlp = jnp.concatenate([d_forth, d_back])

    rows_all = jnp.concatenate(row_steps)
    cot_all = jnp.concatenate(cot_steps)
    hidden_all = jnp.concatenate(hidden_steps)
    d_gu_all = jnp.concatenate(d_gu_steps)
    grad_gu = t_product(rows_all, d_gu_all).reshape(zn, 2, rows_ff, 2 * fold)
    grad_dt = t_product(cot_all, hidden_all).reshape(zn, 2, rows_ff, fold)

    grad_rows = cot.astype(F32)
    unused, second_pull = jax.vjp(rms_scale, residual, gain_second)
    d_res_norm, d_gain_mlp = second_pull(d_normed_mlp)
    d_residual = grad_rows + d_res_norm
    d_branch = d_residual.astype(BF)
    d_branch_pair = jnp.concatenate([d_branch, swap(d_branch, "y")])
    d_mixed = product_t(d_branch_pair, full_out).reshape(2, tok, half)
    grad_out = t_product(mixed, d_branch_pair)

    def ff_block(z_at, x_at):
        gu = lax.dynamic_slice(grad_gu, (z_at, x_at, 0, 0), (1, 1, rows_ff, 2 * fold))
        dt = lax.dynamic_slice(grad_dt, (z_at, x_at, 0, 0), (1, 1, rows_ff, fold))
        return jnp.concatenate([gu, dt], axis=-1)[0, 0]

    ff_grad = jnp.zeros((zn, rows_ff, 3 * fold), F32)
    for far in range(zn - 1, -1, -1):
        to = lax.rem(z + far, zn)
        piece = ff_block(to, x) + swap(ff_block(to, 1 - x).astype(BF), "x").astype(F32)
        if far:
            piece = shifted(piece.astype(BF), "z", far, zn, True).astype(F32)
        ff_grad = lax.dynamic_update_slice(ff_grad, piece[None], (lax.rem(z - far + zn, zn), 0, 0))
    ff_grad = ff_grad.reshape(zn, rows_ff, 3, fold).transpose(2, 1, 0, 3).reshape(3, rows_ff, padded)
    ff_grad = ff_grad[:, :, :cols_ff]

    def out_step(k):
        part = product_t(hidden_steps[k], w_dt)
        return part[:tok] + swap(part[tok:].astype(BF), "c").astype(F32)

    for k in range(1, ring_count):
        part = out_step(k)
        if k == 1:
            o_forth, o_back = part[:cut].astype(BF), part[cut:].astype(BF)
        else:
            o_forth = (lax.ppermute(o_forth, zy, forth).astype(F32) + part[:cut]).astype(BF)
            o_back = (lax.ppermute(o_back, zy, back).astype(F32) + part[cut:]).astype(BF)
    part = out_step(0)
    mlp_out = jnp.concatenate([
        lax.ppermute(o_forth, zy, forth).astype(F32) + part[:cut],
        lax.ppermute(o_back, zy, back).astype(F32) + part[cut:],
    ])
    result = (residual + mlp_out).astype(BF)[None]

    d_branch_y, local_back, cum_back = back_scan_call(d_mixed, branch_y, states, decays)
    leaving = decays[:, 0] * local_back[:, 0]
    carry_back = carried(cum[:, -1], leaving, seq_count, -1)
    ends = jnp.pad(jnp.stack([carry_back, state_in], axis=1), ((0, 0), (0, 6), (0, 0)))
    d_conv, d_gates, d_prm = backward_call(
        branch_x, halo, prm, gates_t, local_back, cum_back, ends, states
    )
    rim = shifted(d_conv[:, :8], zx, -1, seq_count)
    d_ext = jnp.concatenate([d_conv, rim], axis=1)
    d_branch_x = sum(prm[k] * d_ext[:, k : k + tok] for k in range(WIDTH)).astype(BF)
    d_branches = jnp.concatenate([d_branch_x, d_branch_y], axis=2).reshape(2 * tok, 2 * half)
    grad_xy = t_product(normed, d_branches)
    d_normed = product_t(d_branches, full_xy)
    d_normed = d_normed[:tok] + swap(d_normed[tok:].astype(BF), "y").astype(F32)
    unused, first_pull = jax.vjp(rms_scale, tok_own.astype(F32), gain_first)
    d_tok, d_gain_in = first_pull(d_normed)
    tokens_grad = (d_residual + d_tok)[None]

    def ring_sum(pieces_of):
        for k in range(1, ring_count):
            f, b = pieces_of(cw_from[k], 0), pieces_of(ccw_from[k], 1)
            if k > 1:
                f = f + lax.ppermute(forth_sum, zx, forth).astype(F32)
                b = b + lax.ppermute(back_sum, zx, back).astype(F32)
            forth_sum, back_sum = f.astype(BF), b.astype(BF)
        f, b = pieces_of(cw_from[0], 0), pieces_of(ccw_from[0], 1)
        return (
            f + lax.ppermute(forth_sum, zx, forth).astype(F32),
            b + lax.ppermute(back_sum, zx, back).astype(F32),
        )

    def over_cores(blocks, axis):
        keep = lax.dynamic_index_in_dim(blocks, c, axis, False)
        give = lax.dynamic_index_in_dim(blocks, 1 - c, axis, False)
        return keep + swap(give.astype(BF), "c").astype(F32)

    out_blocks = jnp.stack([grad_out[:, :half], grad_out[:, half:]])
    out_blocks = over_cores(out_blocks.reshape(2, zh * 2, 2, 2, share, half), 3)

    def out_piece(linear, direction, blocks=out_blocks):
        src_z, src_x = linear // 2, lax.rem(linear, 2)
        src_h, src_l = src_z // zh, lax.rem(src_z, zh)
        y_src = src_h if direction == 0 else 1 - src_h
        sizes = (1, 1, 1) + blocks.shape[3:]
        return lax.dynamic_slice(blocks, (src_h, src_l * 2 + src_x, y_src, 0, 0), sizes)[0, 0, 0]

    out_sums = ring_sum(out_piece)
    came = [lax.ppermute(out_sums[k].astype(BF), zy, gathered_back[k]).astype(F32) for k in (0, 1)]
    grad_w_out = jnp.concatenate(
        [pick(y == 0, came[0], came[1]), pick(y == 0, came[1], came[0])], axis=1
    )

    gate_blocks = over_cores(d_gates.reshape(2, zh * 2, 2, 2, share, HD), 3)
    xy_blocks = over_cores(grad_xy.reshape(seq_count, 2, 2, share, wide_r), 2)

    def xy_piece(linear, direction):
        y_blk = y if direction == 0 else 1 - y
        xy = lax.dynamic_slice(xy_blocks, (linear, y_blk, 0, 0), (1, 1, share, wide_r))[0, 0]
        return jnp.concatenate([xy, out_piece(linear, direction, gate_blocks)], axis=1)

    xy_sums = ring_sum(xy_piece)
    mine = xy_sums[0][:, :wide_r]
    across = swap(xy_sums[1][:, :wide_r].astype(BF), "y").astype(F32)
    low, high = pick(y == 0, mine, across), pick(y == 0, across, mine)
    grad_w_x = jnp.concatenate([low[:, :half], high[:, :half]], axis=1)
    grad_w_y = jnp.concatenate([low[:, half:], high[:, half:]], axis=1)
    came = [
        lax.ppermute(xy_sums[k][:, wide_r:].astype(BF), zy, gathered_back[k]).astype(F32)
        for k in (0, 1)
    ]
    grad_gate_w = jnp.stack([pick(y == 0, came[0], came[1]), pick(y == 0, came[1], came[0])])
    grad_gate_w = grad_gate_w.transpose(0, 2, 1)

    block = (z * 2 + x) * 4 + y * 2 + c
    small_sum = sum_small(d_prm, ("c", "x"), zn)
    other_half = swap(small_sum, "y")
    small_sum = jnp.concatenate(
        [pick(y == 0, small_sum, other_half), pick(y == 0, other_half, small_sum)], axis=1
    )
    own_small = lax.dynamic_slice(small_sum, (0, block * share), (8, share))
    gains = sum_small(jnp.stack([d_gain_in, d_gain_mlp]), ("c", "x", "y"), zn)
    own_gain = lax.dynamic_slice(gains, (0, block * share), (2, share))
    return (
        result,
        tokens_grad,
        grad_w_x,
        grad_w_y,
        grad_w_out,
        grad_gate_w,
        own_gain[0],
        own_gain[1],
        own_small[:WIDTH],
        own_small[WIDTH : WIDTH + 2],
        own_small[WIDTH + 2],
        ff_grad[0],
        ff_grad[1],
        ff_grad[2].T,
    )


def solution(mesh):
    seq_count, pair_count = mesh.shape["seq"], mesh.shape["fsdp"]
    zn = seq_count // 2
    grid = Mesh(mesh.devices.reshape(zn, 2, pair_count // 2, 2), ("z", "x", "y", "c"))
    seq, fsdp, both = ("z", "x"), ("y", "c"), ("z", "x", "y", "c")
    rows = P(fsdp, seq, None)
    by_row = P(both, None)
    by_col = P(None, both)
    placed = (
        rows, by_row, by_row, by_row, P(None, None, both), P(both), P(both), by_col, by_col, P(both),
        P(seq, fsdp), P(seq, fsdp), P(fsdp, seq), rows,
    )
    out_specs = (
        rows, rows, by_row, by_row, by_row, P(None, None, both), P(both), P(both), by_col, by_col,
        P(both), P(seq, fsdp), P(seq, fsdp), P(fsdp, seq),
    )

    def run(*args):
        hidden_share = args[10].shape[1] // pair_count
        lanes = 128
        fold = -(-hidden_share // (lanes * zn)) * lanes
        return jax.shard_map(
            functools.partial(per_device, zn, fold),
            mesh=grid, in_specs=placed, out_specs=out_specs, check_vma=False,
        )(*args)

    return run
```

```python
import functools

import jax
import jax.numpy as jnp
from jax import lax
from jax.experimental import pallas as pl
from jax.experimental.pallas import tpu as pltpu
from jax.sharding import Mesh
from jax.sharding import PartitionSpec as P

HEADS = 10
HD = 256
WIDTH = 4
HALO = 16
EPS = 1e-06
BF = jnp.bfloat16
F32 = jnp.float32


def swap(value, axis):
    return lax.ppermute(value, axis, [(0, 1), (1, 0)])


def shifted(value, axes, by, count, wrap=False):
    pairs = [(i, (i + by) % count) for i in range(count) if wrap or 0 <= i + by < count]
    return lax.ppermute(value, axes, pairs)


def pick(flag, first, second):
    return jnp.where(flag, first, second)


def tick(*values):
    return lax.optimization_barrier(values)


def dot(left, right, dims):
    return lax.dot_general(left, right, (dims, ((), ())), preferred_element_type=F32)


def product(left, right):
    return dot(left, right, ((1,), (0,)))


def product_t(left, right):
    return dot(left, right, ((1,), (1,)))


def t_product(left, right):
    return dot(left, right, ((0,), (0,)))


def rms_scale(values, gain_scale):
    return values * lax.rsqrt(jnp.mean(values * values, axis=-1, keepdims=True) + EPS) * gain_scale


def gelu_tanh(values):
    return jax.nn.gelu(values, approximate=True)


def gated_product(left, right):
    return gelu_tanh(left) * right


def gelu_both(v):
    inner = 0.7978845608028654 * (v + 0.044715 * v * v * v)
    th = jnp.tanh(inner)
    value = 0.5 * v * (1.0 + th)
    slope = 0.5 * (1.0 + th) + 0.5 * v * (1.0 - th * th) * 0.7978845608028654 * (1.0 + 0.134145 * v * v)
    return value, slope


def minus_expm1(v):
    series = jnp.full_like(v, 1.0)
    for n in range(11, 1, -1):
        series = 1.0 + series * v * (1.0 / n)
    return jnp.where(v > -1.0, -v * series, 1.0 - jnp.exp(v))


def two_parts(v):
    high = v.astype(BF)
    return high, (v - high.astype(F32)).astype(BF)


def wide_dot(left, right, dims):
    high, low = two_parts(left)
    return dot(high, right, dims) + dot(low, right, dims)


def moved(values, by, fill, rows):
    count = values.shape[0]
    rolled = pltpu.roll(values, by % count, 0)
    inside = rows >= by if by > 0 else rows < count + by
    return jnp.where(inside, rolled, fill)


def scan_rows(decay, drive, rows, backward):
    step = 1
    while step < decay.shape[0]:
        by = -step if backward else step
        drive = drive + decay * moved(drive, by, 0.0, rows)
        decay = decay * moved(decay, by, 1.0, rows)
        step *= 2
    return decay, drive


def conv_taps(rows_ref, halo_ref):
    rows = rows_ref[0].astype(F32)
    extended = jnp.concatenate([halo_ref[0].astype(F32), rows], axis=0)
    count = rows.shape[0]
    return [rows] + [extended[HALO - k : HALO - k + count] for k in range(1, WIDTH)]


def gates(conv_out, gate_ref, prm_ref):
    nt = ((1,), (1,))
    high, low = two_parts(conv_out)
    pre_a = dot(high, gate_ref[0], nt) + dot(low, gate_ref[0], nt) + prm_ref[4:5, :]
    pre_x = dot(high, gate_ref[1], nt) + dot(low, gate_ref[1], nt) + prm_ref[5:6, :]
    sig_a = jax.nn.sigmoid(pre_a)
    sig_x = jax.nn.sigmoid(pre_x)
    log_decay = -8.0 * sig_a * prm_ref[6:7, :]
    return sig_a, sig_x, jnp.exp(log_decay), jnp.sqrt(minus_expm1(2.0 * log_decay))


def forward_kernel(rows_ref, halo_ref, prm_ref, gate_ref, decay_ref, local_ref, cum_ref):
    taps = conv_taps(rows_ref, halo_ref)
    conv_out = sum(prm_ref[k : k + 1, :] * taps[k] for k in range(WIDTH))
    sig_a, sig_x, decays, root = gates(conv_out, gate_ref, prm_ref)
    drives = root * sig_x * conv_out
    decay_ref[0] = decays
    rows = lax.broadcasted_iota(jnp.int32, decays.shape, 0)
    cum, local = scan_rows(decays, drives, rows, False)
    cum_ref[0] = cum
    local_ref[0] = local


def back_scan_kernel(d_mixed_ref, branch_y_ref, states_ref, decay_ref, d_y_ref, local_ref, cum_ref):
    value, slope = gelu_both(branch_y_ref[0])
    d_mixed = d_mixed_ref[0]
    d_y_ref[0] = (d_mixed * states_ref[0] * slope).astype(BF)
    rows = lax.broadcasted_iota(jnp.int32, d_mixed.shape, 0)
    coeffs = moved(decay_ref[0], -1, 1.0, rows)
    cum, local = scan_rows(coeffs, d_mixed * value, rows, True)
    cum_ref[0] = cum
    local_ref[0] = local


def backward_kernel(
    rows_ref, halo_ref, prm_ref, gate_ref, local_ref, cum_ref, ends_ref, states_ref,
    d_conv_ref, d_gate_ref, d_prm_ref,
):
    taps = conv_taps(rows_ref, halo_ref)
    conv_out = sum(prm_ref[k : k + 1, :] * taps[k] for k in range(WIDTH))
    sig_a, sig_x, decays, root = gates(conv_out, gate_ref, prm_ref)
    rows = lax.broadcasted_iota(jnp.int32, decays.shape, 0)
    grad = local_ref[0] + cum_ref[0] * ends_ref[0, 0:1, :]
    before = jnp.where(rows >= 1, pltpu.roll(states_ref[0], 1, 0), ends_ref[0, 1:2, :])
    d_log = grad * before * decays - grad * sig_x * conv_out * (decays * decays / root)
    d_pre_a = d_log * (-8.0 * prm_ref[6:7, :]) * sig_a * (1.0 - sig_a)
    d_pre_x = grad * root * conv_out * sig_x * (1.0 - sig_x)
    nn, tn = ((1,), (0,)), ((0,), (0,))
    a_high, a_low = two_parts(d_pre_a)
    x_high, x_low = two_parts(d_pre_x)
    c_high, c_low = two_parts(conv_out)
    d_conv = grad * root * sig_x
    d_conv = d_conv + (dot(a_high, gate_ref[0], nn) + dot(a_low, gate_ref[0], nn))
    d_conv = d_conv + (dot(x_high, gate_ref[1], nn) + dot(x_low, gate_ref[1], nn))
    d_conv_ref[0] = d_conv
    d_gate_a = dot(a_high, c_high, tn) + dot(a_low, c_high, tn) + dot(a_high, c_low, tn)
    d_gate_x = dot(x_high, c_high, tn) + dot(x_low, c_high, tn) + dot(x_high, c_low, tn)
    total = lambda v: jnp.sum(v, axis=0, keepdims=True)
    sums = [total(d_conv * taps[k]) for k in range(WIDTH)]
    sums += [total(d_pre_a), total(d_pre_x), total(d_log * (-8.0 * sig_a))]
    sums.append(jnp.zeros_like(sums[0]))
    d_prm = jnp.concatenate(sums, axis=0)
    first = pl.program_id(1) == 0

    @pl.when(first)
    def _():
        d_gate_ref[0] = d_gate_a
        d_gate_ref[1] = d_gate_x
        d_prm_ref[...] = d_prm

    @pl.when(jnp.logical_not(first))
    def _():
        d_gate_ref[0] += d_gate_a
        d_gate_ref[1] += d_gate_x
        d_prm_ref[...] += d_prm


def head_specs(tok):
    rows = pl.BlockSpec((1, tok, HD), lambda h, q: (q, 0, h))
    halo = pl.BlockSpec((1, HALO, HD), lambda h, q: (q, 0, h))
    prm = pl.BlockSpec((8, HD), lambda h, q: (0, h))
    gate = pl.BlockSpec((2, HD, HD), lambda h, q: (0, h, 0))
    ends = pl.BlockSpec((1, 8, HD), lambda h, q: (q, 0, h))
    return rows, halo, prm, gate, ends


PARAMS = dict(vmem_limit_bytes=48 * 1024 * 1024)
COST = pl.CostEstimate(flops=0, bytes_accessed=0, transcendentals=0)


def forward_call(branch_x, halo, prm, gate):
    seqs, tok, half = branch_x.shape
    rows_s, halo_s, prm_s, gate_s, _ = head_specs(tok)
    out = jax.ShapeDtypeStruct(branch_x.shape, F32)
    return pl.pallas_call(
        forward_kernel,
        grid=(half // HD, seqs),
        in_specs=[rows_s, halo_s, prm_s, gate_s],
        out_specs=[rows_s] * 3,
        out_shape=[out] * 3,
        compiler_params=pltpu.CompilerParams(**PARAMS),
        cost_estimate=COST,
        name="recurrence_forward",
    )(branch_x, halo, prm, gate)


def back_scan_call(d_mixed, branch_y, states, decays):
    seqs, tok, half = d_mixed.shape
    rows_s = head_specs(tok)[0]
    out = jax.ShapeDtypeStruct(d_mixed.shape, F32)
    return pl.pallas_call(
        back_scan_kernel,
        grid=(half // HD, seqs),
        in_specs=[rows_s] * 4,
        out_specs=[rows_s] * 3,
        out_shape=[jax.ShapeDtypeStruct(d_mixed.shape, BF), out, out],
        compiler_params=pltpu.CompilerParams(**PARAMS),
        cost_estimate=COST,
        name="recurrence_back_scan",
    )(d_mixed, branch_y, states, decays)


def backward_call(branch_x, halo, prm, gate, local, cum, ends, states):
    seqs, tok, half = branch_x.shape
    rows_s, halo_s, prm_s, gate_s, ends_s = head_specs(tok)
    return pl.pallas_call(
        backward_kernel,
        grid=(half // HD, seqs),
        in_specs=[rows_s, halo_s, prm_s, gate_s, rows_s, rows_s, ends_s, rows_s],
        out_specs=[rows_s, gate_s, prm_s],
        out_shape=[
            jax.ShapeDtypeStruct(branch_x.shape, F32),
            jax.ShapeDtypeStruct(gate.shape, F32),
            jax.ShapeDtypeStruct(prm.shape, F32),
        ],
        compiler_params=pltpu.CompilerParams(**PARAMS),
        cost_estimate=COST,
        name="recurrence_backward",
    )(branch_x, halo, prm, gate, local, cum, ends, states)


def place_kernel(plan, count_in, *refs):
    index = {axis: lax.axis_index(axis) for axis in ("z", "x", "y", "c")}
    for source, start, size, out, target in plan:
        refs[count_in + out][target(index)] = refs[source][:, start : start + size]


def place(plan, pieces, outs, name):
    whole = pl.BlockSpec(memory_space=pltpu.VMEM)
    return pl.pallas_call(
        functools.partial(place_kernel, plan, len(pieces)),
        in_specs=[whole] * len(pieces),
        out_specs=[whole] * len(outs),
        out_shape=[jax.ShapeDtypeStruct(shape, BF) for shape in outs],
        cost_estimate=COST,
        compiler_params=pltpu.CompilerParams(**PARAMS),
        name=name,
    )(*pieces)


def rows_at(block, share, offset=None, size=None):
    def target(index):
        rows = pl.ds(pl.multiple_of(block(index) * share, 16), share)
        if size is None:
            return rows, slice(None)
        return rows, pl.ds(offset(index), size)

    return target


def home_kernel(zn, fold, count, cols_ff, *refs):
    lanes = 128
    for far in range(count):
        start = lax.rem(lax.axis_index("z") - far + zn, zn) * fold
        for j in range(fold // lanes):
            at = start + j * lanes

            @pl.when(at < cols_ff)
            def _(far=far, j=j, at=at):
                dest = pl.ds(pl.multiple_of(at, lanes), lanes)
                for n in range(3):
                    col = n * fold + j * lanes
                    refs[count + n][:, dest] = refs[far][:, col : col + lanes].astype(F32)


def place_feed_forward_grads(pieces, rows_ff, cols_ff, fold, zn):
    whole = pl.BlockSpec(memory_space=pltpu.VMEM)
    return pl.pallas_call(
        functools.partial(home_kernel, zn, fold, len(pieces), cols_ff),
        in_specs=[whole] * len(pieces),
        out_specs=[whole] * 3,
        out_shape=[jax.ShapeDtypeStruct((rows_ff, cols_ff), F32)] * 3,
        cost_estimate=COST,
        compiler_params=pltpu.CompilerParams(**PARAMS),
        name="place_feed_forward_grads",
    )(*pieces)


TN = ((0,), (0,))


def split_blocks(whole_ref, keep_ref, give_ref, share, mine):
    for j in range(4):
        ours = pl.multiple_of((2 * j + mine) * share, 8)
        theirs = pl.multiple_of((2 * j + 1 - mine) * share, 8)
        keep_ref[0, j] = whole_ref[pl.ds(ours, share), :]
        give_ref[0, j] = whole_ref[pl.ds(theirs, share), :].astype(BF)


def yo_kernel(share, where_ref, normed_ref, mixed_ref, d_y_ref, d_out_ref, keep_ref, give_ref, whole_ref):
    half = d_y_ref.shape[1]
    whole_ref[:, :half] = dot(normed_ref[...], d_y_ref[...], TN)
    whole_ref[:, half:] = dot(mixed_ref[...], d_out_ref[...], TN)
    split_blocks(whole_ref, keep_ref, give_ref, share, where_ref[1])


def xg_kernel(share, where_ref, normed_ref, d_gate_ref, d_x_ref, keep_ref, give_ref, whole_ref):
    half = d_x_ref.shape[1]
    whole_ref[:, :half] = dot(normed_ref[...], d_x_ref[...], TN)
    whole_ref[:, half:] = d_gate_ref[0]
    split_blocks(whole_ref, keep_ref, give_ref, share, where_ref[1])


def term_call(kernel, where, specs, args, first, count, share, columns, name):
    block = pl.BlockSpec((1, 4, share, columns), lambda n, where: (n, 0, 0, 0))
    return pl.pallas_call(
        functools.partial(kernel, share),
        grid_spec=pltpu.PrefetchScalarGridSpec(
            num_scalar_prefetch=1,
            grid=(count,),
            in_specs=specs,
            out_specs=[block, block],
            scratch_shapes=[pltpu.VMEM((8 * share, columns), F32)],
        ),
        out_shape=[
            jax.ShapeDtypeStruct((count, 4, share, columns), F32),
            jax.ShapeDtypeStruct((count, 4, share, columns), BF),
        ],
        cost_estimate=COST,
        compiler_params=pltpu.CompilerParams(**PARAMS),
        name=name,
    )(where, *args)


def ff_kernel(steps, fold, where_ref, *refs):
    rows, cots, hidden, d_gu = (refs[n * steps : (n + 1) * steps] for n in range(4))
    keep_ref, give_ref, whole_ref = refs[4 * steps :]
    first = second = 0.0
    for k in range(steps):
        first = first + dot(rows[k][...], d_gu[k][...], TN)
        second = second + dot(cots[k][...], hidden[k][...], TN)
    whole_ref[:, : 2 * fold] = first
    whole_ref[:, 2 * fold :] = second
    size = keep_ref.shape[1]
    mine = where_ref[2]
    keep_ref[0] = whole_ref[pl.ds(pl.multiple_of(mine * size, 8), size), :]
    give_ref[0] = whole_ref[pl.ds(pl.multiple_of((1 - mine) * size, 8), size), :].astype(BF)


def ff_grads_call(where, rows, cots, hidden, d_gu, zn, rows_ff):
    steps, fold = len(rows), hidden[0].shape[1]
    count = rows[0].shape[0]
    part = pl.BlockSpec((count, 2 * rows_ff), lambda far, where: (0, lax.rem(where[0] + far, zn)))
    whole = lambda item: pl.BlockSpec(item.shape, lambda far, where: (0, 0))
    block = pl.BlockSpec((1, rows_ff, 3 * fold), lambda far, where: (far, 0, 0))
    shape = (zn, rows_ff, 3 * fold)
    return pl.pallas_call(
        functools.partial(ff_kernel, steps, fold),
        grid_spec=pltpu.PrefetchScalarGridSpec(
            num_scalar_prefetch=1,
            grid=(zn,),
            in_specs=[part] * (2 * steps) + [whole(item) for item in (*hidden, *d_gu)],
            out_specs=[block, block],
            scratch_shapes=[pltpu.VMEM((2 * rows_ff, 3 * fold), F32)],
        ),
        out_shape=[jax.ShapeDtypeStruct(shape, F32), jax.ShapeDtypeStruct(shape, BF)],
        cost_estimate=COST,
        compiler_params=pltpu.CompilerParams(**PARAMS),
        name="feed_forward_grads",
    )(where, *rows, *cots, *hidden, *d_gu)


def carried(decay, drive, zn, x, by):
    own = jnp.stack([decay, drive])
    beside = swap(own, "x")
    inner = x == 0 if by > 0 else x == 1
    near, far = pick(inner, own, beside), pick(inner, beside, own)
    pair = jnp.stack([near[0] * far[0], near[1] * far[0] + far[1]])
    came = [shifted(pair, "z", by * dist, zn) for dist in range(zn - 1, 0, -1)]
    state = jnp.zeros_like(drive)
    for part in came:
        state = part[0] * state + part[1]
    return pick(inner, state, near[0] * state + near[1])


def per_device(
    zn, fold,
    tokens, w_x, w_y, w_out, gate_w, gain_in, gain_mlp, conv_w, gate_b, rate,
    w_gate, w_up, w_down, cotangent,
):
    z, x, y, c = (lax.axis_index(axis) for axis in ("z", "x", "y", "c"))
    zh = zn // 2
    seq_count = 2 * zn
    tok, width = tokens.shape[1], tokens.shape[2]
    share, wide_r = w_x.shape
    half = wide_r // 2
    rows_ff, cols_ff = w_gate.shape
    zx, zy = ("z", "x"), ("z", "y")
    z_of = [lax.rem(z - k + zn, zn) for k in range(zn)]
    lanes = 128
    every = range(zn)
    hop = lambda value: shifted(value, "z", 1, zn, True)

    spread = []
    for other in (0, 1):
        pairs = []
        for h in (0, 1):
            for zl in range(zh):
                for ys in (0, 1):
                    k = ys ^ other
                    pairs.append(((h * zh + zl) * 2 + ys, (k * zh + zl) * 2 + h))
        spread.append(pairs)
    gathered_back = [[(b, a) for a, b in pairs] for pairs in spread]
    own_half = lambda w: pick(y == 0, w[:, :half], w[:, half:])
    other_half = lambda w: pick(y == 0, w[:, half:], w[:, :half])

    def source(k, across, other):
        def at(i):
            flip = lambda value, on: 1 - value if on else value
            return lax.rem(i["z"] - k + zn, zn), flip(i["x"], across), flip(i["c"], other)

        return at

    def by_rows(at, beside):
        def block(i):
            sz, sx, sc = at(i)
            return ((sz * 2 + sx) * 2 + (1 - i["y"] if beside else i["y"])) * 2 + sc

        return block

    def by_spread(at, second):
        def block(i):
            sz, sx, sc = at(i)
            sh = sz // zh
            return ((lax.rem(sz, zh) * 2 + sx) * 2 + (1 - sh if second else sh)) * 2 + sc

        return block

    def gate_at(at, second):
        rows = by_spread(at, second)

        def target(i):
            start = pl.multiple_of(rows(i) * share, 16)
            return at(i)[0] // zh, pl.ds(start, share), slice(None)

        return target

    params = jnp.concatenate([gain_in[None], gain_mlp[None], conv_w, gate_b, rate[None]])
    count_p = params.shape[0]
    params = jnp.pad(params.T, ((0, 0), (0, lanes - count_p)))
    gate_t = gate_w.transpose(0, 2, 1)
    gate_pieces = [
        lax.ppermute(pick(y == 0, gate_t[k], gate_t[1 - k]), zy, spread[k]) for k in (0, 1)
    ]
    wide_x = half + lanes
    x_own = jnp.concatenate([own_half(w_x), params], axis=1)
    x_other = swap(jnp.concatenate([other_half(w_x), params], axis=1), "y")
    unit_x = jnp.concatenate([x_own, x_other, gate_pieces[0], gate_pieces[1]], axis=1)
    tok_own, cot = tokens[0], cotangent[0]
    cot_z, cot_y = [cot], {}
    unit_x, w_y, w_out, tok_own, ff_raw = tick(unit_x, w_y, w_out, tok_own, (w_gate, w_up, w_down))

    a_z, a_x, a_zc, a_xc = [unit_x], [], [], []
    padded = zn * fold
    widen = lambda w: jnp.pad(w, ((0, 0), (0, padded - cols_ff)))
    ff_wide = [widen(ff_raw[0]), widen(ff_raw[1]), widen(ff_raw[2].T)]

    def ff_piece(z_at):
        return jnp.concatenate(
            [lax.dynamic_slice_in_dim(w, z_at * fold, fold, 1) for w in ff_wide], axis=1
        )

    ff_units = [ff_piece(lax.rem(z + far, zn)) for far in every]
    for k in range(1, zn):
        a_z.append(hop(a_z[-1]))
        a_x.append(swap(a_z[k - 1], "x"))
        a_zc.append(swap(a_z[k - 1], "c"))
        if k > 1:
            a_xc.append(swap(a_x[k - 2], "c"))
        if k == 1:
            tok_other = swap(tok_own, "y")
            a_z, a_x, w_y, w_out, tok_own = tick(a_z, a_x, w_y, w_out, tok_own)
            y_other = swap(other_half(w_y), "y")
            out_halves = [w_out[:, :half], w_out[:, half:]]
            out_parts = [
                lax.ppermute(pick(y == 0, out_halves[i], out_halves[1 - i]), zy, spread[i])
                for i in (0, 1)
            ]
        elif k == 2:
            a_z, a_x, tok_own, tok_other, y_other, out_parts = tick(
                a_z, a_x, tok_own, tok_other, y_other, out_parts
            )
        else:
            a_z, a_x = tick(a_z, a_x)
    tok_f = jnp.stack([tok_own, tok_other]).astype(F32)
    unit_yo = jnp.concatenate([own_half(w_y), y_other, out_parts[0], out_parts[1]], axis=1)
    unit_yo, a_z = tick(unit_yo, a_z)

    b_z, b_x, b_zc, b_xc = [unit_yo, hop(unit_yo)], [], [], []
    a_x.append(swap(a_z[-1], "x"))
    a_zc.append(swap(a_z[-1], "c"))
    a_xc.append(swap(a_x[-2], "c"))
    a_x, a_zc, a_xc, unit_yo, ff_units = tick(a_x, a_zc, a_xc, b_z[0], ff_units)
    b_z[0] = unit_yo
    a_xc.append(swap(a_x[-1], "c"))
    b_x.append(swap(b_z[0], "x"))
    placed, plan = [], []
    for k in every:
        for j, part in enumerate((a_z[k], a_zc[k], a_x[k], a_xc[k])):
            at = source(k, j >= 2, j % 2)
            n = len(placed)
            placed.append(part)
            for beside in (0, 1):
                block = by_rows(at, beside)
                plan.append((n, beside * wide_x, half, 0, rows_at(block, share)))
                plan.append((n, beside * wide_x + half, lanes, 1, rows_at(block, share)))
                plan.append((n, 2 * wide_x + beside * HD, HD, 2, gate_at(at, beside)))
    full_x, full_p, gates_t = place(
        plan, placed, [(width, half), (width, lanes), (2, half, HD)], "place_w_x"
    )
    smalls = full_p[:, :count_p].astype(F32).T
    gain_first, gain_second = smalls[0], smalls[1]
    prm = jnp.pad(smalls[2:], ((0, 1), (0, 0)))
    prm = pick(y == 0, prm[:, :half], prm[:, half:])
    normed = rms_scale(tok_f, gain_first).astype(BF).reshape(2 * tok, width)
    branch_x = product(normed, full_x).astype(BF).reshape(2, tok, half)

    branch_x, b_z = tick(branch_x, b_z)
    b_z.append(hop(b_z[-1]))
    b_x.append(swap(b_z[1], "x"))
    b_zc += [swap(b_z[0], "c"), swap(b_z[1], "c")]
    halo = shifted(branch_x[:, tok - HALO :], zx, 1, seq_count)
    halo, b_z, b_x = tick(halo, b_z, b_x)
    for k in range(3, zn):
        b_z.append(hop(b_z[-1]))
        b_x.append(swap(b_z[k - 1], "x"))
        b_zc.append(swap(b_z[k - 1], "c"))
        b_xc.append(swap(b_x[k - 3], "c"))
        if k == 3:
            decays, local, cum = tick(*forward_call(branch_x, halo, prm, gates_t))
            state_in = carried(cum[:, -1], local[:, -1], zn, x, 1)
            state_in, b_z, b_x = tick(state_in, b_z, b_x)
        else:
            b_z, b_x = tick(b_z, b_x)
    turns = [
        [(far, None) for far in range(1, zn) if far % 3 == 1],
        [(far, 0) for far in range(1, zn) if far % 3 == 2],
        [(far, 1) for far in range(1, zn) if far % 3 == 2],
        [(far, None) for far in range(1, zn) if far % 3 == 0],
    ]

    def sent_along(blocks, turn):
        sent = {}
        for far, part in turns[turn]:
            block = blocks[far]
            cut = block.shape[1] // 2
            if part is not None:
                block = block[:, :cut] if part == 0 else block[:, cut:]
            sent[far, part] = shifted(block, "z", far, zn, True)
        return sent

    def joined(came, fars):
        return {
            far: came[far, None] if (far, None) in came
            else jnp.concatenate([came[far, 0], came[far, 1]], axis=1)
            for far in fars
        }

    far_of = lambda turn: [far for far, _ in turns[turn]]
    ff_units, b_z = tick(ff_units, b_z)
    ff_came, ff_x = sent_along(ff_units, 0), {}
    b_x.append(swap(b_z[-1], "x"))
    b_zc.append(swap(b_z[-1], "c"))
    b_xc += [swap(b_x[-3], "c"), swap(b_x[-2], "c")]
    b_x, cot_z, cot_y, ff_units, ff_came = tick(b_x, cot_z, cot_y, ff_units, ff_came)

    ff_came.update(sent_along(ff_units, 1))
    ff_x[0] = swap(ff_units[0], "x")
    cot_y[0] = swap(cot_z[0], "y")
    b_xc.append(swap(b_x[-1], "c"))
    placed, plan = [], []
    for k in every:
        for j, part in enumerate((b_z[k], b_zc[k], b_x[k], b_xc[k])):
            at = source(k, j >= 2, j % 2)
            n = len(placed)
            placed.append(part)
            column = lambda i, at=at: pl.multiple_of((at(i)[0] // zh) * half, lanes)
            for beside in (0, 1):
                plan.append((n, beside * half, half, 0, rows_at(by_rows(at, beside), share)))
                plan.append(
                    (n, (2 + beside) * half, half, 1, rows_at(by_spread(at, beside), share, column, half))
                )
    full_y, full_out = place(plan, placed, [(width, half), (half, width)], "place_w_y_w_out")
    branch_y = product(normed, full_y).reshape(2, tok, half)
    states = local + cum * state_in[:, None]
    mixed = (states * gelu_tanh(branch_y)).astype(BF).reshape(2 * tok, half)
    out_sum = product(mixed, full_out)
    out_own, out_give = out_sum[:tok], out_sum[tok:].astype(BF)
    out_own, out_give, ff_came, ff_x, ff_units, cot_z, cot_y = tick(
        out_own, out_give, ff_came, ff_x, ff_units, cot_z, cot_y
    )
    out_came = swap(out_give, "y")
    ff_came.update(sent_along(ff_units, 2))
    ff_x.update({far: swap(piece, "x") for far, piece in joined(ff_came, far_of(0)).items()})
    cot_z.append(hop(cot_z[0]))
    out_came, out_own, ff_came, ff_x, ff_units, cot_z = tick(
        out_came, out_own, ff_came, ff_x, ff_units, cot_z
    )
    residual = tok_own.astype(F32) + out_own + out_came.astype(F32)
    normed_mlp = rms_scale(residual, gain_second).astype(BF)

    row_z, row_y = [normed_mlp, hop(normed_mlp)], {0: swap(normed_mlp, "y")}
    ff_came.update(sent_along(ff_units, 3))
    ff_x.update({far: swap(piece, "x") for far, piece in joined(ff_came, far_of(1)).items()})
    cot_y[1] = swap(cot_z[1], "y")
    row_z, row_y, cot_z, cot_y, ff_came, ff_x = tick(row_z, row_y, cot_z, cot_y, ff_came, ff_x)
    ff_x.update({far: swap(piece, "x") for far, piece in joined(ff_came, far_of(3)).items()})
    row_z.append(hop(row_z[-1]))
    cot_z.append(hop(cot_z[-1]))
    row_y[1] = swap(row_z[1], "y")
    row_z, row_y, cot_z, ff_x = tick(row_z, row_y, cot_z, ff_x)
    ff_pieces = joined(ff_came, range(1, zn))
    ff_pieces[0] = ff_units[0]
    placed, plan = [], []
    for k in every:
        for across, part in enumerate((ff_pieces[k], ff_x[k])):
            at = source(k, across, 0)
            block = lambda i, at=at: at(i)[0] * 2 + at(i)[1]
            n = len(placed)
            placed.append(part)
            plan.append((n, 0, 2 * fold, 0, rows_at(block, rows_ff)))
            plan.append((n, 2 * fold, fold, 1, rows_at(block, rows_ff)))
    w_gu, w_dt = place(plan, placed, [(width, 2 * fold), (width, fold)], "place_feed_forward")

    def with_cores(pair):
        return jnp.concatenate(list(pair) + [swap(part, "c") for part in pair])

    def feed_forward(k):
        rows, grads = with_cores((row_z[k], row_y[k])), with_cores((cot_z[k], cot_y[k]))
        gu = product(rows, w_gu)
        d_hidden = product(grads, w_dt)
        hidden, pull = jax.vjp(gated_product, gu[:, :fold], gu[:, fold:])
        d_gu = jnp.concatenate([item.astype(BF) for item in pull(d_hidden)], axis=1)
        return rows, grads, hidden.astype(BF), d_gu, product_t(d_gu, w_gu).reshape(4, tok, width)

    steps, d_parts, d_c, d_y, total = {}, {}, {}, {}, None
    m_parts, m_c, m_y, m_total = {}, {}, {}, None

    def core_give(parts):
        return parts[2:].astype(BF)

    def y_give(parts, came_c):
        return (parts[1] + came_c[1].astype(F32)).astype(BF)

    def own_sum(parts, came_c, came_y):
        return parts[0] + came_c[0].astype(F32) + came_y.astype(F32)

    where = jnp.stack([z, c, x]).astype(jnp.int32)
    order = list(range(1, zn)) + [0]
    for i in range(zn + 2):
        if i < zn:
            k = order[i]
            steps[k] = feed_forward(k)
            d_parts[k] = steps[k][-1]
        if k + 2 < zn and i < zn - 1:
            row_z.append(hop(row_z[-1]))
        if k + 2 < zn and i < zn - 1:
            cot_z.append(hop(cot_z[-1]))
        if i < zn - 2:
            row_y[k + 1] = swap(row_z[k + 1], "y")
            cot_y[k + 1] = swap(cot_z[k + 1], "y")
        if i < 2 or i == zn + 1:
            for n in [k] if i < 2 else order[2:]:
                m_parts[n] = product_t(steps[n][2], w_dt).reshape(4, tok, width)
        if 1 <= i <= 2:
            m_c[order[i - 1]] = swap(core_give(m_parts[order[i - 1]]), "c")
        if 1 <= i <= zn:
            d_c[order[i - 1]] = swap(core_give(d_parts[order[i - 1]]), "c")
        if 2 <= i:
            k = order[i - 2]
            d_y[k] = swap(y_give(d_parts[k], d_c[k]), "y")
        if 3 <= i:
            k = order[i - 3]
            term = own_sum(d_parts[k], d_c[k], d_y[k])
            total = hop((term if total is None else total.astype(F32) + term).astype(BF))
        if i in (2, 4):
            k = order[i // 2 - 1]
            m_y[k] = swap(y_give(m_parts[k], m_c[k]), "y")
        if i == 4:
            m_total = hop(own_sum(m_parts[1], m_c[1], m_y[1]).astype(BF))
        if i == zn:
            ff_keep, ff_give = tick(*ff_grads_call(
                where, *([steps[k][n] for k in every] for n in range(4)), zn, rows_ff
            ))
            ff_give = {far: ff_give[far] for far in every}
        if i == zn + 1:
            break
        steps, row_z, row_y, cot_z, cot_y, d_parts, d_c, d_y, total, m_parts, m_c, m_y, m_total = tick(
            steps, row_z, row_y, cot_z, cot_y, d_parts, d_c, d_y, total, m_parts, m_c, m_y, m_total
        )
        steps = {k: step[:4] for k, step in steps.items()}

    ff_sent, ff_home = {}, {}

    def cut_block(block, part):
        middle = 3 * fold // 2
        return block if part is None else block[:, :middle] if part == 0 else block[:, middle:]

    def give_across(turn):
        for far, part in turn:
            ff_sent[far, part] = swap(cut_block(ff_give[far], part), "x")

    def own_and_sent(far, part):
        return (cut_block(ff_keep[far], part) + ff_sent[far, part].astype(F32)).astype(BF)

    def send_home(turn):
        for far, part in turns[turn]:
            ff_home[far, part] = shifted(own_and_sent(far, part), "z", far, zn, True)

    give_across(turns[3] + turns[1])
    total, d_y, ff_sent, ff_give, m_total, m_parts = tick(total, d_y, ff_sent, ff_give, m_total, m_parts)

    d_normed_mlp = own_sum(d_parts[0], d_c[0], d_y[0]) + total.astype(F32)
    unused, second_pull = jax.vjp(rms_scale, residual, gain_second)
    d_res_norm, d_gain_mlp = second_pull(d_normed_mlp)
    d_residual = cot.astype(F32) + d_res_norm
    d_branch = d_residual.astype(BF)
    d_other = swap(d_branch, "y")
    send_home(3)
    give_across(turns[2])
    for k in order[2:]:
        m_c[k] = swap(core_give(m_parts[k]), "c")
    d_branch, d_other, ff_sent, ff_give, m_total, m_c = tick(d_branch, d_other, ff_sent, ff_give, m_total, m_c)

    d_branch_pair = jnp.concatenate([d_branch, d_other])
    d_mixed = product_t(d_branch_pair, full_out).reshape(2, tok, half)
    d_branch_y, local_back, cum_back = back_scan_call(d_mixed, branch_y, states, decays)
    leaving = decays[:, 0] * local_back[:, 0]
    for k in order[2:]:
        m_y[k] = swap(y_give(m_parts[k], m_c[k]), "y")
    send_home(1)
    give_across(turns[0])
    d_flat_y = d_branch_y.reshape(2 * tok, half)
    eight = 8 * share
    z_at = lambda n, where, first: lax.rem(where[0] - n - first + 2 * zn, zn)
    full_spec = pl.BlockSpec((2 * tok, half), lambda n, where: (0, 0))

    def yo_terms(first, count):
        specs = [
            pl.BlockSpec((2 * tok, eight), lambda n, where: (0, z_at(n, where, first))),
            pl.BlockSpec((2 * tok, eight), lambda n, where: (0, lax.rem(z_at(n, where, first), zh))),
            full_spec,
            pl.BlockSpec((2 * tok, half), lambda n, where: (0, z_at(n, where, first) // zh)),
        ]
        args = (normed, mixed, d_flat_y, d_branch_pair)
        return term_call(yo_kernel, where, specs, args, first, count, share, 2 * half, "grad_w_y_w_out")

    def x_terms(first, count):
        specs = [
            pl.BlockSpec((2 * tok, eight), lambda n, where: (0, z_at(n, where, first))),
            pl.BlockSpec(
                (1, eight, HD),
                lambda n, where: (z_at(n, where, first) // zh, lax.rem(z_at(n, where, first), zh), 0),
            ),
            full_spec,
        ]
        args = (normed, d_gates, d_flat_x)
        return term_call(xg_kernel, where, specs, args, first, count, share, half + HD, "grad_w_x")

    yo_a = yo_terms(1, 2)
    leaving, d_branch_y, yo_a, m_y, m_total, ff_home, ff_sent, ff_give = tick(
        leaving, d_branch_y, yo_a, m_y, m_total, ff_home, ff_sent, ff_give
    )

    carry_back = carried(cum[:, -1], leaving, zn, x, -1)
    ends = jnp.pad(jnp.stack([carry_back, state_in], axis=1), ((0, 0), (0, 6), (0, 0)))
    yo_ac = swap(yo_a[1], "c")
    ends, yo_a, yo_ac, d_flat_y, ff_sent, ff_give, m_y, m_total = tick(
        ends, yo_a, yo_ac, d_flat_y, ff_sent, ff_give, m_y, m_total
    )

    yo, xg = {}, {}

    def hold(terms, kept, came, first):
        for n in range(came.shape[0]):
            terms[(first + n) % zn] = (kept, came, n)

    def at_x(term, which):
        kept, came, n = term
        part = lambda v: lax.dynamic_slice(
            v.reshape((-1, 2, 2) + v.shape[2:]), (n, which, 0, 0, 0), (1, 1, 2) + v.shape[2:]
        )[0, 0]
        return part(kept) + part(came).astype(F32)

    def x_give(term):
        return at_x(term, 1 - x).astype(BF)

    hold(yo, yo_a[0], yo_ac, 1)
    yo_x = {1: swap(x_give(yo[1]), "x")}
    send_home(2)
    d_conv, d_gates, d_prm = tick(*backward_call(
        branch_x, halo, prm, gates_t, local_back, cum_back, ends, states
    ))
    rim = shifted(d_conv[:, :8], zx, -1, seq_count)
    yo_b = yo_terms(3, zn - 2)
    rim, yo_x, yo_b, ff_home, ff_sent, ff_give, m_total, m_y = tick(
        rim, yo_x, yo_b, ff_home, ff_sent, ff_give, m_total, m_y
    )
    yo_bc = swap(yo_b[1], "c")

    d_ext = jnp.concatenate([d_conv, rim], axis=1)
    d_branch_x = sum(prm[k] * d_ext[:, k : k + tok] for k in range(WIDTH)).astype(BF)
    d_flat_x = d_branch_x.reshape(2 * tok, half)

    def add(total, terms, came_x, k):
        return total.astype(F32) + at_x(terms[k], x) + came_x[k].astype(F32)

    def return_rows(sums):
        mine = z // zh
        return [
            lax.ppermute(
                lax.dynamic_index_in_dim(sums, mine if k == 0 else 1 - mine, 0, False).astype(BF),
                zy, gathered_back[k],
            )
            for k in (0, 1)
        ]

    def returned_rows(came):
        came = [item.astype(F32) for item in came]
        return pick(y == 0, came[0], came[1]), pick(y == 0, came[1], came[0])

    def return_columns(sums):
        return swap(lax.dynamic_index_in_dim(sums, 1 - y, 0, False).astype(BF), "y")

    def returned_columns(sums, came):
        mine, across = lax.dynamic_index_in_dim(sums, y, 0, False), came.astype(F32)
        return jnp.concatenate([pick(y == 0, mine, across), pick(y == 0, across, mine)], axis=1)

    xg_x, xg_total = {}, None
    zero = jnp.zeros((), F32)
    yo_total = add(zero, yo, yo_x, 1)
    for t in range(zn + 1):
        if t < zn - 1:
            if t == 0:
                yo_total = hop(yo_total.astype(BF))
            else:
                k = order[t]
                m_total = m_total.astype(F32) + own_sum(m_parts[k], m_c[k], m_y[k])
                rows = 2 * share
                both = jnp.concatenate([yo_total.astype(BF).reshape(rows, -1), m_total.astype(BF)])
                both = hop(both)
                yo_total, m_total = both[:rows].reshape(2, share, -1), both[rows:]
            k = order[t + 1]
            yo_x[k] = swap(x_give(yo[k]), "x")
        if t >= 2:
            xg_total = hop(xg_total.astype(BF))
        if t in (1, 2):
            pair = order[:2] if t == 1 else order[2:]
            came = swap(jnp.stack([x_give(xg[k]) for k in pair]), "x")
            xg_x.update({k: came[i] for i, k in enumerate(pair)})
        if t == 0:
            send_home(0)
            xg_a = x_terms(1, zn)
            xg_ac = swap(xg_a[1], "c")
        elif t == 1:
            d_normed = product_t(d_flat_x, full_x) + product_t(d_flat_y, full_y)
            d_came = swap(d_normed[tok:].astype(BF), "y")
        elif t == 2:
            unused, first_pull = jax.vjp(rms_scale, tok_own.astype(F32), gain_first)
            d_tok, d_gain_in = first_pull(d_normed[:tok] + d_came.astype(F32))
            tokens_grad = (d_residual + d_tok)[None]
            small = jnp.concatenate([d_prm, jnp.stack([d_gain_in, d_gain_mlp]).reshape(4, half)])
            small = small + swap(small, "c")
        elif t == 3:
            small = small + swap(small, "x")
            give_across([(0, None)])
        if t == zn - 1:
            out_came = return_rows(yo_total[:, :, half:])
        if t == zn:
            y_came = return_columns(yo_total[:, :, :half])
        if t == zn:
            small = small + sum(shifted(small, "z", by, zn, True) for by in range(1, zn))
            ff_home = joined(ff_home, range(1, zn))
            ff_home[0] = own_and_sent(0, None)
            g_gate, g_up, g_down = place_feed_forward_grads(
                [ff_home[far] for far in every], rows_ff, cols_ff, fold, zn,
            )
        if t == 0:
            yo_x, yo_total, xg_a, xg_ac, yo_bc, d_flat_y = tick(
                yo_x, yo_total, xg_a, xg_ac, yo_bc, d_flat_y
            )
            hold(yo, yo_b[0], yo_bc, 3)
            hold(xg, xg_a[0], xg_ac, 1)
        elif t == 1:
            yo_x, yo_total, xg_x, d_normed, d_came, ff_home, m_total, xg_a, xg_ac, ff_give = tick(
                yo_x, yo_total, xg_x, d_normed, d_came, ff_home, m_total, xg_a, xg_ac, ff_give
            )
            hold(xg, xg_a[0], xg_ac, 1)
            xg_total = add(zero, xg, xg_x, 1)
        elif t < zn:
            if t == 2:
                yo_x, yo_total, xg_x, xg_total, small, m_total = tick(
                    yo_x, yo_total, xg_x, xg_total, small, m_total
                )
                m_term = own_sum(m_parts[0], m_c[0], m_y[0])
                result = (residual + m_total.astype(F32) + m_term).astype(BF)[None]
            else:
                yo_total, xg_x, xg_total, small, out_came, ff_sent = tick(
                    yo_total, xg_x, xg_total, small, out_came, ff_sent
                )
        else:
            xg_x, xg_total, small, y_came, out_came, yo_total = tick(
                xg_x, xg_total, small, y_came, out_came, yo_total
            )
        if t >= 2:
            xg_total = add(xg_total, xg, xg_x, order[t - 1])
        if t < zn - 1:
            yo_total = add(yo_total, yo, yo_x, order[t + 1])
    grad_w_x = returned_columns(xg_total[:, :, :half], return_columns(xg_total[:, :, :half]))
    grad_gate_w = jnp.stack(returned_rows(return_rows(xg_total[:, :, half:]))).transpose(0, 2, 1)
    grad_w_y = returned_columns(yo_total[:, :, :half], y_came)
    grad_w_out = jnp.concatenate(returned_rows(out_came), axis=1)

    beside = swap(small, "y")
    both_halves = jnp.concatenate(
        [pick(y == 0, small, beside)[:8], pick(y == 0, beside, small)[:8]], axis=1
    )
    gains = (small + beside)[8:].reshape(2, 2 * half)
    at = ((z * 2 + x) * 4 + y * 2 + c) * share
    own_small = lax.dynamic_slice_in_dim(both_halves, at, share, 1)
    own_gain = lax.dynamic_slice_in_dim(gains, at, share, 1)
    return (
        result,
        tokens_grad,
        grad_w_x,
        grad_w_y,
        grad_w_out,
        grad_gate_w,
        own_gain[0],
        own_gain[1],
        own_small[:WIDTH],
        own_small[WIDTH : WIDTH + 2],
        own_small[WIDTH + 2],
        g_gate,
        g_up,
        g_down.T,
    )


PRECISE = lax.Precision.HIGHEST


def passed_along(value, axis, by):
    devices = lax.axis_size(axis)
    pairs = [(i, i + by) for i in range(devices) if 0 <= i + by < devices]
    return lax.ppermute(value, axis, pairs)


def entering(value, axis, join, neutral, backward):
    count, mine = (lax.axis_size(axis), lax.axis_index(axis))
    pieces = jax.tree.map(lambda part: lax.all_gather(part, axis), value)
    if backward:
        pieces = jax.tree.map(lambda part: part[::-1], pieces)
        mine = count - 1 - mine
    total = jax.tree.map(
        lambda part, zero: jnp.full_like(part, 0) + jnp.asarray(zero, part.dtype), value, neutral
    )

    def step(position, total):
        longer = join(total, jax.tree.map(lambda part: part[position], pieces))
        return jax.tree.map(lambda new, old: jnp.where(position < mine, new, old), longer, total)

    return lax.fori_loop(0, count - 1, step, total)


def affine_pair(earlier, latter):
    return (earlier[0] * latter[0], earlier[1] * latter[0] + latter[1])


def causal_conv(extended, conv_full, tok_count):
    conv_out = conv_full[0] * extended[WIDTH - 1 : WIDTH - 1 + tok_count]
    for tap_index in range(1, WIDTH):
        conv_out = (
            conv_out
            + conv_full[tap_index]
            * extended[WIDTH - 1 - tap_index : WIDTH - 1 - tap_index + tok_count]
        )
    return conv_out


def recurrence_inputs(conv_out, gate_full, bias_full, rate_full):
    tok_count = conv_out.shape[0]
    blocks = gate_full.reshape(2, HD, HEADS, HD)
    grouped = conv_out.reshape(tok_count, HEADS, HD)
    pre_a = (
        jnp.einsum("thi,ihj->thj", grouped, blocks[0], precision=PRECISE).reshape(tok_count, -1)
        + bias_full[0]
    )
    pre_x = (
        jnp.einsum("thi,ihj->thj", grouped, blocks[1], precision=PRECISE).reshape(tok_count, -1)
        + bias_full[1]
    )
    log_decay = -8.0 * jax.nn.sigmoid(pre_a) * rate_full
    decays = jnp.exp(log_decay)
    drives = jnp.sqrt(-jnp.expm1(2.0 * log_decay)) * jax.nn.sigmoid(pre_x) * conv_out
    return (decays, drives)


def fetch_recurrent(w_x, w_y, w_out, gate_w, gain_in, gain_mlp, conv_w, gate_b, rate):
    return (
        lax.all_gather(w_x, ("seq", "fsdp"), axis=0, tiled=True),
        lax.all_gather(w_y, ("seq", "fsdp"), axis=0, tiled=True),
        lax.all_gather(w_out, ("seq", "fsdp"), axis=0, tiled=True),
        lax.all_gather(gate_w, ("seq", "fsdp"), axis=2, tiled=True),
        lax.all_gather(gain_in, ("seq", "fsdp"), axis=0, tiled=True),
        lax.all_gather(gain_mlp, ("seq", "fsdp"), axis=0, tiled=True),
        lax.all_gather(conv_w, ("seq", "fsdp"), axis=1, tiled=True),
        lax.all_gather(gate_b, ("seq", "fsdp"), axis=1, tiled=True),
        lax.all_gather(rate, ("seq", "fsdp"), axis=0, tiled=True),
    )


def fetch_feedforward(w_gate, w_up, w_down):
    return (
        lax.all_gather(w_gate, "seq", axis=0, tiled=True),
        lax.all_gather(w_up, "seq", axis=0, tiled=True),
        lax.all_gather(w_down, "seq", axis=1, tiled=True),
    )


def split_owner(values, dim, seq_count, pair_count):
    shape = values.shape
    share = shape[dim] // (seq_count * pair_count)
    return values.reshape(shape[:dim] + (seq_count, pair_count, share) + shape[dim + 1 :])


def merge_owner(values, dim):
    shape = values.shape
    return values.reshape(shape[:dim] + (shape[dim + 2],) + shape[dim + 3 :])


def sum_recurrent(grads):
    seq_count = lax.axis_size("seq")
    pair_count = lax.axis_size("fsdp")
    dims = (0, 0, 0, 2, 0, 0, 1, 1, 0)
    split = tuple((split_owner(item, dim, seq_count, pair_count) for item, dim in zip(grads, dims)))
    paired = (
        lax.psum_scatter(split[0], "fsdp", scatter_dimension=1, tiled=True),
        lax.psum_scatter(split[1], "fsdp", scatter_dimension=1, tiled=True),
        lax.psum_scatter(split[2], "fsdp", scatter_dimension=1, tiled=True),
        lax.psum_scatter(split[3], "fsdp", scatter_dimension=3, tiled=True),
        lax.psum_scatter(split[4], "fsdp", scatter_dimension=1, tiled=True),
        lax.psum_scatter(split[5], "fsdp", scatter_dimension=1, tiled=True),
        lax.psum_scatter(split[6], "fsdp", scatter_dimension=2, tiled=True),
        lax.psum_scatter(split[7], "fsdp", scatter_dimension=2, tiled=True),
        lax.psum_scatter(split[8], "fsdp", scatter_dimension=1, tiled=True),
    )
    summed = (
        lax.psum_scatter(paired[0], "seq", scatter_dimension=0, tiled=True),
        lax.psum_scatter(paired[1], "seq", scatter_dimension=0, tiled=True),
        lax.psum_scatter(paired[2], "seq", scatter_dimension=0, tiled=True),
        lax.psum_scatter(paired[3], "seq", scatter_dimension=2, tiled=True),
        lax.psum_scatter(paired[4], "seq", scatter_dimension=0, tiled=True),
        lax.psum_scatter(paired[5], "seq", scatter_dimension=0, tiled=True),
        lax.psum_scatter(paired[6], "seq", scatter_dimension=1, tiled=True),
        lax.psum_scatter(paired[7], "seq", scatter_dimension=1, tiled=True),
        lax.psum_scatter(paired[8], "seq", scatter_dimension=0, tiled=True),
    )
    return tuple((merge_owner(item, dim) for item, dim in zip(summed, dims)))


def per_device_gathered(
    tokens,
    w_x,
    w_y,
    w_out,
    gate_w,
    gain_in,
    gain_mlp,
    conv_w,
    gate_b,
    rate,
    w_gate,
    w_up,
    w_down,
    cotangent,
):
    gathered = fetch_recurrent(w_x, w_y, w_out, gate_w, gain_in, gain_mlp, conv_w, gate_b, rate)
    full_x, full_y, full_out = (gathered[0], gathered[1], gathered[2])
    gate_f = gathered[3].astype(jnp.float32)
    gain_first = gathered[4].astype(jnp.float32)
    gain_second = gathered[5].astype(jnp.float32)
    conv_f = gathered[6].astype(jnp.float32)
    bias_f = gathered[7].astype(jnp.float32)
    rate_f = gathered[8].astype(jnp.float32)
    slice_gate, slice_up, slice_down = fetch_feedforward(w_gate, w_up, w_down)
    tok_rows = tokens[0].astype(jnp.float32)
    tok_count = tok_rows.shape[0]
    model_width = tok_rows.shape[1]
    width_r = full_x.shape[1]
    normed = rms_scale(tok_rows, gain_first).astype(jnp.bfloat16)
    branch_x = product(normed, full_x).astype(jnp.bfloat16)
    branch_y = product(normed, full_y)
    carried = passed_along(branch_x[tok_count - (WIDTH - 1) :], "seq", 1)
    extended = jnp.concatenate([carried, branch_x], axis=0).astype(jnp.float32)
    conv_out = causal_conv(extended, conv_f, tok_count)
    decays, drives = recurrence_inputs(conv_out, gate_f, bias_f, rate_f)
    cum_decay, local_state = lax.associative_scan(affine_pair, (decays, drives), axis=0)
    ones_r = jnp.ones((width_r,), jnp.float32)
    zeros_r = jnp.zeros((width_r,), jnp.float32)
    carry_in = entering(
        (cum_decay[-1], local_state[-1]), "seq", affine_pair, (ones_r, zeros_r), False
    )
    state_in = carry_in[1]
    states = local_state + cum_decay * state_in
    gate_y = gelu_tanh(branch_y)
    mixed_rows = (states * gate_y).astype(jnp.bfloat16)
    residual = tok_rows + product(mixed_rows, full_out)
    normed_mlp = rms_scale(residual, gain_second).astype(jnp.bfloat16)
    rows_all = lax.all_gather(normed_mlp[None], "fsdp", axis=0, tiled=True).reshape(-1, model_width)
    gate_pre = product(rows_all, slice_gate)
    up_proj = product(rows_all, slice_up)
    hidden = gated_product(gate_pre, up_proj).astype(jnp.bfloat16)
    mlp_out = lax.psum_scatter(product(hidden, slice_down), "fsdp", scatter_dimension=0, tiled=True)
    result = (residual + mlp_out).astype(jnp.bfloat16)[None]
    fresh = lax.optimization_barrier((w_x, w_y, w_out, w_gate, w_up, w_down, mlp_out))
    again = fetch_recurrent(
        fresh[0], fresh[1], fresh[2], gate_w, gain_in, gain_mlp, conv_w, gate_b, rate
    )
    full_x, full_y, full_out = (again[0], again[1], again[2])
    slice_gate, slice_up, slice_down = fetch_feedforward(fresh[3], fresh[4], fresh[5])
    grad_rows = cotangent[0].astype(jnp.float32)
    grad_all = lax.all_gather(cotangent, "fsdp", axis=0, tiled=True).reshape(-1, model_width)
    d_hidden = product(grad_all, slice_down.T)
    grad_down = product(hidden.T, grad_all)
    unused, mlp_pull = jax.vjp(gated_product, gate_pre, up_proj)
    d_gate_f, d_up_f = mlp_pull(d_hidden)
    d_gate = d_gate_f.astype(jnp.bfloat16)
    d_up = d_up_f.astype(jnp.bfloat16)
    grad_gate = product(rows_all.T, d_gate)
    grad_up = product(rows_all.T, d_up)
    feed_grads = (
        lax.psum_scatter(grad_gate, "seq", scatter_dimension=0, tiled=True),
        lax.psum_scatter(grad_up, "seq", scatter_dimension=0, tiled=True),
        lax.psum_scatter(grad_down, "seq", scatter_dimension=1, tiled=True),
    )
    d_normed_mlp = lax.psum_scatter(
        product(d_gate, slice_gate.T) + product(d_up, slice_up.T),
        "fsdp",
        scatter_dimension=0,
        tiled=True,
    )
    unused, second_pull = jax.vjp(rms_scale, residual, gain_second)
    d_res_norm, d_gain_mlp = second_pull(d_normed_mlp)
    d_residual = grad_rows + d_res_norm
    d_branch = d_residual.astype(jnp.bfloat16)
    grad_out = product(mixed_rows.T, d_branch)
    d_mixed = product(d_branch, full_out.T)
    d_states = d_mixed * gate_y
    unused, y_pull = jax.vjp(gelu_tanh, branch_y)
    d_branch_y = y_pull(d_mixed * states)[0].astype(jnp.bfloat16)
    flipped = decays[::-1]
    coeffs = jnp.concatenate([jnp.ones((1, width_r), jnp.float32), flipped[:-1]], axis=0)
    cum_back, local_back = lax.associative_scan(affine_pair, (coeffs, d_states[::-1]), axis=0)
    outgoing = (cum_back[-1] * flipped[-1], local_back[-1] * flipped[-1])
    carry_back = entering(outgoing, "seq", affine_pair, (ones_r, zeros_r), True)
    state_grad = (local_back + cum_back * carry_back[1])[::-1]
    before = jnp.concatenate([state_in[None], states[:-1]], axis=0)
    unused, gate_pull = jax.vjp(recurrence_inputs, conv_out, gate_f, bias_f, rate_f)
    d_conv, d_gate_w, d_bias, d_rate = gate_pull((state_grad * before, state_grad))

    def conv_only(ext_rows, taps):
        return causal_conv(ext_rows, taps, tok_count)

    unused, conv_pull = jax.vjp(conv_only, extended, conv_f)
    d_extended, grad_conv = conv_pull(d_conv)
    rim_back = passed_along(d_extended[: WIDTH - 1], "seq", -1)
    d_branch_x = (
        d_extended[WIDTH - 1 :] + jnp.pad(rim_back, ((tok_count - (WIDTH - 1), 0), (0, 0)))
    ).astype(jnp.bfloat16)
    grad_x = product(normed.T, d_branch_x)
    grad_y = product(normed.T, d_branch_y)
    d_normed = product(d_branch_x, full_x.T) + product(d_branch_y, full_y.T)
    unused, first_pull = jax.vjp(rms_scale, tok_rows, gain_first)
    d_tok, d_gain_in = first_pull(d_normed)
    tokens_grad = (d_residual + d_tok)[None]
    recurrent_grads = sum_recurrent(
        (grad_x, grad_y, grad_out, d_gate_w, d_gain_in, d_gain_mlp, grad_conv, d_bias, d_rate)
    )
    return (
        result,
        tokens_grad,
        recurrent_grads[0],
        recurrent_grads[1],
        recurrent_grads[2],
        recurrent_grads[3],
        recurrent_grads[4],
        recurrent_grads[5],
        recurrent_grads[6],
        recurrent_grads[7],
        recurrent_grads[8],
        feed_grads[0],
        feed_grads[1],
        feed_grads[2],
    )


def by_mesh_axes(specs):
    names = {("z", "x"): "seq", ("y", "c"): "fsdp", ("z", "x", "y", "c"): ("seq", "fsdp"), None: None}
    return tuple(P(*(names[entry] for entry in spec)) for spec in specs)


def solution(mesh):
    seq_count, pair_count = mesh.shape["seq"], mesh.shape["fsdp"]
    zn = seq_count // 2
    grid = Mesh(mesh.devices.reshape(zn, 2, pair_count // 2, 2), ("z", "x", "y", "c"))
    seq, fsdp, both = ("z", "x"), ("y", "c"), ("z", "x", "y", "c")
    rows = P(fsdp, seq, None)
    by_row = P(both, None)
    by_col = P(None, both)
    placed = (
        rows, by_row, by_row, by_row, P(None, None, both), P(both), P(both), by_col, by_col, P(both),
        P(seq, fsdp), P(seq, fsdp), P(fsdp, seq), rows,
    )
    out_specs = (
        rows, rows, by_row, by_row, by_row, P(None, None, both), P(both), P(both), by_col, by_col,
        P(both), P(seq, fsdp), P(seq, fsdp), P(fsdp, seq),
    )

    lanes = 128

    def run(*args):
        width = args[0].shape[2]
        whole_tiles = width % (16 * mesh.size) == 0 and 2 * width % (lanes * seq_count) == 0
        if whole_tiles and zn >= 4:
            hidden_share = args[10].shape[1] // pair_count
            fold = -(-hidden_share // (lanes * zn)) * lanes
            program = functools.partial(per_device, zn, fold)
            on, ins, outs = grid, placed, out_specs
        else:
            program, on = per_device_gathered, mesh
            ins, outs = by_mesh_axes(placed), by_mesh_axes(out_specs)
        return jax.shard_map(program, mesh=on, in_specs=ins, out_specs=outs, check_vma=False)(*args)

    return run
```

```python
import functools

import jax
import jax.numpy as jnp
from jax import lax
from jax.experimental import pallas as pl
from jax.experimental.pallas import tpu as pltpu
from jax.sharding import Mesh
from jax.sharding import PartitionSpec as P

HEADS = 10
HD = 256
WIDTH = 4
HALO = 16
EPS = 1e-06
BF = jnp.bfloat16
F32 = jnp.float32


def swap(value, axis):
    return lax.ppermute(value, axis, [(0, 1), (1, 0)])


def shifted(value, axes, by, count, wrap=False):
    pairs = [(i, (i + by) % count) for i in range(count) if wrap or 0 <= i + by < count]
    return lax.ppermute(value, axes, pairs)


def pick(flag, first, second):
    return jnp.where(flag, first, second)


def tick(*values):
    return lax.optimization_barrier(values)


def dot(left, right, dims):
    return lax.dot_general(left, right, (dims, ((), ())), preferred_element_type=F32)


def product(left, right):
    return dot(left, right, ((1,), (0,)))


def product_t(left, right):
    return dot(left, right, ((1,), (1,)))


def t_product(left, right):
    return dot(left, right, ((0,), (0,)))


def rms_scale(values, gain_scale):
    return values * lax.rsqrt(jnp.mean(values * values, axis=-1, keepdims=True) + EPS) * gain_scale


def gelu_tanh(values):
    return jax.nn.gelu(values, approximate=True)


def gated_product(left, right):
    return gelu_tanh(left) * right


def gelu_both(v):
    inner = 0.7978845608028654 * (v + 0.044715 * v * v * v)
    th = jnp.tanh(inner)
    value = 0.5 * v * (1.0 + th)
    slope = 0.5 * (1.0 + th) + 0.5 * v * (1.0 - th * th) * 0.7978845608028654 * (1.0 + 0.134145 * v * v)
    return value, slope


def minus_expm1(v):
    series = jnp.full_like(v, 1.0)
    for n in range(11, 1, -1):
        series = 1.0 + series * v * (1.0 / n)
    return jnp.where(v > -1.0, -v * series, 1.0 - jnp.exp(v))


def two_parts(v):
    high = v.astype(BF)
    return high, (v - high.astype(F32)).astype(BF)


def wide_dot(left, right, dims):
    high, low = two_parts(left)
    return dot(high, right, dims) + dot(low, right, dims)


def moved(values, by, fill, rows):
    count = values.shape[0]
    rolled = pltpu.roll(values, by % count, 0)
    inside = rows >= by if by > 0 else rows < count + by
    return jnp.where(inside, rolled, fill)


def scan_rows(decay, drive, rows, backward):
    step = 1
    while step < decay.shape[0]:
        by = -step if backward else step
        drive = drive + decay * moved(drive, by, 0.0, rows)
        decay = decay * moved(decay, by, 1.0, rows)
        step *= 2
    return decay, drive


def conv_taps(rows_ref, halo_ref):
    rows = rows_ref[0].astype(F32)
    extended = jnp.concatenate([halo_ref[0].astype(F32), rows], axis=0)
    count = rows.shape[0]
    return [rows] + [extended[HALO - k : HALO - k + count] for k in range(1, WIDTH)]


def gates(conv_out, gate_ref, prm_ref):
    nt = ((1,), (1,))
    high, low = two_parts(conv_out)
    pre_a = dot(high, gate_ref[0], nt) + dot(low, gate_ref[0], nt) + prm_ref[4:5, :]
    pre_x = dot(high, gate_ref[1], nt) + dot(low, gate_ref[1], nt) + prm_ref[5:6, :]
    sig_a = jax.nn.sigmoid(pre_a)
    sig_x = jax.nn.sigmoid(pre_x)
    log_decay = -8.0 * sig_a * prm_ref[6:7, :]
    return sig_a, sig_x, jnp.exp(log_decay), jnp.sqrt(minus_expm1(2.0 * log_decay))


def forward_kernel(rows_ref, halo_ref, prm_ref, gate_ref, decay_ref, local_ref, cum_ref):
    taps = conv_taps(rows_ref, halo_ref)
    conv_out = sum(prm_ref[k : k + 1, :] * taps[k] for k in range(WIDTH))
    sig_a, sig_x, decays, root = gates(conv_out, gate_ref, prm_ref)
    drives = root * sig_x * conv_out
    decay_ref[0] = decays
    rows = lax.broadcasted_iota(jnp.int32, decays.shape, 0)
    cum, local = scan_rows(decays, drives, rows, False)
    cum_ref[0] = cum
    local_ref[0] = local


def back_scan_kernel(d_mixed_ref, branch_y_ref, states_ref, decay_ref, d_y_ref, local_ref, cum_ref):
    value, slope = gelu_both(branch_y_ref[0])
    d_mixed = d_mixed_ref[0]
    d_y_ref[0] = (d_mixed * states_ref[0] * slope).astype(BF)
    rows = lax.broadcasted_iota(jnp.int32, d_mixed.shape, 0)
    coeffs = moved(decay_ref[0], -1, 1.0, rows)
    cum, local = scan_rows(coeffs, d_mixed * value, rows, True)
    cum_ref[0] = cum
    local_ref[0] = local


def backward_kernel(
    rows_ref, halo_ref, prm_ref, gate_ref, local_ref, cum_ref, ends_ref, states_ref,
    d_conv_ref, d_gate_ref, d_prm_ref,
):
    taps = conv_taps(rows_ref, halo_ref)
    conv_out = sum(prm_ref[k : k + 1, :] * taps[k] for k in range(WIDTH))
    sig_a, sig_x, decays, root = gates(conv_out, gate_ref, prm_ref)
    rows = lax.broadcasted_iota(jnp.int32, decays.shape, 0)
    grad = local_ref[0] + cum_ref[0] * ends_ref[0, 0:1, :]
    before = jnp.where(rows >= 1, pltpu.roll(states_ref[0], 1, 0), ends_ref[0, 1:2, :])
    d_log = grad * before * decays - grad * sig_x * conv_out * (decays * decays / root)
    d_pre_a = d_log * (-8.0 * prm_ref[6:7, :]) * sig_a * (1.0 - sig_a)
    d_pre_x = grad * root * conv_out * sig_x * (1.0 - sig_x)
    nn, tn = ((1,), (0,)), ((0,), (0,))
    a_high, a_low = two_parts(d_pre_a)
    x_high, x_low = two_parts(d_pre_x)
    c_high, c_low = two_parts(conv_out)
    d_conv = grad * root * sig_x
    d_conv = d_conv + (dot(a_high, gate_ref[0], nn) + dot(a_low, gate_ref[0], nn))
    d_conv = d_conv + (dot(x_high, gate_ref[1], nn) + dot(x_low, gate_ref[1], nn))
    d_conv_ref[0] = d_conv
    d_gate_a = dot(a_high, c_high, tn) + dot(a_low, c_high, tn) + dot(a_high, c_low, tn)
    d_gate_x = dot(x_high, c_high, tn) + dot(x_low, c_high, tn) + dot(x_high, c_low, tn)
    total = lambda v: jnp.sum(v, axis=0, keepdims=True)
    sums = [total(d_conv * taps[k]) for k in range(WIDTH)]
    sums += [total(d_pre_a), total(d_pre_x), total(d_log * (-8.0 * sig_a))]
    sums.append(jnp.zeros_like(sums[0]))
    d_prm = jnp.concatenate(sums, axis=0)
    first = pl.program_id(1) == 0

    @pl.when(first)
    def _():
        d_gate_ref[0] = d_gate_a
        d_gate_ref[1] = d_gate_x
        d_prm_ref[...] = d_prm

    @pl.when(jnp.logical_not(first))
    def _():
        d_gate_ref[0] += d_gate_a
        d_gate_ref[1] += d_gate_x
        d_prm_ref[...] += d_prm


def head_specs(tok):
    rows = pl.BlockSpec((1, tok, HD), lambda h, q: (q, 0, h))
    halo = pl.BlockSpec((1, HALO, HD), lambda h, q: (q, 0, h))
    prm = pl.BlockSpec((8, HD), lambda h, q: (0, h))
    gate = pl.BlockSpec((2, HD, HD), lambda h, q: (0, h, 0))
    ends = pl.BlockSpec((1, 8, HD), lambda h, q: (q, 0, h))
    return rows, halo, prm, gate, ends


PARAMS = dict(vmem_limit_bytes=48 * 1024 * 1024)
COST = pl.CostEstimate(flops=0, bytes_accessed=0, transcendentals=0)


def forward_call(branch_x, halo, prm, gate):
    seqs, tok, half = branch_x.shape
    rows_s, halo_s, prm_s, gate_s, _ = head_specs(tok)
    out = jax.ShapeDtypeStruct(branch_x.shape, F32)
    return pl.pallas_call(
        forward_kernel,
        grid=(half // HD, seqs),
        in_specs=[rows_s, halo_s, prm_s, gate_s],
        out_specs=[rows_s] * 3,
        out_shape=[out] * 3,
        compiler_params=pltpu.CompilerParams(**PARAMS),
        cost_estimate=COST,
        name="recurrence_forward",
    )(branch_x, halo, prm, gate)


def back_scan_call(d_mixed, branch_y, states, decays):
    seqs, tok, half = d_mixed.shape
    rows_s = head_specs(tok)[0]
    out = jax.ShapeDtypeStruct(d_mixed.shape, F32)
    return pl.pallas_call(
        back_scan_kernel,
        grid=(half // HD, seqs),
        in_specs=[rows_s] * 4,
        out_specs=[rows_s] * 3,
        out_shape=[jax.ShapeDtypeStruct(d_mixed.shape, BF), out, out],
        compiler_params=pltpu.CompilerParams(**PARAMS),
        cost_estimate=COST,
        name="recurrence_back_scan",
    )(d_mixed, branch_y, states, decays)


def backward_call(branch_x, halo, prm, gate, local, cum, ends, states):
    seqs, tok, half = branch_x.shape
    rows_s, halo_s, prm_s, gate_s, ends_s = head_specs(tok)
    return pl.pallas_call(
        backward_kernel,
        grid=(half // HD, seqs),
        in_specs=[rows_s, halo_s, prm_s, gate_s, rows_s, rows_s, ends_s, rows_s],
        out_specs=[rows_s, gate_s, prm_s],
        out_shape=[
            jax.ShapeDtypeStruct(branch_x.shape, F32),
            jax.ShapeDtypeStruct(gate.shape, F32),
            jax.ShapeDtypeStruct(prm.shape, F32),
        ],
        compiler_params=pltpu.CompilerParams(**PARAMS),
        cost_estimate=COST,
        name="recurrence_backward",
    )(branch_x, halo, prm, gate, local, cum, ends, states)


def place_kernel(plan, count_in, *refs):
    index = {axis: lax.axis_index(axis) for axis in ("z", "x", "y", "c")}
    for source, start, size, out, target in plan:
        refs[count_in + out][target(index)] = refs[source][:, start : start + size]


def place(plan, pieces, outs, name):
    whole = pl.BlockSpec(memory_space=pltpu.VMEM)
    return pl.pallas_call(
        functools.partial(place_kernel, plan, len(pieces)),
        in_specs=[whole] * len(pieces),
        out_specs=[whole] * len(outs),
        out_shape=[jax.ShapeDtypeStruct(shape, BF) for shape in outs],
        cost_estimate=COST,
        compiler_params=pltpu.CompilerParams(**PARAMS),
        name=name,
    )(*pieces)


def rows_at(block, share, offset=None, size=None):
    def target(index):
        rows = pl.ds(pl.multiple_of(block(index) * share, 16), share)
        if size is None:
            return rows, slice(None)
        return rows, pl.ds(offset(index), size)

    return target


def home_kernel(zn, fold, count, cols_ff, *refs):
    lanes = 128
    for far in range(count):
        start = lax.rem(lax.axis_index("z") - far + zn, zn) * fold
        for j in range(fold // lanes):
            at = start + j * lanes

            @pl.when(at < cols_ff)
            def _(far=far, j=j, at=at):
                dest = pl.ds(pl.multiple_of(at, lanes), lanes)
                for n in range(3):
                    col = n * fold + j * lanes
                    refs[count + n][:, dest] = refs[far][:, col : col + lanes].astype(F32)


def place_feed_forward_grads(pieces, rows_ff, cols_ff, fold, zn):
    whole = pl.BlockSpec(memory_space=pltpu.VMEM)
    return pl.pallas_call(
        functools.partial(home_kernel, zn, fold, len(pieces), cols_ff),
        in_specs=[whole] * len(pieces),
        out_specs=[whole] * 3,
        out_shape=[jax.ShapeDtypeStruct((rows_ff, cols_ff), F32)] * 3,
        cost_estimate=COST,
        compiler_params=pltpu.CompilerParams(**PARAMS),
        name="place_feed_forward_grads",
    )(*pieces)


TN = ((0,), (0,))


def split_blocks(whole_ref, keep_ref, give_ref, share, mine):
    for j in range(4):
        ours = pl.multiple_of((2 * j + mine) * share, 8)
        theirs = pl.multiple_of((2 * j + 1 - mine) * share, 8)
        keep_ref[0, j] = whole_ref[pl.ds(ours, share), :]
        give_ref[0, j] = whole_ref[pl.ds(theirs, share), :].astype(BF)


def yo_kernel(share, where_ref, normed_ref, mixed_ref, d_y_ref, d_out_ref, keep_ref, give_ref, whole_ref):
    half = d_y_ref.shape[1]
    whole_ref[:, :half] = dot(normed_ref[...], d_y_ref[...], TN)
    whole_ref[:, half:] = dot(mixed_ref[...], d_out_ref[...], TN)
    split_blocks(whole_ref, keep_ref, give_ref, share, where_ref[1])


def xg_kernel(share, where_ref, normed_ref, d_gate_ref, d_x_ref, keep_ref, give_ref, whole_ref):
    half = d_x_ref.shape[1]
    whole_ref[:, :half] = dot(normed_ref[...], d_x_ref[...], TN)
    whole_ref[:, half:] = d_gate_ref[0]
    split_blocks(whole_ref, keep_ref, give_ref, share, where_ref[1])


def term_call(kernel, where, specs, args, first, count, share, columns, name):
    block = pl.BlockSpec((1, 4, share, columns), lambda n, where: (n, 0, 0, 0))
    return pl.pallas_call(
        functools.partial(kernel, share),
        grid_spec=pltpu.PrefetchScalarGridSpec(
            num_scalar_prefetch=1,
            grid=(count,),
            in_specs=specs,
            out_specs=[block, block],
            scratch_shapes=[pltpu.VMEM((8 * share, columns), F32)],
        ),
        out_shape=[
            jax.ShapeDtypeStruct((count, 4, share, columns), F32),
            jax.ShapeDtypeStruct((count, 4, share, columns), BF),
        ],
        cost_estimate=COST,
        compiler_params=pltpu.CompilerParams(**PARAMS),
        name=name,
    )(where, *args)


def ff_kernel(steps, fold, where_ref, *refs):
    rows, cots, hidden, d_gu = (refs[n * steps : (n + 1) * steps] for n in range(4))
    keep_ref, give_ref, whole_ref = refs[4 * steps :]
    first = second = 0.0
    for k in range(steps):
        first = first + dot(rows[k][...], d_gu[k][...], TN)
        second = second + dot(cots[k][...], hidden[k][...], TN)
    whole_ref[:, : 2 * fold] = first
    whole_ref[:, 2 * fold :] = second
    size = keep_ref.shape[1]
    mine = where_ref[2]
    keep_ref[0] = whole_ref[pl.ds(pl.multiple_of(mine * size, 8), size), :]
    give_ref[0] = whole_ref[pl.ds(pl.multiple_of((1 - mine) * size, 8), size), :].astype(BF)


def ff_grads_call(where, rows, cots, hidden, d_gu, zn, rows_ff):
    steps, fold = len(rows), hidden[0].shape[1]
    count = rows[0].shape[0]
    part = pl.BlockSpec((count, 2 * rows_ff), lambda far, where: (0, lax.rem(where[0] + far, zn)))
    whole = lambda item: pl.BlockSpec(item.shape, lambda far, where: (0, 0))
    block = pl.BlockSpec((1, rows_ff, 3 * fold), lambda far, where: (far, 0, 0))
    shape = (zn, rows_ff, 3 * fold)
    return pl.pallas_call(
        functools.partial(ff_kernel, steps, fold),
        grid_spec=pltpu.PrefetchScalarGridSpec(
            num_scalar_prefetch=1,
            grid=(zn,),
            in_specs=[part] * (2 * steps) + [whole(item) for item in (*hidden, *d_gu)],
            out_specs=[block, block],
            scratch_shapes=[pltpu.VMEM((2 * rows_ff, 3 * fold), F32)],
        ),
        out_shape=[jax.ShapeDtypeStruct(shape, F32), jax.ShapeDtypeStruct(shape, BF)],
        cost_estimate=COST,
        compiler_params=pltpu.CompilerParams(**PARAMS),
        name="feed_forward_grads",
    )(where, *rows, *cots, *hidden, *d_gu)


def carried(decay, drive, zn, x, by):
    own = jnp.stack([decay, drive])
    beside = swap(own, "x")
    inner = x == 0 if by > 0 else x == 1
    near, far = pick(inner, own, beside), pick(inner, beside, own)
    pair = jnp.stack([near[0] * far[0], near[1] * far[0] + far[1]])
    came = [shifted(pair, "z", by * dist, zn) for dist in range(zn - 1, 0, -1)]
    state = jnp.zeros_like(drive)
    for part in came:
        state = part[0] * state + part[1]
    return pick(inner, state, near[0] * state + near[1])


def per_device(
    zn, fold,
    tokens, w_x, w_y, w_out, gate_w, gain_in, gain_mlp, conv_w, gate_b, rate,
    w_gate, w_up, w_down, cotangent,
):
    z, x, y, c = (lax.axis_index(axis) for axis in ("z", "x", "y", "c"))
    zh = zn // 2
    seq_count = 2 * zn
    tok, width = tokens.shape[1], tokens.shape[2]
    share, wide_r = w_x.shape
    half = wide_r // 2
    rows_ff, cols_ff = w_gate.shape
    zx, zy = ("z", "x"), ("z", "y")
    z_of = [lax.rem(z - k + zn, zn) for k in range(zn)]
    lanes = 128
    every = range(zn)
    hop = lambda value: shifted(value, "z", 1, zn, True)

    spread = []
    for other in (0, 1):
        pairs = []
        for h in (0, 1):
            for zl in range(zh):
                for ys in (0, 1):
                    k = ys ^ other
                    pairs.append(((h * zh + zl) * 2 + ys, (k * zh + zl) * 2 + h))
        spread.append(pairs)
    gathered_back = [[(b, a) for a, b in pairs] for pairs in spread]
    own_half = lambda w: pick(y == 0, w[:, :half], w[:, half:])
    other_half = lambda w: pick(y == 0, w[:, half:], w[:, :half])

    def source(k, across, other):
        def at(i):
            flip = lambda value, on: 1 - value if on else value
            return lax.rem(i["z"] - k + zn, zn), flip(i["x"], across), flip(i["c"], other)

        return at

    def by_rows(at, beside):
        def block(i):
            sz, sx, sc = at(i)
            return ((sz * 2 + sx) * 2 + (1 - i["y"] if beside else i["y"])) * 2 + sc

        return block

    def by_spread(at, second):
        def block(i):
            sz, sx, sc = at(i)
            sh = sz // zh
            return ((lax.rem(sz, zh) * 2 + sx) * 2 + (1 - sh if second else sh)) * 2 + sc

        return block

    def gate_at(at, second):
        rows = by_spread(at, second)

        def target(i):
            start = pl.multiple_of(rows(i) * share, 16)
            return at(i)[0] // zh, pl.ds(start, share), slice(None)

        return target

    params = jnp.concatenate([gain_in[None], gain_mlp[None], conv_w, gate_b, rate[None]])
    count_p = params.shape[0]
    params = jnp.pad(params.T, ((0, 0), (0, lanes - count_p)))
    gate_t = gate_w.transpose(0, 2, 1)
    gate_pieces = [
        lax.ppermute(pick(y == 0, gate_t[k], gate_t[1 - k]), zy, spread[k]) for k in (0, 1)
    ]
    wide_x = half + lanes
    x_own = jnp.concatenate([own_half(w_x), params], axis=1)
    x_other = swap(jnp.concatenate([other_half(w_x), params], axis=1), "y")
    unit_x = jnp.concatenate([x_own, x_other, gate_pieces[0], gate_pieces[1]], axis=1)
    tok_own, cot = tokens[0], cotangent[0]
    cot_z, cot_y = [cot], {}
    unit_x, w_y, w_out, tok_own, ff_raw = tick(unit_x, w_y, w_out, tok_own, (w_gate, w_up, w_down))

    a_z, a_x, a_zc, a_xc = [unit_x], [], [], []
    padded = zn * fold
    widen = lambda w: jnp.pad(w, ((0, 0), (0, padded - cols_ff)))
    ff_wide = [widen(ff_raw[0]), widen(ff_raw[1]), widen(ff_raw[2].T)]

    def ff_piece(z_at):
        return jnp.concatenate(
            [lax.dynamic_slice_in_dim(w, z_at * fold, fold, 1) for w in ff_wide], axis=1
        )

    ff_units = [ff_piece(lax.rem(z + far, zn)) for far in every]
    for k in range(1, zn):
        a_z.append(hop(a_z[-1]))
        a_x.append(swap(a_z[k - 1], "x"))
        a_zc.append(swap(a_z[k - 1], "c"))
        if k > 1:
            a_xc.append(swap(a_x[k - 2], "c"))
        if k == 1:
            tok_other = swap(tok_own, "y")
            y_other = swap(other_half(w_y), "y")
            a_z, a_x, w_out = tick(a_z, a_x, w_out)
            out_halves = [w_out[:, :half], w_out[:, half:]]
            out_parts = [
                lax.ppermute(pick(y == 0, out_halves[i], out_halves[1 - i]), zy, spread[i])
                for i in (0, 1)
            ]
        elif k == 2:
            a_z, a_x, tok_own, tok_other, y_other, out_parts = tick(
                a_z, a_x, tok_own, tok_other, y_other, out_parts
            )
        else:
            a_z, a_x = tick(a_z, a_x)
    tok_f = jnp.stack([tok_own, tok_other]).astype(F32)
    unit_yo = jnp.concatenate([own_half(w_y), y_other, out_parts[0], out_parts[1]], axis=1)
    unit_yo, a_z = tick(unit_yo, a_z)

    b_z, b_x, b_zc, b_xc = [unit_yo, hop(unit_yo)], [], [], []
    a_x.append(swap(a_z[-1], "x"))
    a_zc.append(swap(a_z[-1], "c"))
    a_xc.append(swap(a_x[-2], "c"))
    a_x, a_zc, a_xc, unit_yo, ff_units = tick(a_x, a_zc, a_xc, b_z[0], ff_units)
    b_z[0] = unit_yo
    a_xc.append(swap(a_x[-1], "c"))
    b_x.append(swap(b_z[0], "x"))
    placed, plan = [], []
    for k in every:
        for j, part in enumerate((a_z[k], a_zc[k], a_x[k], a_xc[k])):
            at = source(k, j >= 2, j % 2)
            n = len(placed)
            placed.append(part)
            for beside in (0, 1):
                block = by_rows(at, beside)
                plan.append((n, beside * wide_x, half, 0, rows_at(block, share)))
                plan.append((n, beside * wide_x + half, lanes, 1, rows_at(block, share)))
                plan.append((n, 2 * wide_x + beside * HD, HD, 2, gate_at(at, beside)))
    full_x, full_p, gates_t = place(
        plan, placed, [(width, half), (width, lanes), (2, half, HD)], "place_w_x"
    )
    smalls = full_p[:, :count_p].astype(F32).T
    gain_first, gain_second = smalls[0], smalls[1]
    prm = jnp.pad(smalls[2:], ((0, 1), (0, 0)))
    prm = pick(y == 0, prm[:, :half], prm[:, half:])
    normed = rms_scale(tok_f, gain_first).astype(BF).reshape(2 * tok, width)
    branch_x = product(normed, full_x).astype(BF).reshape(2, tok, half)

    branch_x, b_z = tick(branch_x, b_z)
    b_z.append(hop(b_z[-1]))
    b_x.append(swap(b_z[1], "x"))
    b_zc += [swap(b_z[0], "c"), swap(b_z[1], "c")]
    halo = shifted(branch_x[:, tok - HALO :], zx, 1, seq_count)
    halo, b_z, b_x = tick(halo, b_z, b_x)
    for k in range(3, zn):
        b_z.append(hop(b_z[-1]))
        b_x.append(swap(b_z[k - 1], "x"))
        b_zc.append(swap(b_z[k - 1], "c"))
        b_xc.append(swap(b_x[k - 3], "c"))
        if k == 3:
            decays, local, cum = tick(*forward_call(branch_x, halo, prm, gates_t))
            state_in = carried(cum[:, -1], local[:, -1], zn, x, 1)
            state_in, b_z, b_x = tick(state_in, b_z, b_x)
        else:
            b_z, b_x = tick(b_z, b_x)
    turns = [
        [(far, None) for far in range(1, zn) if far % 3 == 1],
        [(far, 0) for far in range(1, zn) if far % 3 == 2],
        [(far, 1) for far in range(1, zn) if far % 3 == 2],
        [(far, None) for far in range(1, zn) if far % 3 == 0],
    ]

    def sent_along(blocks, turn):
        sent = {}
        for far, part in turns[turn]:
            block = blocks[far]
            cut = block.shape[1] // 2
            if part is not None:
                block = block[:, :cut] if part == 0 else block[:, cut:]
            sent[far, part] = shifted(block, "z", far, zn, True)
        return sent

    def joined(came, fars):
        return {
            far: came[far, None] if (far, None) in came
            else jnp.concatenate([came[far, 0], came[far, 1]], axis=1)
            for far in fars
        }

    far_of = lambda turn: [far for far, _ in turns[turn]]
    ff_units, b_z = tick(ff_units, b_z)
    ff_came, ff_x = sent_along(ff_units, 0), {}
    b_x.append(swap(b_z[-1], "x"))
    b_zc.append(swap(b_z[-1], "c"))
    b_xc += [swap(b_x[-3], "c"), swap(b_x[-2], "c")]
    b_x, cot_z, cot_y, ff_units, ff_came = tick(b_x, cot_z, cot_y, ff_units, ff_came)

    ff_came.update(sent_along(ff_units, 1))
    ff_x[0] = swap(ff_units[0], "x")
    cot_y[0] = swap(cot_z[0], "y")
    b_xc.append(swap(b_x[-1], "c"))
    placed, plan = [], []
    for k in every:
        for j, part in enumerate((b_z[k], b_zc[k], b_x[k], b_xc[k])):
            at = source(k, j >= 2, j % 2)
            n = len(placed)
            placed.append(part)
            column = lambda i, at=at: pl.multiple_of((at(i)[0] // zh) * half, lanes)
            for beside in (0, 1):
                plan.append((n, beside * half, half, 0, rows_at(by_rows(at, beside), share)))
                plan.append(
                    (n, (2 + beside) * half, half, 1, rows_at(by_spread(at, beside), share, column, half))
                )
    full_y, full_out = place(plan, placed, [(width, half), (half, width)], "place_w_y_w_out")
    branch_y = product(normed, full_y).reshape(2, tok, half)
    states = local + cum * state_in[:, None]
    mixed = (states * gelu_tanh(branch_y)).astype(BF).reshape(2 * tok, half)
    out_sum = product(mixed, full_out)
    out_own, out_give = out_sum[:tok], out_sum[tok:].astype(BF)
    out_own, out_give, ff_came, ff_x, ff_units, cot_z, cot_y = tick(
        out_own, out_give, ff_came, ff_x, ff_units, cot_z, cot_y
    )
    out_came = swap(out_give, "y")
    ff_came.update(sent_along(ff_units, 2))
    ff_x.update({far: swap(piece, "x") for far, piece in joined(ff_came, far_of(0)).items()})
    cot_z.append(hop(cot_z[0]))
    out_came, out_own, ff_came, ff_x, ff_units, cot_z = tick(
        out_came, out_own, ff_came, ff_x, ff_units, cot_z
    )
    residual = tok_own.astype(F32) + out_own + out_came.astype(F32)
    normed_mlp = rms_scale(residual, gain_second).astype(BF)

    row_z, row_y = [normed_mlp, hop(normed_mlp)], {0: swap(normed_mlp, "y")}
    ff_came.update(sent_along(ff_units, 3))
    ff_x.update({far: swap(piece, "x") for far, piece in joined(ff_came, far_of(1)).items()})
    cot_y[1] = swap(cot_z[1], "y")
    row_z, row_y, cot_z, cot_y, ff_came, ff_x = tick(row_z, row_y, cot_z, cot_y, ff_came, ff_x)
    ff_x.update({far: swap(piece, "x") for far, piece in joined(ff_came, far_of(3)).items()})
    row_z.append(hop(row_z[-1]))
    cot_z.append(hop(cot_z[-1]))
    row_y[1] = swap(row_z[1], "y")
    row_z, row_y, cot_z, ff_x = tick(row_z, row_y, cot_z, ff_x)
    ff_pieces = joined(ff_came, range(1, zn))
    ff_pieces[0] = ff_units[0]
    placed, plan = [], []
    for k in every:
        for across, part in enumerate((ff_pieces[k], ff_x[k])):
            at = source(k, across, 0)
            block = lambda i, at=at: at(i)[0] * 2 + at(i)[1]
            n = len(placed)
            placed.append(part)
            plan.append((n, 0, 2 * fold, 0, rows_at(block, rows_ff)))
            plan.append((n, 2 * fold, fold, 1, rows_at(block, rows_ff)))
    w_gu, w_dt = place(plan, placed, [(width, 2 * fold), (width, fold)], "place_feed_forward")

    def with_cores(pair):
        return jnp.concatenate(list(pair) + [swap(part, "c") for part in pair])

    def feed_forward(k):
        rows, grads = with_cores((row_z[k], row_y[k])), with_cores((cot_z[k], cot_y[k]))
        gu = product(rows, w_gu)
        d_hidden = product(grads, w_dt)
        hidden, pull = jax.vjp(gated_product, gu[:, :fold], gu[:, fold:])
        d_gu = jnp.concatenate([item.astype(BF) for item in pull(d_hidden)], axis=1)
        return rows, grads, hidden.astype(BF), d_gu, product_t(d_gu, w_gu).reshape(4, tok, width)

    steps, d_parts, d_c, d_y, total = {}, {}, {}, {}, None
    m_parts, m_c, m_y, m_total = {}, {}, {}, None

    def core_give(parts):
        return parts[2:].astype(BF)

    def y_give(parts, came_c):
        return (parts[1] + came_c[1].astype(F32)).astype(BF)

    def own_sum(parts, came_c, came_y):
        return parts[0] + came_c[0].astype(F32) + came_y.astype(F32)

    where = jnp.stack([z, c, x]).astype(jnp.int32)
    order = list(range(1, zn)) + [0]
    for i in range(zn + 2):
        if i < zn:
            k = order[i]
            steps[k] = feed_forward(k)
            d_parts[k] = steps[k][-1]
        if k + 2 < zn and i < zn - 1:
            row_z.append(hop(row_z[-1]))
        if k + 2 < zn and i < zn - 1:
            cot_z.append(hop(cot_z[-1]))
        if i < zn - 2:
            row_y[k + 1] = swap(row_z[k + 1], "y")
            cot_y[k + 1] = swap(cot_z[k + 1], "y")
        if i < 2 or i == zn + 1:
            for n in [k] if i < 2 else order[2:]:
                m_parts[n] = product_t(steps[n][2], w_dt).reshape(4, tok, width)
        if 1 <= i <= 2:
            m_c[order[i - 1]] = swap(core_give(m_parts[order[i - 1]]), "c")
        if 1 <= i <= zn:
            d_c[order[i - 1]] = swap(core_give(d_parts[order[i - 1]]), "c")
        if 2 <= i:
            k = order[i - 2]
            d_y[k] = swap(y_give(d_parts[k], d_c[k]), "y")
        if 3 <= i:
            k = order[i - 3]
            term = own_sum(d_parts[k], d_c[k], d_y[k])
            total = hop((term if total is None else total.astype(F32) + term).astype(BF))
        if i == 4:
            m_y[1] = swap(y_give(m_parts[1], m_c[1]), "y")
        if i == 5:
            m_total = hop(own_sum(m_parts[1], m_c[1], m_y[1]).astype(BF))
        if i == zn:
            ff_keep, ff_give = tick(*ff_grads_call(
                where, *([steps[k][n] for k in every] for n in range(4)), zn, rows_ff
            ))
            ff_give = {far: ff_give[far] for far in every}
        if i == zn + 1:
            break
        steps, row_z, row_y, cot_z, cot_y, d_parts, d_c, d_y, total, m_parts, m_c, m_y, m_total = tick(
            steps, row_z, row_y, cot_z, cot_y, d_parts, d_c, d_y, total, m_parts, m_c, m_y, m_total
        )
        steps = {k: step[:4] for k, step in steps.items()}

    ff_sent, ff_home = {}, {}

    def cut_block(block, part):
        middle = 3 * fold // 2
        return block if part is None else block[:, :middle] if part == 0 else block[:, middle:]

    def give_across(turn):
        for far, part in turn:
            ff_sent[far, part] = swap(cut_block(ff_give[far], part), "x")

    def own_and_sent(far, part):
        return (cut_block(ff_keep[far], part) + ff_sent[far, part].astype(F32)).astype(BF)

    def send_home(turn):
        for far, part in turns[turn]:
            ff_home[far, part] = shifted(own_and_sent(far, part), "z", far, zn, True)

    give_across(turns[3] + turns[1])
    total, d_y, ff_sent, ff_give, m_total, m_parts = tick(total, d_y, ff_sent, ff_give, m_total, m_parts)

    d_normed_mlp = own_sum(d_parts[0], d_c[0], d_y[0]) + total.astype(F32)
    unused, second_pull = jax.vjp(rms_scale, residual, gain_second)
    d_res_norm, d_gain_mlp = second_pull(d_normed_mlp)
    d_residual = cot.astype(F32) + d_res_norm
    d_branch = d_residual.astype(BF)
    d_other = swap(d_branch, "y")
    send_home(3)
    give_across(turns[2])
    for k in order[2:]:
        m_c[k] = swap(core_give(m_parts[k]), "c")
    d_branch, d_other, ff_sent, ff_give, m_total, m_c = tick(d_branch, d_other, ff_sent, ff_give, m_total, m_c)

    d_branch_pair = jnp.concatenate([d_branch, d_other])
    d_mixed = product_t(d_branch_pair, full_out).reshape(2, tok, half)
    d_branch_y, local_back, cum_back = back_scan_call(d_mixed, branch_y, states, decays)
    leaving = decays[:, 0] * local_back[:, 0]
    m_y[2] = swap(y_give(m_parts[2], m_c[2]), "y")
    send_home(1)
    give_across(turns[0])
    d_flat_y = d_branch_y.reshape(2 * tok, half)
    eight = 8 * share
    z_at = lambda n, where, first: lax.rem(where[0] - n - first + 2 * zn, zn)
    full_spec = pl.BlockSpec((2 * tok, half), lambda n, where: (0, 0))

    def yo_terms(first, count):
        specs = [
            pl.BlockSpec((2 * tok, eight), lambda n, where: (0, z_at(n, where, first))),
            pl.BlockSpec((2 * tok, eight), lambda n, where: (0, lax.rem(z_at(n, where, first), zh))),
            full_spec,
            pl.BlockSpec((2 * tok, half), lambda n, where: (0, z_at(n, where, first) // zh)),
        ]
        args = (normed, mixed, d_flat_y, d_branch_pair)
        return term_call(yo_kernel, where, specs, args, first, count, share, 2 * half, "grad_w_y_w_out")

    def x_terms(first, count):
        specs = [
            pl.BlockSpec((2 * tok, eight), lambda n, where: (0, z_at(n, where, first))),
            pl.BlockSpec(
                (1, eight, HD),
                lambda n, where: (z_at(n, where, first) // zh, lax.rem(z_at(n, where, first), zh), 0),
            ),
            full_spec,
        ]
        args = (normed, d_gates, d_flat_x)
        return term_call(xg_kernel, where, specs, args, first, count, share, half + HD, "grad_w_x")

    yo_a = yo_terms(1, 2)
    leaving, d_branch_y, yo_a, m_y, m_total, ff_home, ff_sent, ff_give = tick(
        leaving, d_branch_y, yo_a, m_y, m_total, ff_home, ff_sent, ff_give
    )

    carry_back = carried(cum[:, -1], leaving, zn, x, -1)
    ends = jnp.pad(jnp.stack([carry_back, state_in], axis=1), ((0, 0), (0, 6), (0, 0)))
    yo_ac = swap(yo_a[1], "c")
    ends, yo_a, yo_ac, d_flat_y, ff_sent, ff_give, m_y, m_total = tick(
        ends, yo_a, yo_ac, d_flat_y, ff_sent, ff_give, m_y, m_total
    )

    yo, xg = {}, {}

    def hold(terms, kept, came, first):
        for n in range(came.shape[0]):
            terms[(first + n) % zn] = (kept, came, n)

    def at_x(term, which):
        kept, came, n = term
        part = lambda v: lax.dynamic_slice(
            v.reshape((-1, 2, 2) + v.shape[2:]), (n, which, 0, 0, 0), (1, 1, 2) + v.shape[2:]
        )[0, 0]
        return part(kept) + part(came).astype(F32)

    def x_give(term):
        return at_x(term, 1 - x).astype(BF)

    hold(yo, yo_a[0], yo_ac, 1)
    yo_x = {1: swap(x_give(yo[1]), "x")}
    send_home(2)
    for k in order[2:]:
        m_y[k] = swap(y_give(m_parts[k], m_c[k]), "y")
    d_conv, d_gates, d_prm = tick(*backward_call(
        branch_x, halo, prm, gates_t, local_back, cum_back, ends, states
    ))
    rim = shifted(d_conv[:, :8], zx, -1, seq_count)
    yo_b = yo_terms(3, zn - 2)
    rim, yo_x, yo_b, ff_home, ff_sent, ff_give, m_total, m_y = tick(
        rim, yo_x, yo_b, ff_home, ff_sent, ff_give, m_total, m_y
    )
    yo_bc = swap(yo_b[1], "c")

    d_ext = jnp.concatenate([d_conv, rim], axis=1)
    d_branch_x = sum(prm[k] * d_ext[:, k : k + tok] for k in range(WIDTH)).astype(BF)
    d_flat_x = d_branch_x.reshape(2 * tok, half)

    def add(total, terms, came_x, k):
        return total.astype(F32) + at_x(terms[k], x) + came_x[k].astype(F32)

    def return_rows(sums):
        mine = z // zh
        return [
            lax.ppermute(
                lax.dynamic_index_in_dim(sums, mine if k == 0 else 1 - mine, 0, False).astype(BF),
                zy, gathered_back[k],
            )
            for k in (0, 1)
        ]

    def returned_rows(came):
        came = [item.astype(F32) for item in came]
        return pick(y == 0, came[0], came[1]), pick(y == 0, came[1], came[0])

    def return_columns(sums):
        return swap(lax.dynamic_index_in_dim(sums, 1 - y, 0, False).astype(BF), "y")

    def returned_columns(sums, came):
        mine, across = lax.dynamic_index_in_dim(sums, y, 0, False), came.astype(F32)
        return jnp.concatenate([pick(y == 0, mine, across), pick(y == 0, across, mine)], axis=1)

    xg_x, xg_total = {}, None
    zero = jnp.zeros((), F32)
    yo_total = add(zero, yo, yo_x, 1)
    for t in range(zn + 1):
        if t < zn - 1:
            if t == 0:
                yo_total = hop(yo_total.astype(BF))
            else:
                k = order[t]
                m_total = m_total.astype(F32) + own_sum(m_parts[k], m_c[k], m_y[k])
                rows = 2 * share
                both = jnp.concatenate([yo_total.astype(BF).reshape(rows, -1), m_total.astype(BF)])
                both = hop(both)
                yo_total, m_total = both[:rows].reshape(2, share, -1), both[rows:]
            k = order[t + 1]
            yo_x[k] = swap(x_give(yo[k]), "x")
        if t >= 2:
            xg_total = hop(xg_total.astype(BF))
        if t in (1, 2):
            pair = order[:2] if t == 1 else order[2:]
            came = swap(jnp.stack([x_give(xg[k]) for k in pair]), "x")
            xg_x.update({k: came[i] for i, k in enumerate(pair)})
        if t == 0:
            send_home(0)
            xg_a = x_terms(1, zn)
            xg_ac = swap(xg_a[1], "c")
        elif t == 1:
            d_normed = product_t(d_flat_x, full_x) + product_t(d_flat_y, full_y)
            d_came = swap(d_normed[tok:].astype(BF), "y")
        elif t == 2:
            unused, first_pull = jax.vjp(rms_scale, tok_own.astype(F32), gain_first)
            d_tok, d_gain_in = first_pull(d_normed[:tok] + d_came.astype(F32))
            tokens_grad = (d_residual + d_tok)[None]
            small = jnp.concatenate([d_prm, jnp.stack([d_gain_in, d_gain_mlp]).reshape(4, half)])
            small = small + swap(small, "c")
        elif t == 3:
            small = small + swap(small, "x")
            give_across([(0, None)])
        if t == zn - 1:
            out_came = return_rows(yo_total[:, :, half:])
        if t == zn:
            y_came = return_columns(yo_total[:, :, :half])
        if t == zn:
            small = small + sum(shifted(small, "z", by, zn, True) for by in range(1, zn))
            ff_home = joined(ff_home, range(1, zn))
            ff_home[0] = own_and_sent(0, None)
            g_gate, g_up, g_down = place_feed_forward_grads(
                [ff_home[far] for far in every], rows_ff, cols_ff, fold, zn,
            )
        if t == 0:
            yo_x, yo_total, xg_a, xg_ac, yo_bc, d_flat_y = tick(
                yo_x, yo_total, xg_a, xg_ac, yo_bc, d_flat_y
            )
            hold(yo, yo_b[0], yo_bc, 3)
            hold(xg, xg_a[0], xg_ac, 1)
        elif t == 1:
            yo_x, yo_total, xg_x, d_normed, d_came, ff_home, m_total, xg_a, xg_ac, ff_give = tick(
                yo_x, yo_total, xg_x, d_normed, d_came, ff_home, m_total, xg_a, xg_ac, ff_give
            )
            hold(xg, xg_a[0], xg_ac, 1)
            xg_total = add(zero, xg, xg_x, 1)
        elif t < zn:
            if t == 2:
                yo_x, yo_total, xg_x, xg_total, small, m_total = tick(
                    yo_x, yo_total, xg_x, xg_total, small, m_total
                )
                m_term = own_sum(m_parts[0], m_c[0], m_y[0])
                result = (residual + m_total.astype(F32) + m_term).astype(BF)[None]
            else:
                yo_total, xg_x, xg_total, small, out_came, ff_sent = tick(
                    yo_total, xg_x, xg_total, small, out_came, ff_sent
                )
        else:
            xg_x, xg_total, small, y_came, out_came, yo_total = tick(
                xg_x, xg_total, small, y_came, out_came, yo_total
            )
        if t >= 2:
            xg_total = add(xg_total, xg, xg_x, order[t - 1])
        if t < zn - 1:
            yo_total = add(yo_total, yo, yo_x, order[t + 1])
    grad_w_x = returned_columns(xg_total[:, :, :half], return_columns(xg_total[:, :, :half]))
    grad_gate_w = jnp.stack(returned_rows(return_rows(xg_total[:, :, half:]))).transpose(0, 2, 1)
    grad_w_y = returned_columns(yo_total[:, :, :half], y_came)
    grad_w_out = jnp.concatenate(returned_rows(out_came), axis=1)

    beside = swap(small, "y")
    both_halves = jnp.concatenate(
        [pick(y == 0, small, beside)[:8], pick(y == 0, beside, small)[:8]], axis=1
    )
    gains = (small + beside)[8:].reshape(2, 2 * half)
    at = ((z * 2 + x) * 4 + y * 2 + c) * share
    own_small = lax.dynamic_slice_in_dim(both_halves, at, share, 1)
    own_gain = lax.dynamic_slice_in_dim(gains, at, share, 1)
    return (
        result,
        tokens_grad,
        grad_w_x,
        grad_w_y,
        grad_w_out,
        grad_gate_w,
        own_gain[0],
        own_gain[1],
        own_small[:WIDTH],
        own_small[WIDTH : WIDTH + 2],
        own_small[WIDTH + 2],
        g_gate,
        g_up,
        g_down.T,
    )


PRECISE = lax.Precision.HIGHEST


def passed_along(value, axis, by):
    devices = lax.axis_size(axis)
    pairs = [(i, i + by) for i in range(devices) if 0 <= i + by < devices]
    return lax.ppermute(value, axis, pairs)


def entering(value, axis, join, neutral, backward):
    count, mine = (lax.axis_size(axis), lax.axis_index(axis))
    pieces = jax.tree.map(lambda part: lax.all_gather(part, axis), value)
    if backward:
        pieces = jax.tree.map(lambda part: part[::-1], pieces)
        mine = count - 1 - mine
    total = jax.tree.map(
        lambda part, zero: jnp.full_like(part, 0) + jnp.asarray(zero, part.dtype), value, neutral
    )

    def step(position, total):
        longer = join(total, jax.tree.map(lambda part: part[position], pieces))
        return jax.tree.map(lambda new, old: jnp.where(position < mine, new, old), longer, total)

    return lax.fori_loop(0, count - 1, step, total)


def affine_pair(earlier, latter):
    return (earlier[0] * latter[0], earlier[1] * latter[0] + latter[1])


def causal_conv(extended, conv_full, tok_count):
    conv_out = conv_full[0] * extended[WIDTH - 1 : WIDTH - 1 + tok_count]
    for tap_index in range(1, WIDTH):
        conv_out = (
            conv_out
            + conv_full[tap_index]
            * extended[WIDTH - 1 - tap_index : WIDTH - 1 - tap_index + tok_count]
        )
    return conv_out


def recurrence_inputs(conv_out, gate_full, bias_full, rate_full):
    tok_count = conv_out.shape[0]
    blocks = gate_full.reshape(2, HD, HEADS, HD)
    grouped = conv_out.reshape(tok_count, HEADS, HD)
    pre_a = (
        jnp.einsum("thi,ihj->thj", grouped, blocks[0], precision=PRECISE).reshape(tok_count, -1)
        + bias_full[0]
    )
    pre_x = (
        jnp.einsum("thi,ihj->thj", grouped, blocks[1], precision=PRECISE).reshape(tok_count, -1)
        + bias_full[1]
    )
    log_decay = -8.0 * jax.nn.sigmoid(pre_a) * rate_full
    decays = jnp.exp(log_decay)
    drives = jnp.sqrt(-jnp.expm1(2.0 * log_decay)) * jax.nn.sigmoid(pre_x) * conv_out
    return (decays, drives)


def fetch_recurrent(w_x, w_y, w_out, gate_w, gain_in, gain_mlp, conv_w, gate_b, rate):
    return (
        lax.all_gather(w_x, ("seq", "fsdp"), axis=0, tiled=True),
        lax.all_gather(w_y, ("seq", "fsdp"), axis=0, tiled=True),
        lax.all_gather(w_out, ("seq", "fsdp"), axis=0, tiled=True),
        lax.all_gather(gate_w, ("seq", "fsdp"), axis=2, tiled=True),
        lax.all_gather(gain_in, ("seq", "fsdp"), axis=0, tiled=True),
        lax.all_gather(gain_mlp, ("seq", "fsdp"), axis=0, tiled=True),
        lax.all_gather(conv_w, ("seq", "fsdp"), axis=1, tiled=True),
        lax.all_gather(gate_b, ("seq", "fsdp"), axis=1, tiled=True),
        lax.all_gather(rate, ("seq", "fsdp"), axis=0, tiled=True),
    )


def fetch_feedforward(w_gate, w_up, w_down):
    return (
        lax.all_gather(w_gate, "seq", axis=0, tiled=True),
        lax.all_gather(w_up, "seq", axis=0, tiled=True),
        lax.all_gather(w_down, "seq", axis=1, tiled=True),
    )


def split_owner(values, dim, seq_count, pair_count):
    shape = values.shape
    share = shape[dim] // (seq_count * pair_count)
    return values.reshape(shape[:dim] + (seq_count, pair_count, share) + shape[dim + 1 :])


def merge_owner(values, dim):
    shape = values.shape
    return values.reshape(shape[:dim] + (shape[dim + 2],) + shape[dim + 3 :])


def sum_recurrent(grads):
    seq_count = lax.axis_size("seq")
    pair_count = lax.axis_size("fsdp")
    dims = (0, 0, 0, 2, 0, 0, 1, 1, 0)
    split = tuple((split_owner(item, dim, seq_count, pair_count) for item, dim in zip(grads, dims)))
    paired = (
        lax.psum_scatter(split[0], "fsdp", scatter_dimension=1, tiled=True),
        lax.psum_scatter(split[1], "fsdp", scatter_dimension=1, tiled=True),
        lax.psum_scatter(split[2], "fsdp", scatter_dimension=1, tiled=True),
        lax.psum_scatter(split[3], "fsdp", scatter_dimension=3, tiled=True),
        lax.psum_scatter(split[4], "fsdp", scatter_dimension=1, tiled=True),
        lax.psum_scatter(split[5], "fsdp", scatter_dimension=1, tiled=True),
        lax.psum_scatter(split[6], "fsdp", scatter_dimension=2, tiled=True),
        lax.psum_scatter(split[7], "fsdp", scatter_dimension=2, tiled=True),
        lax.psum_scatter(split[8], "fsdp", scatter_dimension=1, tiled=True),
    )
    summed = (
        lax.psum_scatter(paired[0], "seq", scatter_dimension=0, tiled=True),
        lax.psum_scatter(paired[1], "seq", scatter_dimension=0, tiled=True),
        lax.psum_scatter(paired[2], "seq", scatter_dimension=0, tiled=True),
        lax.psum_scatter(paired[3], "seq", scatter_dimension=2, tiled=True),
        lax.psum_scatter(paired[4], "seq", scatter_dimension=0, tiled=True),
        lax.psum_scatter(paired[5], "seq", scatter_dimension=0, tiled=True),
        lax.psum_scatter(paired[6], "seq", scatter_dimension=1, tiled=True),
        lax.psum_scatter(paired[7], "seq", scatter_dimension=1, tiled=True),
        lax.psum_scatter(paired[8], "seq", scatter_dimension=0, tiled=True),
    )
    return tuple((merge_owner(item, dim) for item, dim in zip(summed, dims)))


def per_device_gathered(
    tokens,
    w_x,
    w_y,
    w_out,
    gate_w,
    gain_in,
    gain_mlp,
    conv_w,
    gate_b,
    rate,
    w_gate,
    w_up,
    w_down,
    cotangent,
):
    gathered = fetch_recurrent(w_x, w_y, w_out, gate_w, gain_in, gain_mlp, conv_w, gate_b, rate)
    full_x, full_y, full_out = (gathered[0], gathered[1], gathered[2])
    gate_f = gathered[3].astype(jnp.float32)
    gain_first = gathered[4].astype(jnp.float32)
    gain_second = gathered[5].astype(jnp.float32)
    conv_f = gathered[6].astype(jnp.float32)
    bias_f = gathered[7].astype(jnp.float32)
    rate_f = gathered[8].astype(jnp.float32)
    slice_gate, slice_up, slice_down = fetch_feedforward(w_gate, w_up, w_down)
    tok_rows = tokens[0].astype(jnp.float32)
    tok_count = tok_rows.shape[0]
    model_width = tok_rows.shape[1]
    width_r = full_x.shape[1]
    normed = rms_scale(tok_rows, gain_first).astype(jnp.bfloat16)
    branch_x = product(normed, full_x).astype(jnp.bfloat16)
    branch_y = product(normed, full_y)
    carried = passed_along(branch_x[tok_count - (WIDTH - 1) :], "seq", 1)
    extended = jnp.concatenate([carried, branch_x], axis=0).astype(jnp.float32)
    conv_out = causal_conv(extended, conv_f, tok_count)
    decays, drives = recurrence_inputs(conv_out, gate_f, bias_f, rate_f)
    cum_decay, local_state = lax.associative_scan(affine_pair, (decays, drives), axis=0)
    ones_r = jnp.ones((width_r,), jnp.float32)
    zeros_r = jnp.zeros((width_r,), jnp.float32)
    carry_in = entering(
        (cum_decay[-1], local_state[-1]), "seq", affine_pair, (ones_r, zeros_r), False
    )
    state_in = carry_in[1]
    states = local_state + cum_decay * state_in
    gate_y = gelu_tanh(branch_y)
    mixed_rows = (states * gate_y).astype(jnp.bfloat16)
    residual = tok_rows + product(mixed_rows, full_out)
    normed_mlp = rms_scale(residual, gain_second).astype(jnp.bfloat16)
    rows_all = lax.all_gather(normed_mlp[None], "fsdp", axis=0, tiled=True).reshape(-1, model_width)
    gate_pre = product(rows_all, slice_gate)
    up_proj = product(rows_all, slice_up)
    hidden = gated_product(gate_pre, up_proj).astype(jnp.bfloat16)
    mlp_out = lax.psum_scatter(product(hidden, slice_down), "fsdp", scatter_dimension=0, tiled=True)
    result = (residual + mlp_out).astype(jnp.bfloat16)[None]
    fresh = lax.optimization_barrier((w_x, w_y, w_out, w_gate, w_up, w_down, mlp_out))
    again = fetch_recurrent(
        fresh[0], fresh[1], fresh[2], gate_w, gain_in, gain_mlp, conv_w, gate_b, rate
    )
    full_x, full_y, full_out = (again[0], again[1], again[2])
    slice_gate, slice_up, slice_down = fetch_feedforward(fresh[3], fresh[4], fresh[5])
    grad_rows = cotangent[0].astype(jnp.float32)
    grad_all = lax.all_gather(cotangent, "fsdp", axis=0, tiled=True).reshape(-1, model_width)
    d_hidden = product(grad_all, slice_down.T)
    grad_down = product(hidden.T, grad_all)
    unused, mlp_pull = jax.vjp(gated_product, gate_pre, up_proj)
    d_gate_f, d_up_f = mlp_pull(d_hidden)
    d_gate = d_gate_f.astype(jnp.bfloat16)
    d_up = d_up_f.astype(jnp.bfloat16)
    grad_gate = product(rows_all.T, d_gate)
    grad_up = product(rows_all.T, d_up)
    feed_grads = (
        lax.psum_scatter(grad_gate, "seq", scatter_dimension=0, tiled=True),
        lax.psum_scatter(grad_up, "seq", scatter_dimension=0, tiled=True),
        lax.psum_scatter(grad_down, "seq", scatter_dimension=1, tiled=True),
    )
    d_normed_mlp = lax.psum_scatter(
        product(d_gate, slice_gate.T) + product(d_up, slice_up.T),
        "fsdp",
        scatter_dimension=0,
        tiled=True,
    )
    unused, second_pull = jax.vjp(rms_scale, residual, gain_second)
    d_res_norm, d_gain_mlp = second_pull(d_normed_mlp)
    d_residual = grad_rows + d_res_norm
    d_branch = d_residual.astype(jnp.bfloat16)
    grad_out = product(mixed_rows.T, d_branch)
    d_mixed = product(d_branch, full_out.T)
    d_states = d_mixed * gate_y
    unused, y_pull = jax.vjp(gelu_tanh, branch_y)
    d_branch_y = y_pull(d_mixed * states)[0].astype(jnp.bfloat16)
    flipped = decays[::-1]
    coeffs = jnp.concatenate([jnp.ones((1, width_r), jnp.float32), flipped[:-1]], axis=0)
    cum_back, local_back = lax.associative_scan(affine_pair, (coeffs, d_states[::-1]), axis=0)
    outgoing = (cum_back[-1] * flipped[-1], local_back[-1] * flipped[-1])
    carry_back = entering(outgoing, "seq", affine_pair, (ones_r, zeros_r), True)
    state_grad = (local_back + cum_back * carry_back[1])[::-1]
    before = jnp.concatenate([state_in[None], states[:-1]], axis=0)
    unused, gate_pull = jax.vjp(recurrence_inputs, conv_out, gate_f, bias_f, rate_f)
    d_conv, d_gate_w, d_bias, d_rate = gate_pull((state_grad * before, state_grad))

    def conv_only(ext_rows, taps):
        return causal_conv(ext_rows, taps, tok_count)

    unused, conv_pull = jax.vjp(conv_only, extended, conv_f)
    d_extended, grad_conv = conv_pull(d_conv)
    rim_back = passed_along(d_extended[: WIDTH - 1], "seq", -1)
    d_branch_x = (
        d_extended[WIDTH - 1 :] + jnp.pad(rim_back, ((tok_count - (WIDTH - 1), 0), (0, 0)))
    ).astype(jnp.bfloat16)
    grad_x = product(normed.T, d_branch_x)
    grad_y = product(normed.T, d_branch_y)
    d_normed = product(d_branch_x, full_x.T) + product(d_branch_y, full_y.T)
    unused, first_pull = jax.vjp(rms_scale, tok_rows, gain_first)
    d_tok, d_gain_in = first_pull(d_normed)
    tokens_grad = (d_residual + d_tok)[None]
    recurrent_grads = sum_recurrent(
        (grad_x, grad_y, grad_out, d_gate_w, d_gain_in, d_gain_mlp, grad_conv, d_bias, d_rate)
    )
    return (
        result,
        tokens_grad,
        recurrent_grads[0],
        recurrent_grads[1],
        recurrent_grads[2],
        recurrent_grads[3],
        recurrent_grads[4],
        recurrent_grads[5],
        recurrent_grads[6],
        recurrent_grads[7],
        recurrent_grads[8],
        feed_grads[0],
        feed_grads[1],
        feed_grads[2],
    )


def by_mesh_axes(specs):
    names = {("z", "x"): "seq", ("y", "c"): "fsdp", ("z", "x", "y", "c"): ("seq", "fsdp"), None: None}
    return tuple(P(*(names[entry] for entry in spec)) for spec in specs)


def solution(mesh):
    seq_count, pair_count = mesh.shape["seq"], mesh.shape["fsdp"]
    zn = seq_count // 2
    grid = Mesh(mesh.devices.reshape(zn, 2, pair_count // 2, 2), ("z", "x", "y", "c"))
    seq, fsdp, both = ("z", "x"), ("y", "c"), ("z", "x", "y", "c")
    rows = P(fsdp, seq, None)
    by_row = P(both, None)
    by_col = P(None, both)
    placed = (
        rows, by_row, by_row, by_row, P(None, None, both), P(both), P(both), by_col, by_col, P(both),
        P(seq, fsdp), P(seq, fsdp), P(fsdp, seq), rows,
    )
    out_specs = (
        rows, rows, by_row, by_row, by_row, P(None, None, both), P(both), P(both), by_col, by_col,
        P(both), P(seq, fsdp), P(seq, fsdp), P(fsdp, seq),
    )

    lanes = 128

    def run(*args):
        width = args[0].shape[2]
        whole_tiles = width % (16 * mesh.size) == 0 and 2 * width % (lanes * seq_count) == 0
        if whole_tiles and zn >= 4:
            hidden_share = args[10].shape[1] // pair_count
            fold = -(-hidden_share // (lanes * zn)) * lanes
            program = functools.partial(per_device, zn, fold)
            on, ins, outs = grid, placed, out_specs
        else:
            program, on = per_device_gathered, mesh
            ins, outs = by_mesh_axes(placed), by_mesh_axes(out_specs)
        return jax.shard_map(program, mesh=on, in_specs=ins, out_specs=outs, check_vma=False)(*args)

    return run
```

```python
import functools

import jax
import jax.numpy as jnp
from jax import lax
from jax.experimental import pallas as pl
from jax.experimental.pallas import tpu as pltpu
from jax.sharding import Mesh
from jax.sharding import PartitionSpec as P

HEADS = 10
HD = 256
WIDTH = 4
HALO = 16
EPS = 1e-06
BF = jnp.bfloat16
F32 = jnp.float32


def swap(value, axis):
    return lax.ppermute(value, axis, [(0, 1), (1, 0)])


def shifted(value, axes, by, count, wrap=False):
    pairs = [(i, (i + by) % count) for i in range(count) if wrap or 0 <= i + by < count]
    return lax.ppermute(value, axes, pairs)


def pick(flag, first, second):
    return jnp.where(flag, first, second)


def tick(*values):
    return lax.optimization_barrier(values)


def dot(left, right, dims):
    return lax.dot_general(left, right, (dims, ((), ())), preferred_element_type=F32)


def product(left, right):
    return dot(left, right, ((1,), (0,)))


def product_t(left, right):
    return dot(left, right, ((1,), (1,)))


def t_product(left, right):
    return dot(left, right, ((0,), (0,)))


def rms_scale(values, gain_scale):
    return values * lax.rsqrt(jnp.mean(values * values, axis=-1, keepdims=True) + EPS) * gain_scale


def gelu_tanh(values):
    return jax.nn.gelu(values, approximate=True)


def gated_product(left, right):
    return gelu_tanh(left) * right


def gelu_both(v):
    inner = 0.7978845608028654 * (v + 0.044715 * v * v * v)
    th = jnp.tanh(inner)
    value = 0.5 * v * (1.0 + th)
    slope = 0.5 * (1.0 + th) + 0.5 * v * (1.0 - th * th) * 0.7978845608028654 * (1.0 + 0.134145 * v * v)
    return value, slope


def minus_expm1(v):
    series = jnp.full_like(v, 1.0)
    for n in range(11, 1, -1):
        series = 1.0 + series * v * (1.0 / n)
    return jnp.where(v > -1.0, -v * series, 1.0 - jnp.exp(v))


def two_parts(v):
    high = v.astype(BF)
    return high, (v - high.astype(F32)).astype(BF)


def wide_dot(left, right, dims):
    high, low = two_parts(left)
    return dot(high, right, dims) + dot(low, right, dims)


def moved(values, by, fill, rows):
    count = values.shape[0]
    rolled = pltpu.roll(values, by % count, 0)
    inside = rows >= by if by > 0 else rows < count + by
    return jnp.where(inside, rolled, fill)


def scan_rows(decay, drive, rows, backward):
    step = 1
    while step < decay.shape[0]:
        by = -step if backward else step
        drive = drive + decay * moved(drive, by, 0.0, rows)
        decay = decay * moved(decay, by, 1.0, rows)
        step *= 2
    return decay, drive


def conv_taps(rows_ref, halo_ref):
    rows = rows_ref[0].astype(F32)
    extended = jnp.concatenate([halo_ref[0].astype(F32), rows], axis=0)
    count = rows.shape[0]
    return [rows] + [extended[HALO - k : HALO - k + count] for k in range(1, WIDTH)]


def gates(conv_out, gate_ref, prm_ref):
    nt = ((1,), (1,))
    high, low = two_parts(conv_out)
    pre_a = dot(high, gate_ref[0], nt) + dot(low, gate_ref[0], nt) + prm_ref[4:5, :]
    pre_x = dot(high, gate_ref[1], nt) + dot(low, gate_ref[1], nt) + prm_ref[5:6, :]
    sig_a = jax.nn.sigmoid(pre_a)
    sig_x = jax.nn.sigmoid(pre_x)
    log_decay = -8.0 * sig_a * prm_ref[6:7, :]
    return sig_a, sig_x, jnp.exp(log_decay), jnp.sqrt(minus_expm1(2.0 * log_decay))


def forward_kernel(rows_ref, halo_ref, prm_ref, gate_ref, decay_ref, local_ref, cum_ref):
    taps = conv_taps(rows_ref, halo_ref)
    conv_out = sum(prm_ref[k : k + 1, :] * taps[k] for k in range(WIDTH))
    sig_a, sig_x, decays, root = gates(conv_out, gate_ref, prm_ref)
    drives = root * sig_x * conv_out
    decay_ref[0] = decays
    rows = lax.broadcasted_iota(jnp.int32, decays.shape, 0)
    cum, local = scan_rows(decays, drives, rows, False)
    cum_ref[0] = cum
    local_ref[0] = local


def back_scan_kernel(d_mixed_ref, branch_y_ref, states_ref, decay_ref, d_y_ref, local_ref, cum_ref):
    value, slope = gelu_both(branch_y_ref[0])
    d_mixed = d_mixed_ref[0]
    d_y_ref[0] = (d_mixed * states_ref[0] * slope).astype(BF)
    rows = lax.broadcasted_iota(jnp.int32, d_mixed.shape, 0)
    coeffs = moved(decay_ref[0], -1, 1.0, rows)
    cum, local = scan_rows(coeffs, d_mixed * value, rows, True)
    cum_ref[0] = cum
    local_ref[0] = local


def backward_kernel(
    rows_ref, halo_ref, prm_ref, gate_ref, local_ref, cum_ref, ends_ref, states_ref,
    d_conv_ref, d_gate_ref, d_prm_ref,
):
    taps = conv_taps(rows_ref, halo_ref)
    conv_out = sum(prm_ref[k : k + 1, :] * taps[k] for k in range(WIDTH))
    sig_a, sig_x, decays, root = gates(conv_out, gate_ref, prm_ref)
    rows = lax.broadcasted_iota(jnp.int32, decays.shape, 0)
    grad = local_ref[0] + cum_ref[0] * ends_ref[0, 0:1, :]
    before = jnp.where(rows >= 1, pltpu.roll(states_ref[0], 1, 0), ends_ref[0, 1:2, :])
    d_log = grad * before * decays - grad * sig_x * conv_out * (decays * decays / root)
    d_pre_a = d_log * (-8.0 * prm_ref[6:7, :]) * sig_a * (1.0 - sig_a)
    d_pre_x = grad * root * conv_out * sig_x * (1.0 - sig_x)
    nn, tn = ((1,), (0,)), ((0,), (0,))
    a_high, a_low = two_parts(d_pre_a)
    x_high, x_low = two_parts(d_pre_x)
    c_high, c_low = two_parts(conv_out)
    d_conv = grad * root * sig_x
    d_conv = d_conv + (dot(a_high, gate_ref[0], nn) + dot(a_low, gate_ref[0], nn))
    d_conv = d_conv + (dot(x_high, gate_ref[1], nn) + dot(x_low, gate_ref[1], nn))
    d_conv_ref[0] = d_conv
    d_gate_a = dot(a_high, c_high, tn) + dot(a_low, c_high, tn) + dot(a_high, c_low, tn)
    d_gate_x = dot(x_high, c_high, tn) + dot(x_low, c_high, tn) + dot(x_high, c_low, tn)
    total = lambda v: jnp.sum(v, axis=0, keepdims=True)
    sums = [total(d_conv * taps[k]) for k in range(WIDTH)]
    sums += [total(d_pre_a), total(d_pre_x), total(d_log * (-8.0 * sig_a))]
    sums.append(jnp.zeros_like(sums[0]))
    d_prm = jnp.concatenate(sums, axis=0)
    first = pl.program_id(1) == 0

    @pl.when(first)
    def _():
        d_gate_ref[0] = d_gate_a
        d_gate_ref[1] = d_gate_x
        d_prm_ref[...] = d_prm

    @pl.when(jnp.logical_not(first))
    def _():
        d_gate_ref[0] += d_gate_a
        d_gate_ref[1] += d_gate_x
        d_prm_ref[...] += d_prm


def head_specs(tok):
    rows = pl.BlockSpec((1, tok, HD), lambda h, q: (q, 0, h))
    halo = pl.BlockSpec((1, HALO, HD), lambda h, q: (q, 0, h))
    prm = pl.BlockSpec((8, HD), lambda h, q: (0, h))
    gate = pl.BlockSpec((2, HD, HD), lambda h, q: (0, h, 0))
    ends = pl.BlockSpec((1, 8, HD), lambda h, q: (q, 0, h))
    return rows, halo, prm, gate, ends


PARAMS = dict(vmem_limit_bytes=48 * 1024 * 1024)
COST = pl.CostEstimate(flops=0, bytes_accessed=0, transcendentals=0)


def forward_call(branch_x, halo, prm, gate):
    seqs, tok, half = branch_x.shape
    rows_s, halo_s, prm_s, gate_s, _ = head_specs(tok)
    out = jax.ShapeDtypeStruct(branch_x.shape, F32)
    return pl.pallas_call(
        forward_kernel,
        grid=(half // HD, seqs),
        in_specs=[rows_s, halo_s, prm_s, gate_s],
        out_specs=[rows_s] * 3,
        out_shape=[out] * 3,
        compiler_params=pltpu.CompilerParams(**PARAMS),
        cost_estimate=COST,
        name="recurrence_forward",
    )(branch_x, halo, prm, gate)


def back_scan_call(d_mixed, branch_y, states, decays):
    seqs, tok, half = d_mixed.shape
    rows_s = head_specs(tok)[0]
    out = jax.ShapeDtypeStruct(d_mixed.shape, F32)
    return pl.pallas_call(
        back_scan_kernel,
        grid=(half // HD, seqs),
        in_specs=[rows_s] * 4,
        out_specs=[rows_s] * 3,
        out_shape=[jax.ShapeDtypeStruct(d_mixed.shape, BF), out, out],
        compiler_params=pltpu.CompilerParams(**PARAMS),
        cost_estimate=COST,
        name="recurrence_back_scan",
    )(d_mixed, branch_y, states, decays)


def backward_call(branch_x, halo, prm, gate, local, cum, ends, states):
    seqs, tok, half = branch_x.shape
    rows_s, halo_s, prm_s, gate_s, ends_s = head_specs(tok)
    return pl.pallas_call(
        backward_kernel,
        grid=(half // HD, seqs),
        in_specs=[rows_s, halo_s, prm_s, gate_s, rows_s, rows_s, ends_s, rows_s],
        out_specs=[rows_s, gate_s, prm_s],
        out_shape=[
            jax.ShapeDtypeStruct(branch_x.shape, F32),
            jax.ShapeDtypeStruct(gate.shape, F32),
            jax.ShapeDtypeStruct(prm.shape, F32),
        ],
        compiler_params=pltpu.CompilerParams(**PARAMS),
        cost_estimate=COST,
        name="recurrence_backward",
    )(branch_x, halo, prm, gate, local, cum, ends, states)


def place_kernel(plan, count_in, *refs):
    index = {axis: lax.axis_index(axis) for axis in ("z", "x", "y", "c")}
    for source, start, size, out, target in plan:
        refs[count_in + out][target(index)] = refs[source][:, start : start + size]


def place(plan, pieces, outs, name):
    whole = pl.BlockSpec(memory_space=pltpu.VMEM)
    return pl.pallas_call(
        functools.partial(place_kernel, plan, len(pieces)),
        in_specs=[whole] * len(pieces),
        out_specs=[whole] * len(outs),
        out_shape=[jax.ShapeDtypeStruct(shape, BF) for shape in outs],
        cost_estimate=COST,
        compiler_params=pltpu.CompilerParams(**PARAMS),
        name=name,
    )(*pieces)


def rows_at(block, share, offset=None, size=None):
    def target(index):
        rows = pl.ds(pl.multiple_of(block(index) * share, 16), share)
        if size is None:
            return rows, slice(None)
        return rows, pl.ds(offset(index), size)

    return target


def home_kernel(zn, fold, count, cols_ff, *refs):
    lanes = 128
    for far in range(count):
        start = lax.rem(lax.axis_index("z") - far + zn, zn) * fold
        for j in range(fold // lanes):
            at = start + j * lanes

            @pl.when(at < cols_ff)
            def _(far=far, j=j, at=at):
                dest = pl.ds(pl.multiple_of(at, lanes), lanes)
                for n in range(3):
                    col = n * fold + j * lanes
                    refs[count + n][:, dest] = refs[far][:, col : col + lanes].astype(F32)


def place_feed_forward_grads(pieces, rows_ff, cols_ff, fold, zn):
    whole = pl.BlockSpec(memory_space=pltpu.VMEM)
    return pl.pallas_call(
        functools.partial(home_kernel, zn, fold, len(pieces), cols_ff),
        in_specs=[whole] * len(pieces),
        out_specs=[whole] * 3,
        out_shape=[jax.ShapeDtypeStruct((rows_ff, cols_ff), F32)] * 3,
        cost_estimate=COST,
        compiler_params=pltpu.CompilerParams(**PARAMS),
        name="place_feed_forward_grads",
    )(*pieces)


TN = ((0,), (0,))


def split_blocks(whole_ref, keep_ref, give_ref, share, mine):
    for j in range(4):
        ours = pl.multiple_of((2 * j + mine) * share, 8)
        theirs = pl.multiple_of((2 * j + 1 - mine) * share, 8)
        keep_ref[0, j] = whole_ref[pl.ds(ours, share), :]
        give_ref[0, j] = whole_ref[pl.ds(theirs, share), :].astype(BF)


def yo_kernel(share, where_ref, normed_ref, mixed_ref, d_y_ref, d_out_ref, keep_ref, give_ref, whole_ref):
    half = d_y_ref.shape[1]
    whole_ref[:, :half] = dot(normed_ref[...], d_y_ref[...], TN)
    whole_ref[:, half:] = dot(mixed_ref[...], d_out_ref[...], TN)
    split_blocks(whole_ref, keep_ref, give_ref, share, where_ref[1])


def xg_kernel(share, where_ref, normed_ref, d_gate_ref, d_x_ref, keep_ref, give_ref, whole_ref):
    half = d_x_ref.shape[1]
    whole_ref[:, :half] = dot(normed_ref[...], d_x_ref[...], TN)
    whole_ref[:, half:] = d_gate_ref[0]
    split_blocks(whole_ref, keep_ref, give_ref, share, where_ref[1])


def term_call(kernel, where, specs, args, first, count, share, columns, name):
    block = pl.BlockSpec((1, 4, share, columns), lambda n, where: (n, 0, 0, 0))
    return pl.pallas_call(
        functools.partial(kernel, share),
        grid_spec=pltpu.PrefetchScalarGridSpec(
            num_scalar_prefetch=1,
            grid=(count,),
            in_specs=specs,
            out_specs=[block, block],
            scratch_shapes=[pltpu.VMEM((8 * share, columns), F32)],
        ),
        out_shape=[
            jax.ShapeDtypeStruct((count, 4, share, columns), F32),
            jax.ShapeDtypeStruct((count, 4, share, columns), BF),
        ],
        cost_estimate=COST,
        compiler_params=pltpu.CompilerParams(**PARAMS),
        name=name,
    )(where, *args)


def ff_kernel(steps, fold, where_ref, *refs):
    rows, cots, hidden, d_gu = (refs[n * steps : (n + 1) * steps] for n in range(4))
    keep_ref, give_ref, whole_ref = refs[4 * steps :]
    first = second = 0.0
    for k in range(steps):
        first = first + dot(rows[k][...], d_gu[k][...], TN)
        second = second + dot(cots[k][...], hidden[k][...], TN)
    whole_ref[:, : 2 * fold] = first
    whole_ref[:, 2 * fold :] = second
    size = keep_ref.shape[1]
    mine = where_ref[2]
    keep_ref[0] = whole_ref[pl.ds(pl.multiple_of(mine * size, 8), size), :]
    give_ref[0] = whole_ref[pl.ds(pl.multiple_of((1 - mine) * size, 8), size), :].astype(BF)


def ff_grads_call(where, rows, cots, hidden, d_gu, zn, rows_ff):
    steps, fold = len(rows), hidden[0].shape[1]
    count = rows[0].shape[0]
    part = pl.BlockSpec((count, 2 * rows_ff), lambda far, where: (0, lax.rem(where[0] + far, zn)))
    whole = lambda item: pl.BlockSpec(item.shape, lambda far, where: (0, 0))
    block = pl.BlockSpec((1, rows_ff, 3 * fold), lambda far, where: (far, 0, 0))
    shape = (zn, rows_ff, 3 * fold)
    return pl.pallas_call(
        functools.partial(ff_kernel, steps, fold),
        grid_spec=pltpu.PrefetchScalarGridSpec(
            num_scalar_prefetch=1,
            grid=(zn,),
            in_specs=[part] * (2 * steps) + [whole(item) for item in (*hidden, *d_gu)],
            out_specs=[block, block],
            scratch_shapes=[pltpu.VMEM((2 * rows_ff, 3 * fold), F32)],
        ),
        out_shape=[jax.ShapeDtypeStruct(shape, F32), jax.ShapeDtypeStruct(shape, BF)],
        cost_estimate=COST,
        compiler_params=pltpu.CompilerParams(**PARAMS),
        name="feed_forward_grads",
    )(where, *rows, *cots, *hidden, *d_gu)


def carried(decay, drive, zn, x, by):
    own = jnp.stack([decay, drive])
    beside = swap(own, "x")
    inner = x == 0 if by > 0 else x == 1
    near, far = pick(inner, own, beside), pick(inner, beside, own)
    pair = jnp.stack([near[0] * far[0], near[1] * far[0] + far[1]])
    came = [shifted(pair, "z", by * dist, zn) for dist in range(zn - 1, 0, -1)]
    state = jnp.zeros_like(drive)
    for part in came:
        state = part[0] * state + part[1]
    return pick(inner, state, near[0] * state + near[1])


def per_device(
    zn, fold,
    tokens, w_x, w_y, w_out, gate_w, gain_in, gain_mlp, conv_w, gate_b, rate,
    w_gate, w_up, w_down, cotangent,
):
    z, x, y, c = (lax.axis_index(axis) for axis in ("z", "x", "y", "c"))
    zh = zn // 2
    seq_count = 2 * zn
    tok, width = tokens.shape[1], tokens.shape[2]
    share, wide_r = w_x.shape
    half = wide_r // 2
    rows_ff, cols_ff = w_gate.shape
    zx, zy = ("z", "x"), ("z", "y")
    z_of = [lax.rem(z - k + zn, zn) for k in range(zn)]
    lanes = 128
    every = range(zn)
    hop = lambda value: shifted(value, "z", 1, zn, True)

    spread = []
    for other in (0, 1):
        pairs = []
        for h in (0, 1):
            for zl in range(zh):
                for ys in (0, 1):
                    k = ys ^ other
                    pairs.append(((h * zh + zl) * 2 + ys, (k * zh + zl) * 2 + h))
        spread.append(pairs)
    gathered_back = [[(b, a) for a, b in pairs] for pairs in spread]
    own_half = lambda w: pick(y == 0, w[:, :half], w[:, half:])
    other_half = lambda w: pick(y == 0, w[:, half:], w[:, :half])

    def source(k, across, other):
        def at(i):
            flip = lambda value, on: 1 - value if on else value
            return lax.rem(i["z"] - k + zn, zn), flip(i["x"], across), flip(i["c"], other)

        return at

    def by_rows(at, beside):
        def block(i):
            sz, sx, sc = at(i)
            return ((sz * 2 + sx) * 2 + (1 - i["y"] if beside else i["y"])) * 2 + sc

        return block

    def by_spread(at, second):
        def block(i):
            sz, sx, sc = at(i)
            sh = sz // zh
            return ((lax.rem(sz, zh) * 2 + sx) * 2 + (1 - sh if second else sh)) * 2 + sc

        return block

    def gate_at(at, second):
        rows = by_spread(at, second)

        def target(i):
            start = pl.multiple_of(rows(i) * share, 16)
            return at(i)[0] // zh, pl.ds(start, share), slice(None)

        return target

    params = jnp.concatenate([gain_in[None], gain_mlp[None], conv_w, gate_b, rate[None]])
    count_p = params.shape[0]
    params = jnp.pad(params.T, ((0, 0), (0, lanes - count_p)))
    gate_t = gate_w.transpose(0, 2, 1)
    gate_pieces = [
        lax.ppermute(pick(y == 0, gate_t[k], gate_t[1 - k]), zy, spread[k]) for k in (0, 1)
    ]
    wide_x = half + lanes
    x_own = jnp.concatenate([own_half(w_x), params], axis=1)
    x_other = swap(jnp.concatenate([other_half(w_x), params], axis=1), "y")
    unit_x = jnp.concatenate([x_own, x_other, gate_pieces[0], gate_pieces[1]], axis=1)
    tok_own, cot = tokens[0], cotangent[0]
    cot_z, cot_y = [cot], {}
    unit_x, w_y, w_out, tok_own, ff_raw = tick(unit_x, w_y, w_out, tok_own, (w_gate, w_up, w_down))

    a_z, a_x, a_zc, a_xc = [unit_x], [], [], []
    padded = zn * fold
    widen = lambda w: jnp.pad(w, ((0, 0), (0, padded - cols_ff)))
    ff_wide = [widen(ff_raw[0]), widen(ff_raw[1]), widen(ff_raw[2].T)]

    def ff_piece(z_at):
        return jnp.concatenate(
            [lax.dynamic_slice_in_dim(w, z_at * fold, fold, 1) for w in ff_wide], axis=1
        )

    ff_units = [ff_piece(lax.rem(z + far, zn)) for far in every]
    for k in range(1, zn):
        a_z.append(hop(a_z[-1]))
        a_x.append(swap(a_z[k - 1], "x"))
        a_zc.append(swap(a_z[k - 1], "c"))
        if k > 1:
            a_xc.append(swap(a_x[k - 2], "c"))
        if k == 1:
            tok_other = swap(tok_own, "y")
            y_other = swap(other_half(w_y), "y")
            a_z, a_x, w_out = tick(a_z, a_x, w_out)
            out_halves = [w_out[:, :half], w_out[:, half:]]
            out_parts = [
                lax.ppermute(pick(y == 0, out_halves[i], out_halves[1 - i]), zy, spread[i])
                for i in (0, 1)
            ]
        elif k == 2:
            a_z, a_x, tok_own, tok_other, y_other, out_parts = tick(
                a_z, a_x, tok_own, tok_other, y_other, out_parts
            )
        else:
            a_z, a_x = tick(a_z, a_x)
    tok_f = jnp.stack([tok_own, tok_other]).astype(F32)
    unit_yo = jnp.concatenate([own_half(w_y), y_other, out_parts[0], out_parts[1]], axis=1)
    unit_yo, a_z = tick(unit_yo, a_z)

    b_z, b_x, b_zc, b_xc = [unit_yo, hop(unit_yo)], [], [], []
    a_x.append(swap(a_z[-1], "x"))
    a_zc.append(swap(a_z[-1], "c"))
    a_xc.append(swap(a_x[-2], "c"))
    a_x, a_zc, a_xc, unit_yo, ff_units = tick(a_x, a_zc, a_xc, b_z[0], ff_units)
    b_z[0] = unit_yo
    a_xc.append(swap(a_x[-1], "c"))
    b_x.append(swap(b_z[0], "x"))
    placed, plan = [], []
    for k in every:
        for j, part in enumerate((a_z[k], a_zc[k], a_x[k], a_xc[k])):
            at = source(k, j >= 2, j % 2)
            n = len(placed)
            placed.append(part)
            for beside in (0, 1):
                block = by_rows(at, beside)
                plan.append((n, beside * wide_x, half, 0, rows_at(block, share)))
                plan.append((n, beside * wide_x + half, lanes, 1, rows_at(block, share)))
                plan.append((n, 2 * wide_x + beside * HD, HD, 2, gate_at(at, beside)))
    full_x, full_p, gates_t = place(
        plan, placed, [(width, half), (width, lanes), (2, half, HD)], "place_w_x"
    )
    smalls = full_p[:, :count_p].astype(F32).T
    gain_first, gain_second = smalls[0], smalls[1]
    prm = jnp.pad(smalls[2:], ((0, 1), (0, 0)))
    prm = pick(y == 0, prm[:, :half], prm[:, half:])
    normed = rms_scale(tok_f, gain_first).astype(BF).reshape(2 * tok, width)
    branch_x = product(normed, full_x).astype(BF).reshape(2, tok, half)

    branch_x, b_z = tick(branch_x, b_z)
    b_z.append(hop(b_z[-1]))
    b_x.append(swap(b_z[1], "x"))
    b_zc += [swap(b_z[0], "c"), swap(b_z[1], "c")]
    halo = shifted(branch_x[:, tok - HALO :], zx, 1, seq_count)
    halo, b_z, b_x = tick(halo, b_z, b_x)
    for k in range(3, zn):
        b_z.append(hop(b_z[-1]))
        b_x.append(swap(b_z[k - 1], "x"))
        b_zc.append(swap(b_z[k - 1], "c"))
        b_xc.append(swap(b_x[k - 3], "c"))
        if k == 3:
            decays, local, cum = tick(*forward_call(branch_x, halo, prm, gates_t))
            state_in = carried(cum[:, -1], local[:, -1], zn, x, 1)
            state_in, b_z, b_x = tick(state_in, b_z, b_x)
        else:
            b_z, b_x = tick(b_z, b_x)
    turns = [
        [(far, None) for far in range(1, zn) if far % 3 == 1],
        [(far, 0) for far in range(1, zn) if far % 3 == 2],
        [(far, 1) for far in range(1, zn) if far % 3 == 2],
        [(far, None) for far in range(1, zn) if far % 3 == 0],
    ]

    def sent_along(blocks, turn):
        sent = {}
        for far, part in turns[turn]:
            block = blocks[far]
            cut = block.shape[1] // 2
            if part is not None:
                block = block[:, :cut] if part == 0 else block[:, cut:]
            sent[far, part] = shifted(block, "z", far, zn, True)
        return sent

    def joined(came, fars):
        return {
            far: came[far, None] if (far, None) in came
            else jnp.concatenate([came[far, 0], came[far, 1]], axis=1)
            for far in fars
        }

    far_of = lambda turn: [far for far, _ in turns[turn]]
    ff_units, b_z = tick(ff_units, b_z)
    ff_came, ff_x = sent_along(ff_units, 0), {}
    b_x.append(swap(b_z[-1], "x"))
    b_zc.append(swap(b_z[-1], "c"))
    b_xc += [swap(b_x[-3], "c"), swap(b_x[-2], "c")]
    b_x, cot_z, cot_y, ff_units, ff_came = tick(b_x, cot_z, cot_y, ff_units, ff_came)

    ff_came.update(sent_along(ff_units, 1))
    ff_x[0] = swap(ff_units[0], "x")
    cot_y[0] = swap(cot_z[0], "y")
    b_xc.append(swap(b_x[-1], "c"))
    placed, plan = [], []
    for k in every:
        for j, part in enumerate((b_z[k], b_zc[k], b_x[k], b_xc[k])):
            at = source(k, j >= 2, j % 2)
            n = len(placed)
            placed.append(part)
            column = lambda i, at=at: pl.multiple_of((at(i)[0] // zh) * half, lanes)
            for beside in (0, 1):
                plan.append((n, beside * half, half, 0, rows_at(by_rows(at, beside), share)))
                plan.append(
                    (n, (2 + beside) * half, half, 1, rows_at(by_spread(at, beside), share, column, half))
                )
    full_y, full_out = place(plan, placed, [(width, half), (half, width)], "place_w_y_w_out")
    branch_y = product(normed, full_y).reshape(2, tok, half)
    states = local + cum * state_in[:, None]
    mixed = (states * gelu_tanh(branch_y)).astype(BF).reshape(2 * tok, half)
    out_sum = product(mixed, full_out)
    out_own, out_give = out_sum[:tok], out_sum[tok:].astype(BF)
    out_own, out_give, ff_came, ff_x, ff_units, cot_z, cot_y = tick(
        out_own, out_give, ff_came, ff_x, ff_units, cot_z, cot_y
    )
    out_came = swap(out_give, "y")
    ff_came.update(sent_along(ff_units, 2))
    ff_x.update({far: swap(piece, "x") for far, piece in joined(ff_came, far_of(0)).items()})
    cot_z.append(hop(cot_z[0]))
    out_came, out_own, ff_came, ff_x, ff_units, cot_z = tick(
        out_came, out_own, ff_came, ff_x, ff_units, cot_z
    )
    residual = tok_own.astype(F32) + out_own + out_came.astype(F32)
    normed_mlp = rms_scale(residual, gain_second).astype(BF)

    row_z, row_y = [normed_mlp, hop(normed_mlp)], {0: swap(normed_mlp, "y")}
    ff_came.update(sent_along(ff_units, 3))
    ff_x.update({far: swap(piece, "x") for far, piece in joined(ff_came, far_of(1)).items()})
    cot_y[1] = swap(cot_z[1], "y")
    row_z, row_y, cot_z, cot_y, ff_came, ff_x = tick(row_z, row_y, cot_z, cot_y, ff_came, ff_x)
    ff_x.update({far: swap(piece, "x") for far, piece in joined(ff_came, far_of(3)).items()})
    row_z.append(hop(row_z[-1]))
    cot_z.append(hop(cot_z[-1]))
    row_y[1] = swap(row_z[1], "y")
    row_z, row_y, cot_z, ff_x = tick(row_z, row_y, cot_z, ff_x)
    ff_pieces = joined(ff_came, range(1, zn))
    ff_pieces[0] = ff_units[0]
    placed, plan = [], []
    for k in every:
        for across, part in enumerate((ff_pieces[k], ff_x[k])):
            at = source(k, across, 0)
            block = lambda i, at=at: at(i)[0] * 2 + at(i)[1]
            n = len(placed)
            placed.append(part)
            plan.append((n, 0, 2 * fold, 0, rows_at(block, rows_ff)))
            plan.append((n, 2 * fold, fold, 1, rows_at(block, rows_ff)))
    w_gu, w_dt = place(plan, placed, [(width, 2 * fold), (width, fold)], "place_feed_forward")

    def with_cores(pair):
        return jnp.concatenate(list(pair) + [swap(part, "c") for part in pair])

    def feed_forward(k):
        rows, grads = with_cores((row_z[k], row_y[k])), with_cores((cot_z[k], cot_y[k]))
        gu = product(rows, w_gu)
        d_hidden = product(grads, w_dt)
        hidden, pull = jax.vjp(gated_product, gu[:, :fold], gu[:, fold:])
        d_gu = jnp.concatenate([item.astype(BF) for item in pull(d_hidden)], axis=1)
        return rows, grads, hidden.astype(BF), d_gu, product_t(d_gu, w_gu).reshape(4, tok, width)

    steps, d_parts, d_c, d_y, total = {}, {}, {}, {}, None
    m_parts, m_c, m_y, m_total = {}, {}, {}, None

    def core_give(parts):
        return parts[2:].astype(BF)

    def y_give(parts, came_c):
        return (parts[1] + came_c[1].astype(F32)).astype(BF)

    def own_sum(parts, came_c, came_y):
        return parts[0] + came_c[0].astype(F32) + came_y.astype(F32)

    where = jnp.stack([z, c, x]).astype(jnp.int32)
    order = list(range(1, zn)) + [0]
    for i in range(zn + 2):
        if i < zn:
            k = order[i]
            steps[k] = feed_forward(k)
            d_parts[k] = steps[k][-1]
        if k + 2 < zn and i < zn - 1:
            row_z.append(hop(row_z[-1]))
        if k + 2 < zn and i < zn - 1:
            cot_z.append(hop(cot_z[-1]))
        if i < zn - 2:
            row_y[k + 1] = swap(row_z[k + 1], "y")
            cot_y[k + 1] = swap(cot_z[k + 1], "y")
        if i < 2 or i == zn + 1:
            for n in [k] if i < 2 else order[2:]:
                m_parts[n] = product_t(steps[n][2], w_dt).reshape(4, tok, width)
        if 1 <= i <= 2:
            m_c[order[i - 1]] = swap(core_give(m_parts[order[i - 1]]), "c")
        if 1 <= i <= zn:
            d_c[order[i - 1]] = swap(core_give(d_parts[order[i - 1]]), "c")
        if 2 <= i:
            k = order[i - 2]
            d_y[k] = swap(y_give(d_parts[k], d_c[k]), "y")
        if 3 <= i:
            k = order[i - 3]
            term = own_sum(d_parts[k], d_c[k], d_y[k])
            total = hop((term if total is None else total.astype(F32) + term).astype(BF))
        if i == 4:
            m_y[1] = swap(y_give(m_parts[1], m_c[1]), "y")
        if i == 5:
            m_total = hop(own_sum(m_parts[1], m_c[1], m_y[1]).astype(BF))
        if i == zn:
            ff_keep, ff_give = tick(*ff_grads_call(
                where, *([steps[k][n] for k in every] for n in range(4)), zn, rows_ff
            ))
            ff_give = {far: ff_give[far] for far in every}
        if i == zn + 1:
            break
        steps, row_z, row_y, cot_z, cot_y, d_parts, d_c, d_y, total, m_parts, m_c, m_y, m_total = tick(
            steps, row_z, row_y, cot_z, cot_y, d_parts, d_c, d_y, total, m_parts, m_c, m_y, m_total
        )
        steps = {k: step[:4] for k, step in steps.items()}

    ff_sent, ff_home = {}, {}

    def cut_block(block, part):
        middle = 3 * fold // 2
        return block if part is None else block[:, :middle] if part == 0 else block[:, middle:]

    def give_across(turn):
        for far, part in turn:
            ff_sent[far, part] = swap(cut_block(ff_give[far], part), "x")

    def own_and_sent(far, part):
        return (cut_block(ff_keep[far], part) + ff_sent[far, part].astype(F32)).astype(BF)

    def send_home(turn):
        for far, part in turns[turn]:
            ff_home[far, part] = shifted(own_and_sent(far, part), "z", far, zn, True)

    give_across(turns[3] + turns[1])
    total, d_y, ff_sent, ff_give, m_total, m_parts = tick(total, d_y, ff_sent, ff_give, m_total, m_parts)

    d_normed_mlp = own_sum(d_parts[0], d_c[0], d_y[0]) + total.astype(F32)
    unused, second_pull = jax.vjp(rms_scale, residual, gain_second)
    d_res_norm, d_gain_mlp = second_pull(d_normed_mlp)
    d_residual = cot.astype(F32) + d_res_norm
    d_branch = d_residual.astype(BF)
    d_other = swap(d_branch, "y")
    send_home(3)
    give_across(turns[2])
    for k in order[2:]:
        m_c[k] = swap(core_give(m_parts[k]), "c")
    d_branch, d_other, ff_sent, ff_give, m_total, m_c = tick(d_branch, d_other, ff_sent, ff_give, m_total, m_c)

    d_branch_pair = jnp.concatenate([d_branch, d_other])
    d_mixed = product_t(d_branch_pair, full_out).reshape(2, tok, half)
    d_branch_y, local_back, cum_back = back_scan_call(d_mixed, branch_y, states, decays)
    leaving = decays[:, 0] * local_back[:, 0]
    m_y[2] = swap(y_give(m_parts[2], m_c[2]), "y")
    send_home(1)
    give_across(turns[0])
    d_flat_y = d_branch_y.reshape(2 * tok, half)
    eight = 8 * share
    z_at = lambda n, where, first: lax.rem(where[0] - n - first + 2 * zn, zn)
    full_spec = pl.BlockSpec((2 * tok, half), lambda n, where: (0, 0))

    def yo_terms(first, count):
        specs = [
            pl.BlockSpec((2 * tok, eight), lambda n, where: (0, z_at(n, where, first))),
            pl.BlockSpec((2 * tok, eight), lambda n, where: (0, lax.rem(z_at(n, where, first), zh))),
            full_spec,
            pl.BlockSpec((2 * tok, half), lambda n, where: (0, z_at(n, where, first) // zh)),
        ]
        args = (normed, mixed, d_flat_y, d_branch_pair)
        return term_call(yo_kernel, where, specs, args, first, count, share, 2 * half, "grad_w_y_w_out")

    def x_terms(first, count):
        specs = [
            pl.BlockSpec((2 * tok, eight), lambda n, where: (0, z_at(n, where, first))),
            pl.BlockSpec(
                (1, eight, HD),
                lambda n, where: (z_at(n, where, first) // zh, lax.rem(z_at(n, where, first), zh), 0),
            ),
            full_spec,
        ]
        args = (normed, d_gates, d_flat_x)
        return term_call(xg_kernel, where, specs, args, first, count, share, half + HD, "grad_w_x")

    yo_a = yo_terms(1, 2)
    leaving, d_branch_y, yo_a, m_y, m_total, ff_home, ff_sent, ff_give = tick(
        leaving, d_branch_y, yo_a, m_y, m_total, ff_home, ff_sent, ff_give
    )

    carry_back = carried(cum[:, -1], leaving, zn, x, -1)
    ends = jnp.pad(jnp.stack([carry_back, state_in], axis=1), ((0, 0), (0, 6), (0, 0)))
    yo_ac = swap(yo_a[1], "c")

    yo, xg = {}, {}

    def hold(terms, kept, came, first):
        for n in range(came.shape[0]):
            terms[(first + n) % zn] = (kept, came, n)

    def at_x(term, which):
        kept, came, n = term
        part = lambda v: lax.dynamic_slice(
            v.reshape((-1, 2, 2) + v.shape[2:]), (n, which, 0, 0, 0), (1, 1, 2) + v.shape[2:]
        )[0, 0]
        return part(kept) + part(came).astype(F32)

    def x_give(term):
        return at_x(term, 1 - x).astype(BF)

    hold(yo, yo_a[0], yo_ac, 1)
    yo_first = x_give(yo[1])
    ends, yo_a, yo_ac, yo_first, d_flat_y, ff_sent, ff_give, m_y, m_total = tick(
        ends, yo_a, yo_ac, yo_first, d_flat_y, ff_sent, ff_give, m_y, m_total
    )
    hold(yo, yo_a[0], yo_ac, 1)
    yo_x = {1: swap(yo_first, "x")}
    send_home(2)
    for k in order[2:]:
        m_y[k] = swap(y_give(m_parts[k], m_c[k]), "y")
    d_conv, d_gates, d_prm = tick(*backward_call(
        branch_x, halo, prm, gates_t, local_back, cum_back, ends, states
    ))
    rim = shifted(d_conv[:, :8], zx, -1, seq_count)
    yo_b = yo_terms(3, zn - 2)
    rim, yo_x, yo_b, ff_home, ff_sent, ff_give, m_total, m_y = tick(
        rim, yo_x, yo_b, ff_home, ff_sent, ff_give, m_total, m_y
    )
    yo_bc = swap(yo_b[1], "c")

    d_ext = jnp.concatenate([d_conv, rim], axis=1)
    d_branch_x = sum(prm[k] * d_ext[:, k : k + tok] for k in range(WIDTH)).astype(BF)
    d_flat_x = d_branch_x.reshape(2 * tok, half)

    def add(total, terms, came_x, k):
        return total.astype(F32) + at_x(terms[k], x) + came_x[k].astype(F32)

    def return_rows(sums):
        mine = z // zh
        return [
            lax.ppermute(
                lax.dynamic_index_in_dim(sums, mine if k == 0 else 1 - mine, 0, False).astype(BF),
                zy, gathered_back[k],
            )
            for k in (0, 1)
        ]

    def returned_rows(came):
        came = [item.astype(F32) for item in came]
        return pick(y == 0, came[0], came[1]), pick(y == 0, came[1], came[0])

    def return_columns(sums):
        return swap(lax.dynamic_index_in_dim(sums, 1 - y, 0, False).astype(BF), "y")

    def returned_columns(sums, came):
        mine, across = lax.dynamic_index_in_dim(sums, y, 0, False), came.astype(F32)
        return jnp.concatenate([pick(y == 0, mine, across), pick(y == 0, across, mine)], axis=1)

    xg_x, xg_total = {}, None
    zero = jnp.zeros((), F32)
    yo_total = add(zero, yo, yo_x, 1)
    for t in range(zn + 1):
        if t < zn - 1:
            if t == 0:
                yo_total = hop(yo_total.astype(BF))
            else:
                k = order[t]
                m_total = m_total.astype(F32) + own_sum(m_parts[k], m_c[k], m_y[k])
                rows = 2 * share
                both = jnp.concatenate([yo_total.astype(BF).reshape(rows, -1), m_total.astype(BF)])
                both = hop(both)
                yo_total, m_total = both[:rows].reshape(2, share, -1), both[rows:]
            k = order[t + 1]
            yo_x[k] = swap(x_give(yo[k]), "x")
        if t >= 2:
            xg_total = hop(xg_total.astype(BF))
        if t in (1, 2):
            pair = order[:2] if t == 1 else order[2:]
            came = swap(jnp.stack([x_give(xg[k]) for k in pair]), "x")
            xg_x.update({k: came[i] for i, k in enumerate(pair)})
        if t == 0:
            send_home(0)
            xg_a = x_terms(1, zn)
            xg_ac = swap(xg_a[1], "c")
        elif t == 1:
            d_normed = product_t(d_flat_x, full_x) + product_t(d_flat_y, full_y)
            d_came = swap(d_normed[tok:].astype(BF), "y")
        elif t == 2:
            unused, first_pull = jax.vjp(rms_scale, tok_own.astype(F32), gain_first)
            d_tok, d_gain_in = first_pull(d_normed[:tok] + d_came.astype(F32))
            tokens_grad = (d_residual + d_tok)[None]
            small = jnp.concatenate([d_prm, jnp.stack([d_gain_in, d_gain_mlp]).reshape(4, half)])
            small = small + swap(small, "c")
        elif t == 3:
            small = small + swap(small, "x")
            give_across([(0, None)])
        if t == zn:
            out_came = return_rows(yo_total[:, :, half:])
            y_came = return_columns(yo_total[:, :, :half])
        if t == zn:
            doubling = zn & (zn - 1) == 0
            if doubling:
                small = small + shifted(small, "z", 1, zn, True)
            ff_home = joined(ff_home, range(1, zn))
            ff_home[0] = own_and_sent(0, None)
            g_gate, g_up, g_down = place_feed_forward_grads(
                [ff_home[far] for far in every], rows_ff, cols_ff, fold, zn,
            )
        if t == 0:
            yo_x, yo_total, xg_a, xg_ac, yo_bc, d_flat_y = tick(
                yo_x, yo_total, xg_a, xg_ac, yo_bc, d_flat_y
            )
            hold(yo, yo_b[0], yo_bc, 3)
            hold(xg, xg_a[0], xg_ac, 1)
        elif t == 1:
            yo_x, yo_total, xg_x, d_normed, d_came, ff_home, m_total, xg_a, xg_ac, ff_give = tick(
                yo_x, yo_total, xg_x, d_normed, d_came, ff_home, m_total, xg_a, xg_ac, ff_give
            )
            hold(xg, xg_a[0], xg_ac, 1)
            xg_total = add(zero, xg, xg_x, 1)
        elif t < zn:
            if t == 2:
                yo_x, yo_total, xg_x, xg_total, small, m_total = tick(
                    yo_x, yo_total, xg_x, xg_total, small, m_total
                )
                m_term = own_sum(m_parts[0], m_c[0], m_y[0])
                result = (residual + m_total.astype(F32) + m_term).astype(BF)[None]
            else:
                yo_total, xg_x, xg_total, small, ff_sent = tick(
                    yo_total, xg_x, xg_total, small, ff_sent
                )
        else:
            xg_x, xg_total, small, y_came, out_came, yo_total = tick(
                xg_x, xg_total, small, y_came, out_came, yo_total
            )
        if t >= 2:
            xg_total = add(xg_total, xg, xg_x, order[t - 1])
        if t < zn - 1:
            yo_total = add(yo_total, yo, yo_x, order[t + 1])
    grad_w_x = returned_columns(xg_total[:, :, :half], return_columns(xg_total[:, :, :half]))
    grad_gate_w = jnp.stack(returned_rows(return_rows(xg_total[:, :, half:]))).transpose(0, 2, 1)
    grad_w_y = returned_columns(yo_total[:, :, :half], y_came)
    grad_w_out = jnp.concatenate(returned_rows(out_came), axis=1)

    if doubling:
        by = 2
        while by < zn:
            small = small + shifted(small, "z", by, zn, True)
            by *= 2
    else:
        small = small + sum(shifted(small, "z", by, zn, True) for by in range(1, zn))
    beside = swap(small, "y")
    both_halves = jnp.concatenate(
        [pick(y == 0, small, beside)[:8], pick(y == 0, beside, small)[:8]], axis=1
    )
    gains = (small + beside)[8:].reshape(2, 2 * half)
    at = ((z * 2 + x) * 4 + y * 2 + c) * share
    own_small = lax.dynamic_slice_in_dim(both_halves, at, share, 1)
    own_gain = lax.dynamic_slice_in_dim(gains, at, share, 1)
    return (
        result,
        tokens_grad,
        grad_w_x,
        grad_w_y,
        grad_w_out,
        grad_gate_w,
        own_gain[0],
        own_gain[1],
        own_small[:WIDTH],
        own_small[WIDTH : WIDTH + 2],
        own_small[WIDTH + 2],
        g_gate,
        g_up,
        g_down.T,
    )


PRECISE = lax.Precision.HIGHEST


def passed_along(value, axis, by):
    devices = lax.axis_size(axis)
    pairs = [(i, i + by) for i in range(devices) if 0 <= i + by < devices]
    return lax.ppermute(value, axis, pairs)


def entering(value, axis, join, neutral, backward):
    count, mine = (lax.axis_size(axis), lax.axis_index(axis))
    pieces = jax.tree.map(lambda part: lax.all_gather(part, axis), value)
    if backward:
        pieces = jax.tree.map(lambda part: part[::-1], pieces)
        mine = count - 1 - mine
    total = jax.tree.map(
        lambda part, zero: jnp.full_like(part, 0) + jnp.asarray(zero, part.dtype), value, neutral
    )

    def step(position, total):
        longer = join(total, jax.tree.map(lambda part: part[position], pieces))
        return jax.tree.map(lambda new, old: jnp.where(position < mine, new, old), longer, total)

    return lax.fori_loop(0, count - 1, step, total)


def affine_pair(earlier, latter):
    return (earlier[0] * latter[0], earlier[1] * latter[0] + latter[1])


def causal_conv(extended, conv_full, tok_count):
    conv_out = conv_full[0] * extended[WIDTH - 1 : WIDTH - 1 + tok_count]
    for tap_index in range(1, WIDTH):
        conv_out = (
            conv_out
            + conv_full[tap_index]
            * extended[WIDTH - 1 - tap_index : WIDTH - 1 - tap_index + tok_count]
        )
    return conv_out


def recurrence_inputs(conv_out, gate_full, bias_full, rate_full):
    tok_count = conv_out.shape[0]
    blocks = gate_full.reshape(2, HD, HEADS, HD)
    grouped = conv_out.reshape(tok_count, HEADS, HD)
    pre_a = (
        jnp.einsum("thi,ihj->thj", grouped, blocks[0], precision=PRECISE).reshape(tok_count, -1)
        + bias_full[0]
    )
    pre_x = (
        jnp.einsum("thi,ihj->thj", grouped, blocks[1], precision=PRECISE).reshape(tok_count, -1)
        + bias_full[1]
    )
    log_decay = -8.0 * jax.nn.sigmoid(pre_a) * rate_full
    decays = jnp.exp(log_decay)
    drives = jnp.sqrt(-jnp.expm1(2.0 * log_decay)) * jax.nn.sigmoid(pre_x) * conv_out
    return (decays, drives)


def fetch_recurrent(w_x, w_y, w_out, gate_w, gain_in, gain_mlp, conv_w, gate_b, rate):
    return (
        lax.all_gather(w_x, ("seq", "fsdp"), axis=0, tiled=True),
        lax.all_gather(w_y, ("seq", "fsdp"), axis=0, tiled=True),
        lax.all_gather(w_out, ("seq", "fsdp"), axis=0, tiled=True),
        lax.all_gather(gate_w, ("seq", "fsdp"), axis=2, tiled=True),
        lax.all_gather(gain_in, ("seq", "fsdp"), axis=0, tiled=True),
        lax.all_gather(gain_mlp, ("seq", "fsdp"), axis=0, tiled=True),
        lax.all_gather(conv_w, ("seq", "fsdp"), axis=1, tiled=True),
        lax.all_gather(gate_b, ("seq", "fsdp"), axis=1, tiled=True),
        lax.all_gather(rate, ("seq", "fsdp"), axis=0, tiled=True),
    )


def fetch_feedforward(w_gate, w_up, w_down):
    return (
        lax.all_gather(w_gate, "seq", axis=0, tiled=True),
        lax.all_gather(w_up, "seq", axis=0, tiled=True),
        lax.all_gather(w_down, "seq", axis=1, tiled=True),
    )


def split_owner(values, dim, seq_count, pair_count):
    shape = values.shape
    share = shape[dim] // (seq_count * pair_count)
    return values.reshape(shape[:dim] + (seq_count, pair_count, share) + shape[dim + 1 :])


def merge_owner(values, dim):
    shape = values.shape
    return values.reshape(shape[:dim] + (shape[dim + 2],) + shape[dim + 3 :])


def sum_recurrent(grads):
    seq_count = lax.axis_size("seq")
    pair_count = lax.axis_size("fsdp")
    dims = (0, 0, 0, 2, 0, 0, 1, 1, 0)
    split = tuple((split_owner(item, dim, seq_count, pair_count) for item, dim in zip(grads, dims)))
    paired = (
        lax.psum_scatter(split[0], "fsdp", scatter_dimension=1, tiled=True),
        lax.psum_scatter(split[1], "fsdp", scatter_dimension=1, tiled=True),
        lax.psum_scatter(split[2], "fsdp", scatter_dimension=1, tiled=True),
        lax.psum_scatter(split[3], "fsdp", scatter_dimension=3, tiled=True),
        lax.psum_scatter(split[4], "fsdp", scatter_dimension=1, tiled=True),
        lax.psum_scatter(split[5], "fsdp", scatter_dimension=1, tiled=True),
        lax.psum_scatter(split[6], "fsdp", scatter_dimension=2, tiled=True),
        lax.psum_scatter(split[7], "fsdp", scatter_dimension=2, tiled=True),
        lax.psum_scatter(split[8], "fsdp", scatter_dimension=1, tiled=True),
    )
    summed = (
        lax.psum_scatter(paired[0], "seq", scatter_dimension=0, tiled=True),
        lax.psum_scatter(paired[1], "seq", scatter_dimension=0, tiled=True),
        lax.psum_scatter(paired[2], "seq", scatter_dimension=0, tiled=True),
        lax.psum_scatter(paired[3], "seq", scatter_dimension=2, tiled=True),
        lax.psum_scatter(paired[4], "seq", scatter_dimension=0, tiled=True),
        lax.psum_scatter(paired[5], "seq", scatter_dimension=0, tiled=True),
        lax.psum_scatter(paired[6], "seq", scatter_dimension=1, tiled=True),
        lax.psum_scatter(paired[7], "seq", scatter_dimension=1, tiled=True),
        lax.psum_scatter(paired[8], "seq", scatter_dimension=0, tiled=True),
    )
    return tuple((merge_owner(item, dim) for item, dim in zip(summed, dims)))


def per_device_gathered(
    tokens,
    w_x,
    w_y,
    w_out,
    gate_w,
    gain_in,
    gain_mlp,
    conv_w,
    gate_b,
    rate,
    w_gate,
    w_up,
    w_down,
    cotangent,
):
    gathered = fetch_recurrent(w_x, w_y, w_out, gate_w, gain_in, gain_mlp, conv_w, gate_b, rate)
    full_x, full_y, full_out = (gathered[0], gathered[1], gathered[2])
    gate_f = gathered[3].astype(jnp.float32)
    gain_first = gathered[4].astype(jnp.float32)
    gain_second = gathered[5].astype(jnp.float32)
    conv_f = gathered[6].astype(jnp.float32)
    bias_f = gathered[7].astype(jnp.float32)
    rate_f = gathered[8].astype(jnp.float32)
    slice_gate, slice_up, slice_down = fetch_feedforward(w_gate, w_up, w_down)
    tok_rows = tokens[0].astype(jnp.float32)
    tok_count = tok_rows.shape[0]
    model_width = tok_rows.shape[1]
    width_r = full_x.shape[1]
    normed = rms_scale(tok_rows, gain_first).astype(jnp.bfloat16)
    branch_x = product(normed, full_x).astype(jnp.bfloat16)
    branch_y = product(normed, full_y)
    carried = passed_along(branch_x[tok_count - (WIDTH - 1) :], "seq", 1)
    extended = jnp.concatenate([carried, branch_x], axis=0).astype(jnp.float32)
    conv_out = causal_conv(extended, conv_f, tok_count)
    decays, drives = recurrence_inputs(conv_out, gate_f, bias_f, rate_f)
    cum_decay, local_state = lax.associative_scan(affine_pair, (decays, drives), axis=0)
    ones_r = jnp.ones((width_r,), jnp.float32)
    zeros_r = jnp.zeros((width_r,), jnp.float32)
    carry_in = entering(
        (cum_decay[-1], local_state[-1]), "seq", affine_pair, (ones_r, zeros_r), False
    )
    state_in = carry_in[1]
    states = local_state + cum_decay * state_in
    gate_y = gelu_tanh(branch_y)
    mixed_rows = (states * gate_y).astype(jnp.bfloat16)
    residual = tok_rows + product(mixed_rows, full_out)
    normed_mlp = rms_scale(residual, gain_second).astype(jnp.bfloat16)
    rows_all = lax.all_gather(normed_mlp[None], "fsdp", axis=0, tiled=True).reshape(-1, model_width)
    gate_pre = product(rows_all, slice_gate)
    up_proj = product(rows_all, slice_up)
    hidden = gated_product(gate_pre, up_proj).astype(jnp.bfloat16)
    mlp_out = lax.psum_scatter(product(hidden, slice_down), "fsdp", scatter_dimension=0, tiled=True)
    result = (residual + mlp_out).astype(jnp.bfloat16)[None]
    fresh = lax.optimization_barrier((w_x, w_y, w_out, w_gate, w_up, w_down, mlp_out))
    again = fetch_recurrent(
        fresh[0], fresh[1], fresh[2], gate_w, gain_in, gain_mlp, conv_w, gate_b, rate
    )
    full_x, full_y, full_out = (again[0], again[1], again[2])
    slice_gate, slice_up, slice_down = fetch_feedforward(fresh[3], fresh[4], fresh[5])
    grad_rows = cotangent[0].astype(jnp.float32)
    grad_all = lax.all_gather(cotangent, "fsdp", axis=0, tiled=True).reshape(-1, model_width)
    d_hidden = product(grad_all, slice_down.T)
    grad_down = product(hidden.T, grad_all)
    unused, mlp_pull = jax.vjp(gated_product, gate_pre, up_proj)
    d_gate_f, d_up_f = mlp_pull(d_hidden)
    d_gate = d_gate_f.astype(jnp.bfloat16)
    d_up = d_up_f.astype(jnp.bfloat16)
    grad_gate = product(rows_all.T, d_gate)
    grad_up = product(rows_all.T, d_up)
    feed_grads = (
        lax.psum_scatter(grad_gate, "seq", scatter_dimension=0, tiled=True),
        lax.psum_scatter(grad_up, "seq", scatter_dimension=0, tiled=True),
        lax.psum_scatter(grad_down, "seq", scatter_dimension=1, tiled=True),
    )
    d_normed_mlp = lax.psum_scatter(
        product(d_gate, slice_gate.T) + product(d_up, slice_up.T),
        "fsdp",
        scatter_dimension=0,
        tiled=True,
    )
    unused, second_pull = jax.vjp(rms_scale, residual, gain_second)
    d_res_norm, d_gain_mlp = second_pull(d_normed_mlp)
    d_residual = grad_rows + d_res_norm
    d_branch = d_residual.astype(jnp.bfloat16)
    grad_out = product(mixed_rows.T, d_branch)
    d_mixed = product(d_branch, full_out.T)
    d_states = d_mixed * gate_y
    unused, y_pull = jax.vjp(gelu_tanh, branch_y)
    d_branch_y = y_pull(d_mixed * states)[0].astype(jnp.bfloat16)
    flipped = decays[::-1]
    coeffs = jnp.concatenate([jnp.ones((1, width_r), jnp.float32), flipped[:-1]], axis=0)
    cum_back, local_back = lax.associative_scan(affine_pair, (coeffs, d_states[::-1]), axis=0)
    outgoing = (cum_back[-1] * flipped[-1], local_back[-1] * flipped[-1])
    carry_back = entering(outgoing, "seq", affine_pair, (ones_r, zeros_r), True)
    state_grad = (local_back + cum_back * carry_back[1])[::-1]
    before = jnp.concatenate([state_in[None], states[:-1]], axis=0)
    unused, gate_pull = jax.vjp(recurrence_inputs, conv_out, gate_f, bias_f, rate_f)
    d_conv, d_gate_w, d_bias, d_rate = gate_pull((state_grad * before, state_grad))

    def conv_only(ext_rows, taps):
        return causal_conv(ext_rows, taps, tok_count)

    unused, conv_pull = jax.vjp(conv_only, extended, conv_f)
    d_extended, grad_conv = conv_pull(d_conv)
    rim_back = passed_along(d_extended[: WIDTH - 1], "seq", -1)
    d_branch_x = (
        d_extended[WIDTH - 1 :] + jnp.pad(rim_back, ((tok_count - (WIDTH - 1), 0), (0, 0)))
    ).astype(jnp.bfloat16)
    grad_x = product(normed.T, d_branch_x)
    grad_y = product(normed.T, d_branch_y)
    d_normed = product(d_branch_x, full_x.T) + product(d_branch_y, full_y.T)
    unused, first_pull = jax.vjp(rms_scale, tok_rows, gain_first)
    d_tok, d_gain_in = first_pull(d_normed)
    tokens_grad = (d_residual + d_tok)[None]
    recurrent_grads = sum_recurrent(
        (grad_x, grad_y, grad_out, d_gate_w, d_gain_in, d_gain_mlp, grad_conv, d_bias, d_rate)
    )
    return (
        result,
        tokens_grad,
        recurrent_grads[0],
        recurrent_grads[1],
        recurrent_grads[2],
        recurrent_grads[3],
        recurrent_grads[4],
        recurrent_grads[5],
        recurrent_grads[6],
        recurrent_grads[7],
        recurrent_grads[8],
        feed_grads[0],
        feed_grads[1],
        feed_grads[2],
    )


def by_mesh_axes(specs):
    names = {("z", "x"): "seq", ("y", "c"): "fsdp", ("z", "x", "y", "c"): ("seq", "fsdp"), None: None}
    return tuple(P(*(names[entry] for entry in spec)) for spec in specs)


def solution(mesh):
    seq_count, pair_count = mesh.shape["seq"], mesh.shape["fsdp"]
    zn = seq_count // 2
    grid = Mesh(mesh.devices.reshape(zn, 2, pair_count // 2, 2), ("z", "x", "y", "c"))
    seq, fsdp, both = ("z", "x"), ("y", "c"), ("z", "x", "y", "c")
    rows = P(fsdp, seq, None)
    by_row = P(both, None)
    by_col = P(None, both)
    placed = (
        rows, by_row, by_row, by_row, P(None, None, both), P(both), P(both), by_col, by_col, P(both),
        P(seq, fsdp), P(seq, fsdp), P(fsdp, seq), rows,
    )
    out_specs = (
        rows, rows, by_row, by_row, by_row, P(None, None, both), P(both), P(both), by_col, by_col,
        P(both), P(seq, fsdp), P(seq, fsdp), P(fsdp, seq),
    )

    lanes = 128

    def run(*args):
        width = args[0].shape[2]
        whole_tiles = width % (16 * mesh.size) == 0 and 2 * width % (lanes * seq_count) == 0
        if whole_tiles and zn >= 4:
            hidden_share = args[10].shape[1] // pair_count
            fold = -(-hidden_share // (lanes * zn)) * lanes
            program = functools.partial(per_device, zn, fold)
            on, ins, outs = grid, placed, out_specs
        else:
            program, on = per_device_gathered, mesh
            ins, outs = by_mesh_axes(placed), by_mesh_axes(out_specs)
        return jax.shard_map(program, mesh=on, in_specs=ins, out_specs=outs, check_vma=False)(*args)

    return run
```
